32 devices in a mesh: prow: 4 (over y, core), pcol: 8 (over z, x).
Axes of the slice: x: 2, y: 2, z: 4, core: 2. Of those that a mesh axis runs over, the one named last changes fastest.
Arguments:
- sigma_top: float32 [3584, 3584], P('pcol', 'prow')
- structure: int32 [1792], replicated, may hold values from 0 to 3583, as said below
- u_panel: float32 [1792, 1024], P('pcol', 'prow'), may hold values from -0.3 to 0.3
- d_term: float32 [1024, 1024], P('pcol', 'prow'), may hold values from -6 to 6
Outputs:
- sigma_sj: float32 [1792, 1024], P('pcol', 'prow')
- sigma_jj: float32 [1024, 1024], P('pcol', 'prow')
The draws below stay inside these ranges and needn't reach their ends.
Inputs may be any that keep to these rules, and one draw needn't show every extreme that they name: sigma_top is symmetric; structure is strictly increasing; its first entry is 0 and its last is 3583; each aligned block of 896 ancestor rows holds at most 560 structure rows, and the first block holds exactly 560.
All inputs are finite; a program needn't handle non-finite values.
Results may differ from the reference program's by a relative error of at most 0.000075.
Values sent between devices are 32-bit elements; how exact they have to be, the bound alone decides.
No kernel may reach another device: no remote copies, remote signals or barrier semaphores. Data moves between devices by JAX's collectives and lax.ppermute only.
A program may use at most 64 MiB of HBM per device.

```python
import math
import jax
import jax.numpy as jnp
from jax import lax

WIDTH = 1024
ROWS_DEV = 224
STRUCT = 1792
ORDER = 3584
OWNER_BLK = 896
N_PCOL = 8


def draw_sigma_top(key, part):
    key = jax.random.fold_in(key, 11)
    base = jax.random.normal(key, (ORDER, ORDER), jnp.float32)
    sym = (base + base.T) * (0.4 / math.sqrt(2.0 * ORDER))
    return sym + jnp.eye(ORDER, dtype=jnp.float32)


def draw_structure(key, part):
    key = jax.random.fold_in(key, 23)
    key_delta, key_sign, key_perm = jax.random.split(key, 3)
    blocks = ORDER // OWNER_BLK
    pairs = blocks // 2
    half = OWNER_BLK // 2
    spread = OWNER_BLK // 8
    delta = jax.random.randint(key_delta, (pairs,), 0, spread + 1)
    delta = delta.at[0].set(spread)
    signs = jax.random.randint(key_sign, (pairs,), 0, 2) * 2 - 1
    signs = signs.at[0].set(1)
    counts = jnp.stack([half + signs * delta, half - signs * delta], axis=1).reshape(blocks)
    perm_keys = jax.random.split(key_perm, blocks)
    perms = jax.vmap(lambda k: jax.random.permutation(k, OWNER_BLK))(perm_keys)
    anchor = jnp.zeros((blocks,), jnp.int32).at[blocks - 1].set(OWNER_BLK - 1)
    anchor_rank = jnp.take_along_axis(perms, anchor[:, None], axis=1)
    ranks = jnp.mod(perms - anchor_rank, OWNER_BLK)
    chosen = (ranks < counts[:, None]).reshape(ORDER)
    rows = jnp.nonzero(chosen, size=STRUCT, fill_value=ORDER - 1)[0]
    return rows.astype(jnp.int32)


def block_levels(stream_key, shape, cuts, least, top_value):
    gain = 1.0
    for dim, parts in cuts:
        steps = jax.random.uniform(jax.random.fold_in(jax.random.fold_in(stream_key, 6), dim), (parts,), jnp.float32, least / len(cuts), top_value / len(cuts))
        gain = gain * jnp.repeat(jnp.exp(steps), shape[dim] // parts).reshape((-1,) + (1,) * (len(shape) - 1 - dim))
    return gain


def bell_draw(own_key, shape, deviation, limit, shards=(), kind=jnp.bfloat16):
    result = jax.random.normal(own_key, shape, jnp.float32) * deviation
    if len(shards) > 0:
        result = block_levels(own_key, shape, shards, -0.22, 0.18) * result
    return jnp.clip(result, min=-limit, max=limit).astype(kind)


def setup_inputs(seed: int = 0) -> dict:
    arg_keys = jax.random.split(jax.random.key(seed), 5)
    sigma_top = draw_sigma_top(jax.random.fold_in(arg_keys[4], 71), 0)
    structure = draw_structure(jax.random.fold_in(arg_keys[4], 71), 0)
    u_panel = bell_draw(arg_keys[2], (STRUCT, WIDTH), 0.05, 0.3, ((0, 8), (1, 4)), jnp.float32)
    d_term = bell_draw(arg_keys[3], (WIDTH, WIDTH), 1.0, 6.0, ((0, 8), (1, 4)), jnp.float32)
    return dict(sigma_top=sigma_top, structure=structure, u_panel=u_panel, d_term=d_term)


def reference(sigma_top, structure, u_panel, d_term):
    position = jnp.arange(STRUCT, dtype=jnp.int32)
    source = (position % ROWS_DEV) * N_PCOL + position // ROWS_DEV
    rowmap = structure[source.astype(jnp.int32)]
    placed = jnp.zeros((ORDER, WIDTH), jnp.float32).at[rowmap].set(u_panel)
    image = jnp.dot(sigma_top, placed, precision=lax.Precision.HIGHEST, preferred_element_type=jnp.float32)
    sigma_sj = -image[rowmap]
    correction = jnp.dot(u_panel.T, sigma_sj, precision=lax.Precision.HIGHEST, preferred_element_type=jnp.float32)
    sigma_jj = d_term - correction
    return sigma_sj, sigma_jj
```

```python
import functools

import jax
import jax.numpy as jnp
from jax import lax
from jax.experimental import pallas as pl
from jax.experimental.pallas import tpu as pltpu
from jax.sharding import PartitionSpec as P

LANES = 128
BLOCK_CAP = 560
VMEM = pl.BlockSpec(memory_space=pltpu.VMEM)
SMEM = pl.BlockSpec(memory_space=pltpu.SMEM)
PARAMS = pltpu.CompilerParams(vmem_limit_bytes=48 * 2**20)


def split(v):
    high = v.astype(jnp.bfloat16)
    return high, (v - high.astype(jnp.float32)).astype(jnp.bfloat16)


def split3(v):
    high = v.astype(jnp.bfloat16)
    rest = v - high.astype(jnp.float32)
    mid = rest.astype(jnp.bfloat16)
    return high, mid, (rest - mid.astype(jnp.float32)).astype(jnp.bfloat16)


def dot(a, b, dims=((1,), (0,))):
    return lax.dot_general(a, b, (dims, ((), ())), preferred_element_type=jnp.float32)


def dot3(a, b, dims=((1,), (0,))):
    ah, al = a
    bh, bl = b
    return dot(ah, bh, dims) + (dot(ah, bl, dims) + dot(al, bh, dims))


def one_hot(mask):
    return jnp.where(mask, 1.0, 0.0).astype(jnp.bfloat16)


def select_kernel(cols_ref, sigma_ref, out_ref):
    rows, width = sigma_ref.shape
    cap = cols_ref.shape[1]
    place = one_hot(lax.broadcasted_iota(jnp.int32, (width, cap), 0) == cols_ref[...])
    high, low = split(sigma_ref[...])
    picked = dot(high, place) + dot(low, place)
    full = cap // LANES
    for i in range(full):
        out_ref[rows * i : rows * (i + 1), :] = picked[:, LANES * i : LANES * (i + 1)]
    tail = picked[:, LANES * full :]
    out_ref[rows * full :, :] = jnp.concatenate([tail[: rows // 2], tail[rows // 2 :]], axis=1)


def image_term(block_ref, u_rows, rows):
    cap, w = u_rows.shape
    full = cap // LANES
    half = rows // 2
    body = jnp.concatenate([block_ref[rows * i : rows * (i + 1), :] for i in range(full)], axis=1)
    term = dot3(split(body), split(u_rows[: LANES * full]))
    tail = split(block_ref[rows * full :, :])
    last = u_rows[LANES * full :]
    zero = jnp.zeros_like(last)
    top = dot3(tail, split(jnp.concatenate([last, zero], axis=0)))
    bottom = dot3(tail, split(jnp.concatenate([zero, last], axis=0)))
    return term + jnp.concatenate([top, bottom], axis=0)


def rows_from(us_ref, start, count, w):
    base = pl.multiple_of((start // 8) * 8, 8)
    size = count + 8
    lanes = [
        pltpu.roll(us_ref[k, pl.ds(base, size), :], size - (start - base), 0)[:count]
        for k in range(us_ref.shape[0])
    ]
    return jnp.concatenate(lanes, axis=1)[:, :w]


def first_kernel(n_blocks, rows, info_ref, *refs):
    nc = len(refs) - n_blocks - 2
    u_refs, block_refs = refs[:nc], refs[nc : nc + n_blocks]
    us_ref, image_ref = refs[-2:]
    m, w = u_refs[0].shape
    n = m * nc
    for k, u_ref in enumerate(u_refs):
        u = u_ref[...]
        if w % LANES:
            u = jnp.concatenate([u, jnp.zeros((m, LANES - w % LANES), jnp.float32)], axis=1)
        for i in range(us_ref.shape[0]):
            us_ref[i, pl.ds(info_ref[n_blocks + k], m, stride=nc), :] = u[:, LANES * i : LANES * (i + 1)]
    us_ref[:, n:, :] = jnp.zeros((us_ref.shape[0], us_ref.shape[1] - n, LANES), jnp.float32)
    cap = us_ref.shape[1] - n - 8
    image = None
    for b, block_ref in enumerate(block_refs):
        term = image_term(block_ref, rows_from(us_ref, info_ref[b], cap, w), rows)
        image = term if image is None else image + term
    image_ref[...] = image


def rest_kernel(n, info_ref, slot_ref, us_ref, part_ref, *refs):
    block_refs, out_ref = refs[:-1], refs[-1]
    rows, w = part_ref.shape
    cap = us_ref.shape[1] - n - 8
    image = part_ref[...]
    def add(b, block_ref, image):
        return image + image_term(block_ref, rows_from(us_ref, info_ref[b], cap, w), rows)

    if len(block_refs[0].shape) == 3:
        stack = block_refs[0]
        image = lax.fori_loop(0, stack.shape[0], lambda b, v: add(b, stack.at[b], v), image)
    else:
        for b, block_ref in enumerate(block_refs):
            image = add(b, block_ref, image)
    place = one_hot(lax.broadcasted_iota(jnp.int32, (out_ref.shape[0], rows), 0) == slot_ref[...])
    high, mid, low = split3(image)
    out_ref[...] = dot(place, high) + (dot(place, mid) + dot(place, low))


def pick_kernel(from_ref, got_ref, out_ref):
    m, k = out_ref.shape[0], got_ref.shape[0]
    place = one_hot(lax.broadcasted_iota(jnp.int32, (m, k), 1) == from_ref[...])
    high, mid, low = split3(got_ref[...])
    out_ref[...] = -(dot(place, high) + (dot(place, mid) + dot(place, low)))


def correction_kernel(info_ref, mine_ref, other_ref, *refs):
    u_refs, out_ref = refs[:-1], refs[-1]
    m = mine_ref.shape[0]
    mine, other = split(mine_ref[...]), split(other_ref[...])
    for b, u_ref in enumerate(u_refs):
        dims = ((0,), (0,))
        term = dot3(split(u_ref[:m, :]), mine, dims) + dot3(split(u_ref[m:, :]), other, dims)
        out_ref[info_ref[b]] = term


def call(kernel, out_shape, specs, *args):
    many = isinstance(out_shape, (list, tuple))
    return pl.pallas_call(
        kernel,
        out_shape=out_shape,
        in_specs=list(specs),
        out_specs=[VMEM] * len(out_shape) if many else VMEM,
        compiler_params=PARAMS,
    )(*args)


def f32(*shape):
    return jax.ShapeDtypeStruct(shape, jnp.float32)


def shift(v, axis, size, by):
    return lax.ppermute(v, axis, [(k, (k + by) % size) for k in range(size)])


def swap(v, axis, size):
    return lax.ppermute(v, axis, [(k, k ^ 1) for k in range(size)])


def spread(v, axis, size):
    blocks = [v] + [shift(v, axis, size, 2 * t) for t in range(1, size // 2)]
    out = []
    for t, block in enumerate(blocks):
        out += [(t, 0, block), (t, 1, swap(block, axis, size))]
    return out


def per_device(sigma_top, structure, u_panel, d_term):
    nc, nr = lax.axis_size("pcol"), lax.axis_size("prow")
    c, r = lax.axis_index("pcol"), lax.axis_index("prow")
    nz = nc // 2
    rows, cols = sigma_top.shape
    m, w = u_panel.shape
    n = structure.shape[0]
    cap = -(-BLOCK_CAP // 64) * 64
    slots = -(-rows // nc)
    iota = lambda size: jnp.arange(size, dtype=jnp.int32)

    from_z = [u_panel] + [shift(u_panel, "pcol", nc, 2 * t) for t in range(1, nz)]
    from_x = [swap(b, "pcol", nc) for b in from_z]
    u_blocks, u_index = [], []
    for t in range(nz):
        owner = jnp.mod(c - 2 * t, nc)
        u_blocks += [from_z[t], from_x[t]]
        u_index += [owner, jnp.bitwise_xor(owner, 1)]

    padded = jnp.concatenate([structure, jnp.full((cap,), 2**30, jnp.int32)])
    starts = jnp.sum(structure[None, :] < (iota(nr) * cols)[:, None], axis=1, dtype=jnp.int32)
    named = lax.dynamic_slice_in_dim(padded, jnp.sum(structure < r * cols, dtype=jnp.int32), cap) - r * cols
    full = cap // LANES
    packed = f32(rows * full + rows // 2, LANES)
    chosen = call(select_kernel, packed, [VMEM] * 2, named[None, :], sigma_top)
    blocks, begin = [], []
    for t, flip, block in spread(chosen, "prow", nr):
        owner = jnp.bitwise_xor(jnp.mod(r - 2 * t, nr), flip)
        blocks.append(block)
        begin.append(starts[owner])

    us, part = call(
        functools.partial(first_kernel, 2, rows),
        [f32(-(-w // LANES), n + cap + 8, LANES), f32(rows, w)],
        [SMEM] + [VMEM] * (nc + 2),
        jnp.stack(begin[:2] + u_index),
        *u_blocks,
        *blocks[:2],
    )

    order = iota(n)
    low = jnp.sum(structure < c * rows, dtype=jnp.int32)
    turn = jnp.mod(order, nc)
    ahead = (low - turn + nc - 1) // nc
    slot = turn * slots + order // nc - ahead
    match = structure[:, None] == (c * rows + iota(rows))[None, :]
    slot_of_row = jnp.max(jnp.where(match, slot[:, None], -1), axis=0)
    later = blocks[2:] if nr <= 4 else [jnp.stack(blocks[2:])]
    sent = call(
        functools.partial(rest_kernel, n),
        f32(nc * slots, w),
        [SMEM] + [VMEM] * (3 + len(later)),
        jnp.stack(begin[2:]),
        slot_of_row[None, :],
        us,
        part,
        *later,
    )
    got = lax.all_to_all(sent, "pcol", split_axis=0, concat_axis=0, tiled=True)

    mine = jnp.sum(jnp.where(iota(nc)[None, :] == c, structure.reshape(m, nc), 0), axis=1)
    source = mine // rows
    before = jnp.sum(source[None, :] < source[:, None], axis=1, dtype=jnp.int32)
    place = source * slots + iota(m) - before
    sigma_sj = call(pick_kernel, f32(m, w), [VMEM] * 2, place[:, None], got)

    wd = w // 2
    pair = jnp.concatenate([u_panel, from_x[0]], axis=0)
    pair = jnp.where(jnp.bitwise_and(c, 1) == 0, pair[:, :wd], pair[:, wd:])
    u_parts, u_where = [], []
    for t, flip, block in spread(pair, "prow", nr):
        u_parts.append(block)
        u_where.append(jnp.bitwise_xor(jnp.mod(r - 2 * t, nr), flip))
    other = swap(sigma_sj, "pcol", nc)
    parts = call(
        correction_kernel,
        f32(nr, wd, w),
        [SMEM] + [VMEM] * (2 + nr),
        jnp.stack(u_where),
        sigma_sj,
        other,
        *u_parts,
    )
    groups = [[2 * k + x for k in range(nz)] for x in range(2)]
    terms = lax.all_to_all(parts, "pcol", split_axis=0, concat_axis=0, axis_index_groups=groups, tiled=True)
    return sigma_sj, d_term - jnp.sum(terms, axis=0)


def solution(mesh):
    placed = (P("pcol", "prow"), P(), P("pcol", "prow"), P("pcol", "prow"))
    return jax.shard_map(
        per_device,
        mesh=mesh,
        in_specs=placed,
        out_specs=(P("pcol", "prow"), P("pcol", "prow")),
        check_vma=False,
    )
```

```python
import functools

import jax
import jax.numpy as jnp
from jax import lax
from jax.experimental import pallas as pl
from jax.experimental.pallas import tpu as pltpu
from jax.sharding import PartitionSpec as P

LANES = 128
BLOCK_CAP = 560
CAP = -(-BLOCK_CAP // 64) * 64
FULL = CAP // LANES
WIDE = (FULL + 1) * LANES
BF16 = jnp.bfloat16
VMEM = pl.BlockSpec(memory_space=pltpu.VMEM)


def f32(*shape):
    return jax.ShapeDtypeStruct(shape, jnp.float32)


def bf16(*shape):
    return jax.ShapeDtypeStruct(shape, BF16)


def split(v):
    high = v.astype(BF16)
    return high, (v - high.astype(jnp.float32)).astype(BF16)


def split3(v):
    high = v.astype(BF16)
    mid, low = split(v - high.astype(jnp.float32))
    return high, mid, low


def dot(a, b):
    return jnp.dot(a, b, preferred_element_type=jnp.float32)


def pick_rows(place, v):
    high, mid, low = split3(v)
    return dot(place, high) + (dot(place, mid) + dot(place, low))


def one_hot(mask):
    return jnp.where(mask, 1.0, 0.0)


def count(mask):
    return jnp.sum(jnp.where(mask, 1.0, 0.0)).astype(jnp.int32)


def log2(size):
    return size.bit_length() - 1


def each(refs, owners, fn):
    if owners is None:
        pl.loop(0, refs[0].shape[0])(lambda i: fn(i, refs[0].at[i]))
    else:
        for owner, ref in zip(owners, refs):
            fn(owner, ref)


def select_kernel(structure_ref, sigma_ref, out_ref, place_ref):
    step, steps = pl.program_id(0), pl.num_programs(0)
    part, cols = sigma_ref.shape
    n = structure_ref.shape[1]
    rows = out_ref.shape[0] * LANES // CAP

    @pl.when(step == 0)
    def _():
        first = lax.axis_index("prow") * cols
        names = jnp.broadcast_to(structure_ref[...], (8, n))
        shift = lax.rem(n - count(structure_ref[...] < first), n)
        named = pltpu.roll(names, shift, 1)[:1, :CAP] - first
        named = jnp.concatenate([named, named[:, FULL * LANES :]], axis=1)
        at = lax.broadcasted_iota(jnp.int32, (cols, WIDE), 0)
        place_ref[...] = one_hot(at == named).astype(BF16)

    high, low = split(sigma_ref[...])
    place = place_ref[...]
    picked = dot(high, place) + dot(low, place)
    start = step * part
    for i in range(FULL):
        where = pl.multiple_of(rows * i + start, 8)
        out_ref[pl.ds(where, part), :] = picked[:, LANES * i : LANES * (i + 1)]

    @pl.when(step < steps // 2)
    def _():
        where = pl.multiple_of(rows * FULL + start, 8)
        out_ref[pl.ds(where, part), : LANES // 2] = picked[:, FULL * LANES : CAP]

    @pl.when(step >= steps // 2)
    def _():
        where = pl.multiple_of(rows * FULL + start - rows // 2, 8)
        out_ref[pl.ds(where, part), LANES // 2 :] = picked[:, CAP:]


def block_term(block_ref, uh, ul, rows):
    parts = [block_ref[rows * i : rows * (i + 1), :] for i in range(FULL)]
    tail = block_ref[rows * FULL : rows * FULL + rows // 2, :]
    parts.append(jnp.concatenate([tail, pltpu.roll(tail, LANES // 2, 1)], axis=0))
    halves = [split(p) for p in parts]
    highs, lows = [h for h, _ in halves], [l for _, l in halves]
    left = jnp.concatenate(highs + highs + lows, axis=1)
    return dot(left, jnp.concatenate([uh, ul, uh], axis=0))


def prepare_kernel(direct, slots, nr, offsets, n_first, owners, structure_ref, turned_ref, *refs):
    uh_ref, ul_ref, part_ref, to_ref, from_ref, us_ref = refs[-6:]
    m, nc = turned_ref.shape
    w = uh_ref.shape[2]
    n = m * nc
    c = lax.axis_index("pcol")
    r = lax.axis_index("prow")
    z = c // 2
    u_refs = refs[: -6 - n_first] if n_first else refs[:-6]
    first_refs = refs[-6 - n_first : -6]
    rows = part_ref.shape[0]
    names = structure_ref[...]

    def place(owner, u_ref):
        u = u_ref[...]
        if w % LANES:
            u = jnp.concatenate([u, jnp.zeros((m, LANES - w % LANES), jnp.float32)], axis=1)
        for i in range(us_ref.shape[0]):
            us_ref[i, pl.ds(owner, m, stride=nc), :] = u[:, LANES * i : LANES * (i + 1)]

    if direct:
        for (dz, flip), u_ref in zip(offsets, u_refs):
            pl.when((z + dz >= 0) & (z + dz < nc // 2))(
                functools.partial(place, jnp.bitwise_xor(c + 2 * dz, flip), u_ref)
            )
    else:
        each(u_refs, None, place)
    us_ref[:, n:, :] = jnp.zeros((us_ref.shape[0], us_ref.shape[1] - n, LANES), jnp.float32)

    width = rows * 2

    def cut(owner):
        start = count(names < owner * width)
        base = pl.multiple_of((start // 8) * 8, 8)
        size = CAP + 8
        lanes = [
            pltpu.roll(us_ref[k, pl.ds(base, size), :], size - (start - base), 0)[:CAP]
            for k in range(us_ref.shape[0])
        ]
        u = jnp.concatenate(lanes, axis=1)[:, :w]
        u = jnp.concatenate([u, jnp.zeros((WIDE - CAP, w), jnp.float32)], axis=0)
        uh_ref[owner], ul_ref[owner] = split(u)

    if direct:
        for b in range(nr):
            cut(b)
    else:
        pl.loop(0, nr)(cut)
    image = jnp.zeros((rows, w), jnp.float32)
    for owner, block_ref in zip(owners(r), first_refs):
        image = image + block_term(block_ref, uh_ref[owner], ul_ref[owner], rows)
    part_ref[...] = image

    lg = log2(nc)
    row = c * rows + lax.broadcasted_iota(jnp.int32, (rows, n), 0)
    rank = jnp.sum(one_hot(names < row), axis=1, keepdims=True).astype(jnp.int32)
    member = jnp.sum(one_hot(names == row), axis=1, keepdims=True)
    turn = rank & (nc - 1)
    ahead = (count(names < c * rows) - turn + nc - 1) >> lg
    block = turn
    if direct:
        block = 2 * (((turn >> 1) - z) & (nc // 2 - 1)) + ((turn ^ c) & 1)
    slot = jnp.where(member > 0.5, block * slots + (rank >> lg) - ahead, -1)
    at = lax.broadcasted_iota(jnp.int32, (rows, nc * slots), 1)
    to_ref[...] = one_hot(at == slot).T.astype(BF16)

    lane = lax.broadcasted_iota(jnp.int32, (m, nc), 1)
    mine = jnp.sum(jnp.where(lane == c, turned_ref[...], 0).astype(jnp.float32), axis=1, keepdims=True)
    source = jnp.zeros((m, 1), jnp.int32)
    before = jnp.zeros((m, 1), jnp.int32)
    for k in range(1, nc):
        less = mine < float(k * rows)
        source = source + jnp.where(less, 0, 1)
        before = jnp.where(less, before, count(less))
    block = source
    if direct:
        block = 2 * ((z - (source >> 1)) & (nc // 2 - 1)) + ((source ^ c) & 1)
    slot = block * slots + lax.broadcasted_iota(jnp.int32, (m, 1), 0) - before
    at = lax.broadcasted_iota(jnp.int32, (m, nc * slots), 1)
    from_ref[...] = one_hot(at == slot).astype(BF16)


def image_kernel(n_out, owners, uh_ref, ul_ref, part_ref, to_ref, *refs):
    block_refs, out_refs = refs[:-n_out], refs[-n_out:]
    rows = part_ref.shape[0]
    if owners is None:
        stack = block_refs[0]
        add = lambda b, v: v + block_term(stack.at[b], uh_ref[b], ul_ref[b], rows)
        image = lax.fori_loop(0, stack.shape[0], add, part_ref[...])
    else:
        image = part_ref[...]
        for owner, block_ref in zip(owners(lax.axis_index("prow")), block_refs):
            image = image + block_term(block_ref, uh_ref[owner], ul_ref[owner], rows)
    image = pick_rows(to_ref[...], image)
    size = image.shape[0] // n_out
    for k, out_ref in enumerate(out_refs):
        out_ref[...] = image[size * k : size * (k + 1)]


def pick_kernel(from_ref, *refs):
    got = [ref[...] for ref in refs[:-1]]
    got = jnp.concatenate(got, axis=0) if len(got) > 1 else got[0]
    refs[-1][...] = -pick_rows(from_ref[...], got)


def turn_kernel(direct, owners, *refs):
    high_ref, low_ref = refs[-2:]
    z = lax.axis_index("pcol") // 2

    def put(owner, u_ref):
        where = ((owner - z) & (high_ref.shape[0] - 1)) if direct else owner
        high_ref[where], low_ref[where] = split(u_ref[...].T)

    each(refs[:-2], owners(lax.axis_index("prow")) if direct else None, put)


def correction_kernel(high_ref, low_ref, mine_ref, other_ref, *out_refs):
    sh, sl = split(jnp.concatenate([mine_ref[...], other_ref[...]], axis=0))
    nz = high_ref.shape[0]

    def term(t):
        return dot(high_ref[t], sh) + (dot(high_ref[t], sl) + dot(low_ref[t], sh))

    if len(out_refs) > 1:
        for t, out_ref in enumerate(out_refs):
            out_ref[...] = term(t)
    else:

        @pl.loop(0, nz)
        def _(t):
            out_refs[0][t] = term(t)


def call(kernel, out_shape, *args, **kw):
    many = isinstance(out_shape, (list, tuple))
    kw = {"in_specs": [VMEM] * len(args)} | kw
    return pl.pallas_call(
        kernel,
        out_shape=out_shape,
        out_specs=[VMEM] * len(out_shape) if many else VMEM,
        compiler_params=pltpu.CompilerParams(vmem_limit_bytes=20 * 2**20),
        **kw,
    )(*args)


def swap(v, axis, size):
    return lax.ppermute(v, axis, [(k, k ^ 1) for k in range(size)])


def spread(v, size):
    blocks = [v, swap(v, "prow", size)]
    for t in range(1, size // 2):
        far = lax.ppermute(v, "prow", [(k, (k + 2 * t) % size) for k in range(size)])
        blocks += [far, swap(far, "prow", size)]
    return blocks


def relative_owners(size, r):
    out = []
    for t in range(size // 2):
        owner = (r - 2 * t) & (size - 1)
        out += [owner, owner ^ 1]
    return out


def line_gather(u, nc):
    nz = nc // 2
    across = lambda v, ks: lax.ppermute(v, "pcol", [(2 * k + x, 2 * k + 1 - x) for k in ks for x in range(2)])
    along = lambda v, ks, by: lax.ppermute(v, "pcol", [(2 * k + x, 2 * (k + by) + x) for k in ks for x in range(2)])
    offsets, blocks = [(0, 0), (0, 1)], [u, across(u, range(nz))]
    up = down = u
    for t in range(1, nz):
        up = along(up, range(t - 1, nz - 1), 1)
        down = along(down, range(1, nz - t + 1), -1)
        offsets += [(-t, 0), (t, 0), (-t, 1), (t, 1)]
        blocks += [up, down, across(up, range(t, nz)), across(down, range(0, nz - t))]
    return offsets, blocks


def per_device(sigma_top, structure, u_panel, d_term):
    nc, nr = lax.axis_size("pcol"), lax.axis_size("prow")
    c = lax.axis_index("pcol")
    nz = nc // 2
    rows, cols = sigma_top.shape
    m, w = u_panel.shape
    n = structure.shape[0]
    slots = -(-rows // nc)
    direct = nc <= 8
    n_first = 2 if direct else 0
    names = structure.reshape(1, n)
    steps = 4
    part = rows // steps

    if direct:
        offsets, u_blocks = line_gather(u_panel, nc)
        partner = u_blocks[1]
    else:
        offsets, u_blocks = None, [lax.all_gather(u_panel, "pcol")]
        partner = swap(u_panel, "pcol", nc)

    chosen = call(
        select_kernel,
        f32(rows * CAP // LANES, LANES),
        names,
        sigma_top,
        grid=(steps,),
        in_specs=[pl.BlockSpec((1, n), lambda i: (0, 0)), pl.BlockSpec((part, cols), lambda i: (i, 0))],
        scratch_shapes=[pltpu.VMEM((cols, WIDE), BF16)],
    )
    near = [chosen, swap(chosen, "prow", nr)] if direct else []
    owners = functools.partial(relative_owners, nr)
    uh, ul, image, to, source = call(
        functools.partial(
            prepare_kernel, direct, slots, nr, offsets, n_first, lambda r: owners(r)[:2]
        ),
        [bf16(nr, WIDE, w), bf16(nr, WIDE, w), f32(rows, w), bf16(nc * slots, rows), bf16(m, nc * slots)],
        names,
        structure.reshape(m, nc),
        *u_blocks,
        *near,
        scratch_shapes=[pltpu.VMEM((-(-w // LANES), n + CAP + 8, LANES), jnp.float32)],
    )

    if direct:
        later = []
        for t in range(1, nr // 2):
            far = lax.ppermute(chosen, "prow", [(k, (k + 2 * t) % nr) for k in range(nr)])
            far, image = lax.optimization_barrier((far, image))
            later += [far, swap(far, "prow", nr)]
    else:
        later = [lax.all_gather(chosen, "prow")]
    n_out = nc if direct else 1
    sent = call(
        functools.partial(image_kernel, n_out, (lambda r: owners(r)[2:]) if direct else None),
        [f32(nc * slots // n_out, w)] * n_out,
        uh,
        ul,
        image,
        to,
        *later,
    )
    if direct:
        got = [sent[0]]
        for k in range(1, nc):
            got.append(lax.ppermute(sent[k], "pcol", [(i, ((i + 2 * (k // 2)) % nc) ^ (k % 2)) for i in range(nc)]))
    else:
        got = [lax.all_to_all(sent[0], "pcol", split_axis=0, concat_axis=0, tiled=True)]
    sigma_sj = call(pick_kernel, f32(m, w), source, *got)

    wd = w // 2
    pair = jnp.concatenate([u_panel, partner], axis=0)
    pair = jnp.where(jnp.bitwise_and(c, 1) == 0, pair[:, :wd], pair[:, wd:])
    if direct:
        pair, later[0] = lax.optimization_barrier((pair, later[0]))
        pairs = spread(pair, nr)
    else:
        pairs = [lax.all_gather(pair, "prow")]
    turned = call(
        functools.partial(turn_kernel, direct, owners), [bf16(nz, wd, 2 * m), bf16(nz, wd, 2 * m)], *pairs
    )
    other = swap(sigma_sj, "pcol", nc)
    if direct:
        terms = call(correction_kernel, [f32(wd, w)] * nz, *turned, sigma_sj, other)
        total = terms[0]
        for t in range(1, nz):
            total = total + lax.ppermute(terms[t], "pcol", [(k, (k + 2 * t) % nc) for k in range(nc)])
    else:
        terms = call(correction_kernel, f32(nz, wd, w), *turned, sigma_sj, other)
        groups = [[2 * k + x for k in range(nz)] for x in range(2)]
        terms = lax.all_to_all(terms, "pcol", split_axis=0, concat_axis=0, axis_index_groups=groups, tiled=True)
        total = jnp.sum(terms, axis=0)
    return sigma_sj, d_term - total


def solution(mesh):
    placed = (P("pcol", "prow"), P(), P("pcol", "prow"), P("pcol", "prow"))
    return jax.shard_map(
        per_device,
        mesh=mesh,
        in_specs=placed,
        out_specs=(P("pcol", "prow"), P("pcol", "prow")),
        check_vma=False,
    )
```

```python
import functools

import jax
import jax.numpy as jnp
from jax import lax
from jax.experimental import pallas as pl
from jax.experimental.pallas import tpu as pltpu
from jax.sharding import PartitionSpec as P

LANES = 128
BLOCK_CAP = 560
CAP = -(-BLOCK_CAP // 64) * 64
FULL = CAP // LANES
WIDE = (FULL + 1) * LANES
BF16 = jnp.bfloat16
VMEM = pl.BlockSpec(memory_space=pltpu.VMEM)


def f32(*shape):
    return jax.ShapeDtypeStruct(shape, jnp.float32)


def bf16(*shape):
    return jax.ShapeDtypeStruct(shape, BF16)


def split(v):
    high = v.astype(BF16)
    return high, (v - high.astype(jnp.float32)).astype(BF16)


def split3(v):
    high = v.astype(BF16)
    mid, low = split(v - high.astype(jnp.float32))
    return high, mid, low


def dot(a, b):
    return jnp.dot(a, b, preferred_element_type=jnp.float32)


def pick_rows(place, v):
    high, mid, low = split3(v)
    return dot(place, high) + (dot(place, mid) + dot(place, low))


def one_hot(mask):
    return jnp.where(mask, 1.0, 0.0)


def count(mask):
    return jnp.sum(jnp.where(mask, 1.0, 0.0)).astype(jnp.int32)


def log2(size):
    return size.bit_length() - 1


def each(refs, owners, fn):
    if owners is None:
        pl.loop(0, refs[0].shape[0])(lambda i: fn(i, refs[0].at[i]))
    else:
        for owner, ref in zip(owners, refs):
            fn(owner, ref)


def select_kernel(structure_ref, sigma_ref, out_ref, place_ref):
    step, steps = pl.program_id(0), pl.num_programs(0)
    part, cols = sigma_ref.shape
    n = structure_ref.shape[1]
    rows = out_ref.shape[0] * LANES // CAP

    @pl.when(step == 0)
    def _():
        first = lax.axis_index("prow") * cols
        names = jnp.broadcast_to(structure_ref[...], (8, n))
        shift = lax.rem(n - count(structure_ref[...] < first), n)
        named = pltpu.roll(names, shift, 1)[:1, :CAP] - first
        named = jnp.concatenate([named, named[:, FULL * LANES :]], axis=1)
        at = lax.broadcasted_iota(jnp.int32, (cols, WIDE), 0)
        place_ref[...] = one_hot(at == named).astype(BF16)

    high, low = split(sigma_ref[...])
    place = place_ref[...]
    picked = dot(high, place) + dot(low, place)
    start = step * part
    for i in range(FULL):
        where = pl.multiple_of(rows * i + start, 8)
        out_ref[pl.ds(where, part), :] = picked[:, LANES * i : LANES * (i + 1)]

    @pl.when(step < steps // 2)
    def _():
        where = pl.multiple_of(rows * FULL + start, 8)
        out_ref[pl.ds(where, part), : LANES // 2] = picked[:, FULL * LANES : CAP]

    @pl.when(step >= steps // 2)
    def _():
        where = pl.multiple_of(rows * FULL + start - rows // 2, 8)
        out_ref[pl.ds(where, part), LANES // 2 :] = picked[:, CAP:]


def block_term(block_ref, uh, ul, rows):
    parts = [block_ref[rows * i : rows * (i + 1), :] for i in range(FULL)]
    tail = block_ref[rows * FULL : rows * FULL + rows // 2, :]
    parts.append(jnp.concatenate([tail, pltpu.roll(tail, LANES // 2, 1)], axis=0))
    halves = [split(p) for p in parts]
    highs, lows = [h for h, _ in halves], [l for _, l in halves]
    left = jnp.concatenate(highs + highs + lows, axis=1)
    return dot(left, jnp.concatenate([uh, ul, uh], axis=0))


def prepare_kernel(direct, slots, owners, structure_ref, *refs):
    pair_ref = None
    if direct:
        pair_ref, refs = refs[-2], refs[:-2] + refs[-1:]
    uh_ref, ul_ref, part_ref, to_ref, us_ref = refs[-5:]
    nr, _, w = uh_ref.shape
    nc = to_ref.shape[0] // slots
    n_u = nc if direct else 1
    u_refs, first_refs = refs[:n_u], refs[n_u:-5]
    n = structure_ref.shape[1]
    m = n // nc
    c = lax.axis_index("pcol")
    r = lax.axis_index("prow")
    z = c // 2
    rows = part_ref.shape[0]
    names = structure_ref[...]

    def place(owner, u):
        if w % LANES:
            u = jnp.concatenate([u, jnp.zeros((m, LANES - w % LANES), jnp.float32)], axis=1)
        for i in range(us_ref.shape[0]):
            us_ref[i, pl.ds(owner, u.shape[0], stride=nc), :] = u[:, LANES * i : LANES * (i + 1)]

    if direct:
        lane = pl.multiple_of((c & 1) * (w // 2), LANES)
        pair_ref[:m, :] = u_refs[0][:, pl.ds(lane, w // 2)]
        for owner, u_ref in zip(ring_owners(nc, c), u_refs):
            place(owner, u_ref[...])

            @pl.when(owner == jnp.bitwise_xor(c, 1))
            def _():
                pair_ref[m:, :] = u_ref[:, pl.ds(lane, w // 2)]

    else:
        pl.loop(0, nc)(lambda k: place(k, u_refs[0][k]))
    us_ref[:, n:, :] = jnp.zeros((us_ref.shape[0], us_ref.shape[1] - n, LANES), jnp.float32)

    width = rows * 2

    def cut(owner):
        start = count(names < owner * width)
        base = pl.multiple_of((start // 8) * 8, 8)
        size = CAP + 8
        lanes = [
            pltpu.roll(us_ref[k, pl.ds(base, size), :], size - (start - base), 0)[:CAP]
            for k in range(us_ref.shape[0])
        ]
        u = jnp.concatenate(lanes, axis=1)[:, :w]
        u = jnp.concatenate([u, jnp.zeros((WIDE - CAP, w), jnp.float32)], axis=0)
        uh_ref[owner], ul_ref[owner] = split(u)

    if direct:
        for b in range(nr):
            cut(b)
    else:
        pl.loop(0, nr)(cut)
    image = jnp.zeros((rows, w), jnp.float32)
    for owner, block_ref in zip(owners(r), first_refs):
        image = image + block_term(block_ref, uh_ref[owner], ul_ref[owner], rows)
    part_ref[...] = image

    lg = log2(nc)
    row = c * rows + lax.broadcasted_iota(jnp.int32, (rows, n), 0)
    rank = jnp.sum(one_hot(names < row), axis=1, keepdims=True).astype(jnp.int32)
    member = jnp.sum(one_hot(names == row), axis=1, keepdims=True)
    turn = rank & (nc - 1)
    ahead = (count(names < c * rows) - turn + nc - 1) >> lg
    block = turn >> 1
    if direct:
        block = (block - z) & (nc // 2 - 1)
    block = 2 * block + (turn & 1)
    slot = jnp.where(member > 0.5, block * slots + (rank >> lg) - ahead, -1)
    at = lax.broadcasted_iota(jnp.int32, (rows, nc * slots), 1)
    to_ref[...] = one_hot(at == slot).T.astype(BF16)


def image_kernel(n_out, owners, uh_ref, ul_ref, part_ref, to_ref, *refs):
    block_refs, out_refs = refs[:-n_out], refs[-n_out:]
    rows = part_ref.shape[0]
    if owners is None:
        stack = block_refs[0]
        add = lambda b, v: v + block_term(stack.at[b], uh_ref[b], ul_ref[b], rows)
        image = lax.fori_loop(0, stack.shape[0], add, part_ref[...])
    else:
        image = part_ref[...]
        for owner, block_ref in zip(owners(lax.axis_index("prow")), block_refs):
            image = image + block_term(block_ref, uh_ref[owner], ul_ref[owner], rows)
    image = pick_rows(to_ref[...], image)
    size = image.shape[0] // n_out
    for k, out_ref in enumerate(out_refs):
        out_ref[...] = image[size * k : size * (k + 1)]


def turn_kernel(direct, slots, owners, structure_ref, *refs):
    from_ref, high_ref, low_ref = refs[-3:]
    nz = high_ref.shape[0]
    nc = 2 * nz
    rows = slots * nc
    n = structure_ref.shape[1]
    m = n // nc
    names = structure_ref[...]
    c = lax.axis_index("pcol")
    z = c // 2

    def put(owner, u_ref):
        where = ((owner - z) & (nz - 1)) if direct else owner
        high_ref[where], low_ref[where] = split(u_ref[...].T)

    each(refs[:-3], owners(lax.axis_index("prow")) if direct else None, put)

    own = lax.broadcasted_iota(jnp.int32, (m, n), 1) - nc * lax.broadcasted_iota(jnp.int32, (m, n), 0)
    at = lax.broadcasted_iota(jnp.int32, (m, 2 * rows), 1)
    for half, column in enumerate((c, jnp.bitwise_xor(c, 1))):
        mine = jnp.where(own == column, names, 0).astype(jnp.float32)
        mine = jnp.sum(mine, axis=1, keepdims=True)
        source = jnp.zeros((m, 1), jnp.int32)
        before = jnp.zeros((m, 1), jnp.int32)
        for k in range(1, nc):
            less = mine < float(k * rows)
            source = source + jnp.where(less, 0, 1)
            before = jnp.where(less, before, count(less))
        block = source >> 1
        if direct:
            block = (z - block) & (nz - 1)
        block = 2 * (block + nz * ((source ^ c) & 1)) + (column & 1)
        slot = block * slots + lax.broadcasted_iota(jnp.int32, (m, 1), 0) - before
        from_ref[m * half : m * (half + 1), :] = one_hot(at == slot).astype(BF16)


def correction_kernel(from_ref, high_ref, low_ref, *refs):
    nz = high_ref.shape[0]
    n_in = 2 if len(refs) == 4 else 2 * nz
    got = jnp.concatenate([ref[...] for ref in refs[:n_in]], axis=0)
    sj_ref, out_refs = refs[n_in], refs[n_in + 1 :]
    both = -pick_rows(from_ref[...], got)
    sj_ref[...] = both[: sj_ref.shape[0]]
    sh, sl = split(both)

    def term(t):
        return dot(high_ref[t], sh) + (dot(high_ref[t], sl) + dot(low_ref[t], sh))

    if len(out_refs) > 1:
        for t, out_ref in enumerate(out_refs):
            out_ref[...] = term(t)
    else:

        @pl.loop(0, nz)
        def _(t):
            out_refs[0][t] = term(t)


def call(kernel, out_shape, *args, **kw):
    many = isinstance(out_shape, (list, tuple))
    kw = {"in_specs": [VMEM] * len(args)} | kw
    return pl.pallas_call(
        kernel,
        out_shape=out_shape,
        out_specs=[VMEM] * len(out_shape) if many else VMEM,
        compiler_params=pltpu.CompilerParams(vmem_limit_bytes=20 * 2**20),
        **kw,
    )(*args)


def swap(v, axis, size):
    return lax.ppermute(v, axis, [(k, k ^ 1) for k in range(size)])


def spread(v, size):
    blocks = [v, swap(v, "prow", size)]
    for t in range(1, size // 2):
        far = lax.ppermute(v, "prow", [(k, (k + 2 * t) % size) for k in range(size)])
        blocks += [far, swap(far, "prow", size)]
    return blocks


def relative_owners(size, r):
    out = []
    for t in range(size // 2):
        owner = (r - 2 * t) & (size - 1)
        out += [owner, owner ^ 1]
    return out


def ring_gather(u, nc):
    ring = [2 * z for z in range(nc // 2)] + [2 * z + 1 for z in reversed(range(nc // 2))]
    pairs = [(ring[q - 1], ring[q]) for q in range(nc)]
    back = [(b, a) for a, b in pairs]
    blocks = [u]
    up = down = u
    for step in range(1, nc // 2):
        up, down = lax.ppermute(up, "pcol", pairs), lax.ppermute(down, "pcol", back)
        blocks += [up, down]
    return blocks + [lax.ppermute(up, "pcol", pairs)]


def ring_owners(nc, c):
    q = jnp.where((c & 1) == 0, c >> 1, nc - 1 - (c >> 1))
    out = []
    for k in range(nc):
        step = (k + 1) // 2
        at = (q - step if k % 2 else q + step) & (nc - 1)
        out.append(jnp.where(at < nc // 2, 2 * at, 2 * (nc - 1 - at) + 1))
    return out


def per_device(sigma_top, structure, u_panel, d_term):
    nc, nr = lax.axis_size("pcol"), lax.axis_size("prow")
    c = lax.axis_index("pcol")
    nz = nc // 2
    rows, cols = sigma_top.shape
    m, w = u_panel.shape
    wd = w // 2
    n = structure.shape[0]
    slots = -(-rows // nc)
    direct = nc <= 8
    names = structure.reshape(1, n)
    steps = 4
    part = rows // steps
    groups = [[2 * k + x for k in range(nz)] for x in range(2)]
    owners = functools.partial(relative_owners, nr)

    chosen = call(
        select_kernel,
        f32(rows * CAP // LANES, LANES),
        names,
        sigma_top,
        grid=(steps,),
        in_specs=[pl.BlockSpec((1, n), lambda i: (0, 0)), pl.BlockSpec((part, cols), lambda i: (i, 0))],
        scratch_shapes=[pltpu.VMEM((cols, WIDE), BF16)],
    )
    near = [chosen, swap(chosen, "prow", nr)] if direct else []
    if direct:
        u_all = ring_gather(u_panel, nc)
    else:
        u_all = [lax.all_gather(u_panel, "pcol")]
    out = [bf16(nr, WIDE, w), bf16(nr, WIDE, w), f32(rows, w), bf16(nc * slots, rows)]
    if direct:
        out.append(f32(2 * m, wd))
    uh, ul, image, to, *pair = call(
        functools.partial(prepare_kernel, direct, slots, lambda r: owners(r)[:2]),
        out,
        names,
        *u_all,
        *near,
        scratch_shapes=[pltpu.VMEM((-(-w // LANES), n + CAP + 8, LANES), jnp.float32)],
    )

    if direct:
        later = []
        for t in range(1, nr // 2):
            far = lax.ppermute(chosen, "prow", [(k, (k + 2 * t) % nr) for k in range(nr)])
            far, image = lax.optimization_barrier((far, image))
            later += [far, swap(far, "prow", nr)]
        pair, later[0] = lax.optimization_barrier((pair[0], later[0]))
        pairs = spread(pair, nr)
    else:
        later = [lax.all_gather(chosen, "prow")]
        pair = jnp.concatenate([u_panel, swap(u_panel, "pcol", nc)], axis=0)
        pair = jnp.where(jnp.bitwise_and(c, 1) == 0, pair[:, :wd], pair[:, wd:])
        pairs = [lax.all_gather(pair, "prow")]
    n_out = nz if direct else 1
    sent = call(
        functools.partial(image_kernel, n_out, (lambda r: owners(r)[2:]) if direct else None),
        [f32(nc * slots // n_out, w)] * n_out,
        uh,
        ul,
        image,
        to,
        *later,
    )
    if direct:
        got = [sent[0]]
        for t in range(1, nz):
            got.append(lax.ppermute(sent[t], "pcol", [(k, (k + 2 * t) % nc) for k in range(nc)]))
    else:
        blocks = sent[0].reshape(nz, 2 * slots, w)
        blocks = lax.all_to_all(blocks, "pcol", split_axis=0, concat_axis=0, axis_index_groups=groups, tiled=True)
        got = [blocks.reshape(nc * slots, w)]
    got = got + [swap(v, "pcol", nc) for v in got]

    source, high, low = call(
        functools.partial(turn_kernel, direct, slots, owners),
        [bf16(2 * m, 2 * nc * slots), bf16(nz, wd, 2 * m), bf16(nz, wd, 2 * m)],
        names,
        *pairs,
    )
    parts = [f32(wd, w)] * nz if direct else [f32(nz, wd, w)]
    sigma_sj, *terms = call(correction_kernel, [f32(m, w)] + parts, source, high, low, *got)
    if direct:
        total = terms[0]
        for t in range(1, nz):
            total = total + lax.ppermute(terms[t], "pcol", [(k, (k + 2 * t) % nc) for k in range(nc)])
    else:
        terms = lax.all_to_all(terms[0], "pcol", split_axis=0, concat_axis=0, axis_index_groups=groups, tiled=True)
        total = jnp.sum(terms, axis=0)
    return sigma_sj, d_term - total


def solution(mesh):
    placed = (P("pcol", "prow"), P(), P("pcol", "prow"), P("pcol", "prow"))
    return jax.shard_map(
        per_device,
        mesh=mesh,
        in_specs=placed,
        out_specs=(P("pcol", "prow"), P("pcol", "prow")),
        check_vma=False,
    )
```

```python
import functools

import jax
import jax.numpy as jnp
from jax import lax
from jax.experimental import pallas as pl
from jax.experimental.pallas import tpu as pltpu
from jax.sharding import PartitionSpec as P

LANES = 128
BLOCK_CAP = 560
CAP = -(-BLOCK_CAP // 64) * 64
FULL = CAP // LANES
WIDE = (FULL + 1) * LANES
BF16 = jnp.bfloat16
VMEM = pl.BlockSpec(memory_space=pltpu.VMEM)
HBM = pl.BlockSpec(memory_space=pltpu.HBM)


def f32(*shape):
    return jax.ShapeDtypeStruct(shape, jnp.float32)


def bf16(*shape):
    return jax.ShapeDtypeStruct(shape, BF16)


def split(v):
    high = v.astype(BF16)
    return high, (v - high.astype(jnp.float32)).astype(BF16)


def split3(v):
    high = v.astype(BF16)
    mid, low = split(v - high.astype(jnp.float32))
    return high, mid, low


def dot(a, b):
    return jnp.dot(a, b, preferred_element_type=jnp.float32)


def pick_rows(place, v):
    high, mid, low = split3(v)
    return dot(place, high) + (dot(place, mid) + dot(place, low))


def one_hot(mask):
    return jnp.where(mask, 1.0, 0.0)


def count(mask):
    return jnp.sum(jnp.where(mask, 1.0, 0.0)).astype(jnp.int32)


def log2(size):
    return size.bit_length() - 1


def each(refs, owners, fn):
    if owners is None:
        pl.loop(0, refs[0].shape[0])(lambda i: fn(i, refs[0].at[i]))
    else:
        for owner, ref in zip(owners, refs):
            fn(owner, ref)


def select_kernel(structure_ref, sigma_ref, u_ref, out_ref, top_ref, low_ref, held_ref, sems):
    rows, cols = held_ref.shape
    n = structure_ref.shape[1]
    parts = sems.shape[0] - 2
    part = rows // parts
    copies = []
    for k in range(parts):
        at = pl.ds(part * k, part)
        copies.append(pltpu.make_async_copy(sigma_ref.at[at, :], held_ref.at[at, :], sems.at[k]))
        copies[-1].start()
    half = top_ref.shape[0]
    halves = []
    for k, ref in enumerate((top_ref, low_ref)):
        halves.append(pltpu.make_async_copy(u_ref.at[pl.ds(half * k, half), :], ref, sems.at[parts + k]))
        halves[-1].start()
    first = lax.axis_index("prow") * cols
    names = jnp.broadcast_to(structure_ref[...], (8, n))
    shift = lax.rem(n - count(structure_ref[...] < first), n)
    named = pltpu.roll(names, shift, 1)[:1, :CAP] - first
    named = jnp.concatenate([named, named[:, FULL * LANES :]], axis=1)
    at = lax.broadcasted_iota(jnp.int32, (cols, WIDE), 0)
    place = one_hot(at == named).astype(BF16)
    for k in range(parts):
        copies[k].wait()
        high, low = split(held_ref[part * k : part * (k + 1), :])
        picked = dot(high, place) + dot(low, place)
        for i in range(FULL):
            at = rows * i + part * k
            out_ref[at : at + part, :] = picked[:, LANES * i : LANES * (i + 1)]
        at = rows * FULL + part * (k % (parts // 2))
        if k < parts // 2:
            out_ref[at : at + part, : LANES // 2] = picked[:, FULL * LANES : CAP]
        else:
            out_ref[at : at + part, LANES // 2 :] = picked[:, CAP:]
    for copy in halves:
        copy.wait()


def block_term(block_ref, uh, ul, rows):
    parts = [block_ref[rows * i : rows * (i + 1), :] for i in range(FULL)]
    tail = block_ref[rows * FULL : rows * FULL + rows // 2, :]
    parts.append(jnp.concatenate([tail, pltpu.roll(tail, LANES // 2, 1)], axis=0))
    halves = [split(p) for p in parts]
    highs, lows = [h for h, _ in halves], [l for _, l in halves]
    left = jnp.concatenate(highs + highs + lows, axis=1)
    return dot(left, jnp.concatenate([uh, ul, uh], axis=0))


def prepare_kernel(direct, nc, owners, structure_ref, *refs):
    pair_ref = None
    if direct:
        pair_ref, refs = refs[-2], refs[:-2] + refs[-1:]
    uh_ref, ul_ref, part_ref, us_ref = refs[-4:]
    nr, _, w = uh_ref.shape
    n_u = 2 * nc if direct else 1
    u_refs, first_refs = refs[:n_u], refs[n_u:-4]
    n = structure_ref.shape[1]
    m = n // nc
    c = lax.axis_index("pcol")
    r = lax.axis_index("prow")
    rows = part_ref.shape[0]
    names = structure_ref[...]

    def place(owner, u):
        if w % LANES:
            u = jnp.concatenate([u, jnp.zeros((m, LANES - w % LANES), jnp.float32)], axis=1)
        for i in range(us_ref.shape[0]):
            us_ref[i, pl.ds(owner, u.shape[0], stride=nc), :] = u[:, LANES * i : LANES * (i + 1)]

    if direct:
        lane = pl.multiple_of((c & 1) * (w // 2), LANES)
        size = m // 2
        for h in range(2):
            pair_ref[size * h : size * (h + 1), :] = u_refs[h][:, pl.ds(lane, w // 2)]
        for (owner, h), u_ref in zip(ring_owners(nc, c), u_refs):
            place(nc * size * h + owner, u_ref[...])
            at = m + size * h

            @pl.when(owner == jnp.bitwise_xor(c, 1))
            def _():
                pair_ref[at : at + size, :] = u_ref[:, pl.ds(lane, w // 2)]

    else:
        pl.loop(0, nc)(lambda k: place(k, u_refs[0][k]))
    us_ref[:, n:, :] = jnp.zeros((us_ref.shape[0], us_ref.shape[1] - n, LANES), jnp.float32)

    width = rows * 2

    def cut(owner):
        start = count(names < owner * width)
        base = pl.multiple_of((start // 8) * 8, 8)
        size = CAP + 8
        lanes = [
            pltpu.roll(us_ref[k, pl.ds(base, size), :], size - (start - base), 0)[:CAP]
            for k in range(us_ref.shape[0])
        ]
        u = jnp.concatenate(lanes, axis=1)[:, :w]
        u = jnp.concatenate([u, jnp.zeros((WIDE - CAP, w), jnp.float32)], axis=0)
        uh_ref[owner], ul_ref[owner] = split(u)

    if direct:
        for b in range(nr):
            cut(b)
    else:
        pl.loop(0, nr)(cut)
    image = jnp.zeros((rows, w), jnp.float32)
    for owner, block_ref in zip(owners(r), first_refs):
        image = image + block_term(block_ref, uh_ref[owner], ul_ref[owner], rows)
    part_ref[...] = image


def row_order(names, c, rows, nc, slots, direct):
    n = names.shape[1]
    z = c // 2
    lg = log2(nc)
    row = c * rows + lax.broadcasted_iota(jnp.int32, (rows, n), 0)
    rank = jnp.sum(one_hot(names < row), axis=1, keepdims=True).astype(jnp.int32)
    member = jnp.sum(one_hot(names == row), axis=1, keepdims=True)
    turn = rank & (nc - 1)
    ahead = (count(names < c * rows) - turn + nc - 1) >> lg
    block = turn >> 1
    if direct:
        block = (block - z) & (nc // 2 - 1)
    block = 2 * block + (turn & 1)
    slot = jnp.where(member > 0.5, block * slots + (rank >> lg) - ahead, -1)
    at = lax.broadcasted_iota(jnp.int32, (rows, nc * slots), 1)
    return one_hot(at == slot).T.astype(BF16)


def near_kernel(direct, slots, owners, structure_ref, uh_ref, ul_ref, part_ref, *refs):
    block_refs, (image_ref, to_ref) = refs[:-2], refs[-2:]
    rows = part_ref.shape[0]
    image = part_ref[...]
    for owner, block_ref in zip(owners(lax.axis_index("prow")), block_refs):
        image = image + block_term(block_ref, uh_ref[owner], ul_ref[owner], rows)
    image_ref[...] = image
    nc = to_ref.shape[0] // slots
    to_ref[...] = row_order(structure_ref[...], lax.axis_index("pcol"), rows, nc, slots, direct)


def image_kernel(n_out, owners, uh_ref, ul_ref, part_ref, to_ref, *refs):
    block_refs, out_refs = refs[:-n_out], refs[-n_out:]
    rows = part_ref.shape[0]
    image = part_ref[...]
    if owners is None:
        stack = block_refs[0]
        add = lambda b, v: v + block_term(stack.at[b], uh_ref[b], ul_ref[b], rows)
        image = lax.fori_loop(0, stack.shape[0], add, image)
    else:
        for owner, block_ref in zip(owners(lax.axis_index("prow")), block_refs):
            image = image + block_term(block_ref, uh_ref[owner], ul_ref[owner], rows)
    image = pick_rows(to_ref[...], image)
    size = image.shape[0] // n_out
    for k, out_ref in enumerate(out_refs):
        out_ref[...] = image[size * k : size * (k + 1)]


def turn_kernel(direct, slots, owners, structure_ref, *refs):
    from_ref, high_ref, low_ref = refs[-3:]
    nz = high_ref.shape[0]
    nc = 2 * nz
    rows = slots * nc
    n = structure_ref.shape[1]
    m = n // nc
    names = structure_ref[...]
    c = lax.axis_index("pcol")
    z = c // 2

    def put(owner, u_ref):
        where = ((owner - z) & (nz - 1)) if direct else owner
        high_ref[where], low_ref[where] = split(u_ref[...].T)

    each(refs[:-3], owners(lax.axis_index("prow")) if direct else None, put)

    own = lax.broadcasted_iota(jnp.int32, (m, n), 1) - nc * lax.broadcasted_iota(jnp.int32, (m, n), 0)
    at = lax.broadcasted_iota(jnp.int32, (m, 2 * rows), 1)
    for half, column in enumerate((c, jnp.bitwise_xor(c, 1))):
        mine = jnp.where(own == column, names, 0).astype(jnp.float32)
        mine = jnp.sum(mine, axis=1, keepdims=True)
        source = jnp.zeros((m, 1), jnp.int32)
        before = jnp.zeros((m, 1), jnp.int32)
        for k in range(1, nc):
            less = mine < float(k * rows)
            source = source + jnp.where(less, 0, 1)
            before = jnp.where(less, before, count(less))
        block = source >> 1
        if direct:
            block = (z - block) & (nz - 1)
        block = 2 * (block + nz * ((source ^ c) & 1)) + (column & 1)
        slot = block * slots + lax.broadcasted_iota(jnp.int32, (m, 1), 0) - before
        from_ref[m * half : m * (half + 1), :] = one_hot(at == slot).astype(BF16)


def correction_kernel(from_ref, high_ref, low_ref, *refs):
    nz = high_ref.shape[0]
    n_in = 2 if len(refs) == 4 else 2 * nz
    got = jnp.concatenate([ref[...] for ref in refs[:n_in]], axis=0)
    sj_ref, out_refs = refs[n_in], refs[n_in + 1 :]
    both = -pick_rows(from_ref[...], got)
    sj_ref[...] = both[: sj_ref.shape[0]]
    sh, sl = split(both)

    def term(t):
        return dot(high_ref[t], sh) + (dot(high_ref[t], sl) + dot(low_ref[t], sh))

    if len(out_refs) > 1:
        for t, out_ref in enumerate(out_refs):
            out_ref[...] = term(t)
    else:

        @pl.loop(0, nz)
        def _(t):
            out_refs[0][t] = term(t)


def call(kernel, out_shape, *args, flops=0, vmem=20, **kw):
    many = isinstance(out_shape, (list, tuple))
    size = sum(v.size * v.dtype.itemsize for v in jax.tree.leaves((out_shape, args)))
    kw = {"in_specs": [VMEM] * len(args)} | kw
    return pl.pallas_call(
        kernel,
        out_shape=out_shape,
        out_specs=[VMEM] * len(out_shape) if many else VMEM,
        cost_estimate=pl.CostEstimate(flops=flops, bytes_accessed=size, transcendentals=0),
        compiler_params=pltpu.CompilerParams(vmem_limit_bytes=vmem * 2**20),
        **kw,
    )(*args)


def swap(v, axis, size):
    return lax.ppermute(v, axis, [(k, k ^ 1) for k in range(size)])


def spread(v, size, after):
    blocks = [v, swap(v, "prow", size)]
    for t in range(1, size // 2):
        far = lax.ppermute(v, "prow", [(k, (k + 2 * t) % size) for k in range(size)])
        far, _ = lax.optimization_barrier((far, after))
        blocks += [far, swap(far, "prow", size)]
    return blocks


def relative_owners(size, r):
    out = []
    for t in range(size // 2):
        owner = (r - 2 * t) & (size - 1)
        out += [owner, owner ^ 1]
    return out


def ring_gather(halves, nc):
    ring = [2 * z for z in range(nc // 2)] + [2 * z + 1 for z in reversed(range(nc // 2))]
    pairs = [(ring[q - 1], ring[q]) for q in range(nc)]
    back = [(b, a) for a, b in pairs]
    held = [(v, v) for v in halves]
    blocks = list(halves)
    for step in range(1, nc // 2):
        for h in range(2):
            held[h] = lax.ppermute(held[h][0], "pcol", pairs), lax.ppermute(held[h][1], "pcol", back)
            blocks += held[h]
    return blocks + [lax.ppermute(held[0][0], "pcol", pairs), lax.ppermute(held[1][1], "pcol", back)]


def ring_owners(nc, c):
    q = jnp.where((c & 1) == 0, c >> 1, nc - 1 - (c >> 1))
    out = [(c, 0), (c, 1)]
    for step in range(1, nc // 2 + 1):
        for h in range(2):
            for sign in (-1, 1) if step < nc // 2 else (-1,):
                at = (q + sign * step) & (nc - 1)
                out.append((jnp.where(at < nc // 2, 2 * at, 2 * (nc - 1 - at) + 1), h))
    return out


def per_device(sigma_top, structure, u_panel, d_term):
    nc, nr = lax.axis_size("pcol"), lax.axis_size("prow")
    c = lax.axis_index("pcol")
    nz = nc // 2
    rows, cols = sigma_top.shape
    m, w = u_panel.shape
    wd = w // 2
    n = structure.shape[0]
    slots = -(-rows // nc)
    direct = nc <= 8
    names = structure.reshape(1, n)
    groups = [[2 * k + x for k in range(nz)] for x in range(2)]
    owners = functools.partial(relative_owners, nr)

    chosen, *halves = call(
        select_kernel,
        [f32(rows * CAP // LANES, LANES), f32(m // 2, w), f32(m // 2, w)],
        names,
        sigma_top,
        u_panel,
        in_specs=[VMEM, HBM, HBM],
        scratch_shapes=[pltpu.VMEM((rows, cols), jnp.float32), pltpu.SemaphoreType.DMA((6,))],
        flops=4 * rows * cols * WIDE,
        vmem=52,
    )
    near = [chosen, swap(chosen, "prow", nr)] if direct else []
    if direct:
        u_all = ring_gather(halves, nc)
    else:
        u_all = [lax.all_gather(u_panel, "pcol")]
    term = 6 * rows * WIDE * w
    uh, ul, image, *pair = call(
        functools.partial(prepare_kernel, direct, nc, lambda r: owners(r)[:2]),
        [bf16(nr, WIDE, w), bf16(nr, WIDE, w), f32(rows, w)] + [f32(2 * m, wd)] * direct,
        names,
        *u_all,
        *near,
        scratch_shapes=[pltpu.VMEM((-(-w // LANES), n + CAP + 8, LANES), jnp.float32)],
        flops=2 * term,
    )
    beside, later = [], []
    if direct:
        for t in range(1, nr // 2):
            far = lax.ppermute(chosen, "prow", [(k, (k + 2 * t) % nr) for k in range(nr)])
            far, _ = lax.optimization_barrier((far, image))
            beside.append(far)
            later.append(swap(far, "prow", nr))
    else:
        later = [lax.all_gather(chosen, "prow")]
    image, to = call(
        functools.partial(near_kernel, direct, slots, lambda r: owners(r)[2::2]),
        [f32(rows, w), bf16(nc * slots, rows)],
        names,
        uh,
        ul,
        image,
        *beside,
        flops=term,
    )
    n_out = nz if direct else 1
    sent = call(
        functools.partial(image_kernel, n_out, (lambda r: owners(r)[3::2]) if direct else None),
        [f32(nc * slots // n_out, w)] * n_out,
        uh,
        ul,
        image,
        to,
        *later,
        flops=term,
    )
    if direct:
        pair, _ = lax.optimization_barrier((pair[0], beside[0]))
        pairs = spread(pair, nr, sent[0])
    else:
        pair = jnp.concatenate([u_panel, swap(u_panel, "pcol", nc)], axis=0)
        pair = jnp.where(jnp.bitwise_and(c, 1) == 0, pair[:, :wd], pair[:, wd:])
        pairs = [lax.all_gather(pair, "prow")]
    if direct:
        got = [sent[0]]
        for t in range(1, nz):
            got.append(lax.ppermute(sent[t], "pcol", [(k, (k + 2 * t) % nc) for k in range(nc)]))
    else:
        blocks = sent[0].reshape(nz, 2 * slots, w)
        blocks = lax.all_to_all(blocks, "pcol", split_axis=0, concat_axis=0, axis_index_groups=groups, tiled=True)
        got = [blocks.reshape(nc * slots, w)]
    got = got + [swap(v, "pcol", nc) for v in got]

    source, high, low = call(
        functools.partial(turn_kernel, direct, slots, owners),
        [bf16(2 * m, 2 * nc * slots), bf16(nz, wd, 2 * m), bf16(nz, wd, 2 * m)],
        names,
        *pairs,
    )
    parts = [f32(wd, w)] * nz if direct else [f32(nz, wd, w)]
    sigma_sj, *terms = call(correction_kernel, [f32(m, w)] + parts, source, high, low, *got, flops=term)
    if direct:
        total = terms[0]
        for t in range(1, nz):
            total = total + lax.ppermute(terms[t], "pcol", [(k, (k + 2 * t) % nc) for k in range(nc)])
    else:
        terms = lax.all_to_all(terms[0], "pcol", split_axis=0, concat_axis=0, axis_index_groups=groups, tiled=True)
        total = jnp.sum(terms, axis=0)
    return sigma_sj, d_term - total


def solution(mesh):
    placed = (P("pcol", "prow"), P(), P("pcol", "prow"), P("pcol", "prow"))
    return jax.shard_map(
        per_device,
        mesh=mesh,
        in_specs=placed,
        out_specs=(P("pcol", "prow"), P("pcol", "prow")),
        check_vma=False,
    )
```

```python
import functools

import jax
import jax.numpy as jnp
from jax import lax
from jax.experimental import pallas as pl
from jax.experimental.pallas import tpu as pltpu
from jax.sharding import PartitionSpec as P

LANES = 128
BLOCK_CAP = 560
CAP = -(-BLOCK_CAP // 64) * 64
FULL = CAP // LANES
WIDE = (FULL + 1) * LANES
BF16 = jnp.bfloat16
VMEM = pl.BlockSpec(memory_space=pltpu.VMEM)
HBM = pl.BlockSpec(memory_space=pltpu.HBM)


def f32(*shape):
    return jax.ShapeDtypeStruct(shape, jnp.float32)


def bf16(*shape):
    return jax.ShapeDtypeStruct(shape, BF16)


def split(v):
    high = v.astype(BF16)
    return high, (v - high.astype(jnp.float32)).astype(BF16)


def split3(v):
    high = v.astype(BF16)
    mid, low = split(v - high.astype(jnp.float32))
    return high, mid, low


def dot(a, b):
    return jnp.dot(a, b, preferred_element_type=jnp.float32)


def pick_rows(place, v):
    high, mid, low = split3(v)
    return dot(place, high) + (dot(place, mid) + dot(place, low))


def one_hot(mask):
    return jnp.where(mask, 1.0, 0.0)


def count(mask):
    return jnp.sum(jnp.where(mask, 1.0, 0.0)).astype(jnp.int32)


def log2(size):
    return size.bit_length() - 1


def each(refs, owners, fn):
    if owners is None:
        pl.loop(0, refs[0].shape[0])(lambda i: fn(i, refs[0].at[i]))
    else:
        for owner, ref in zip(owners, refs):
            fn(owner, ref)


def select_kernel(structure_ref, sigma_ref, out_ref, held_ref, sems):
    rows, cols = held_ref.shape
    n = structure_ref.shape[0]
    parts = sems.shape[0]
    part = rows // parts
    copies = []
    for k in range(parts):
        at = pl.ds(part * k, part)
        copies.append(pltpu.make_async_copy(sigma_ref.at[at, :], held_ref.at[at, :], sems.at[k]))
        copies[-1].start()
    first = lax.axis_index("prow") * cols
    listed = structure_ref[...].reshape(1, -1)
    names = jnp.broadcast_to(listed, (8, n))
    shift = lax.rem(n - count(listed < first), n)
    named = pltpu.roll(names, shift, 1)[:1, :CAP] - first
    named = jnp.concatenate([named, named[:, FULL * LANES :]], axis=1)
    at = lax.broadcasted_iota(jnp.int32, (cols, WIDE), 0)
    place = one_hot(at == named).astype(BF16)
    for k in range(parts):
        copies[k].wait()
        high, low = split(held_ref[part * k : part * (k + 1), :])
        picked = dot(high, place) + dot(low, place)
        for i in range(FULL):
            at = rows * i + part * k
            out_ref[at : at + part, :] = picked[:, LANES * i : LANES * (i + 1)]
        at = rows * FULL + part * (k % (parts // 2))
        if k < parts // 2:
            out_ref[at : at + part, : LANES // 2] = picked[:, FULL * LANES : CAP]
        else:
            out_ref[at : at + part, LANES // 2 :] = picked[:, CAP:]


def block_term(block_ref, uh, ul, rows):
    parts = [block_ref[rows * i : rows * (i + 1), :] for i in range(FULL)]
    tail = block_ref[rows * FULL : rows * FULL + rows // 2, :]
    parts.append(jnp.concatenate([tail, pltpu.roll(tail, LANES // 2, 1)], axis=0))
    halves = [split(p) for p in parts]
    highs, lows = [h for h, _ in halves], [l for _, l in halves]
    left = jnp.concatenate(highs + highs + lows, axis=1)
    return dot(left, jnp.concatenate([uh, ul, uh], axis=0))


def prepare_kernel(direct, nc, owners, structure_ref, *refs):
    pair_ref = None
    if direct:
        pair_ref, refs = refs[-2], refs[:-2] + refs[-1:]
    uh_ref, ul_ref, part_ref, us_ref = refs[-4:]
    nr, _, w = uh_ref.shape
    n_u = nc if direct else 1
    u_refs, first_refs = refs[:n_u], refs[n_u:-4]
    n = structure_ref.shape[0]
    m = n // nc
    c = lax.axis_index("pcol")
    r = lax.axis_index("prow")
    rows = part_ref.shape[0]
    names = structure_ref[...].reshape(1, -1)

    def place(owner, u):
        if w % LANES:
            u = jnp.concatenate([u, jnp.zeros((m, LANES - w % LANES), jnp.float32)], axis=1)
        for i in range(us_ref.shape[0]):
            us_ref[i, pl.ds(owner, u.shape[0], stride=nc), :] = u[:, LANES * i : LANES * (i + 1)]

    if direct:
        lane = pl.multiple_of((c & 1) * (w // 2), LANES)
        pair_ref[:m, :] = u_refs[0][:, pl.ds(lane, w // 2)]
        for owner, u_ref in zip(ring_owners(nc, c), u_refs):
            place(owner, u_ref[...])

            @pl.when(owner == jnp.bitwise_xor(c, 1))
            def _():
                pair_ref[m:, :] = u_ref[:, pl.ds(lane, w // 2)]

    else:
        pl.loop(0, nc)(lambda k: place(k, u_refs[0][k]))
    us_ref[:, n:, :] = jnp.zeros((us_ref.shape[0], us_ref.shape[1] - n, LANES), jnp.float32)

    width = rows * 2

    def cut(owner):
        start = count(names < owner * width)
        base = pl.multiple_of((start // 8) * 8, 8)
        size = CAP + 8
        lanes = [
            pltpu.roll(us_ref[k, pl.ds(base, size), :], size - (start - base), 0)[:CAP]
            for k in range(us_ref.shape[0])
        ]
        u = jnp.concatenate(lanes, axis=1)[:, :w]
        u = jnp.concatenate([u, jnp.zeros((WIDE - CAP, w), jnp.float32)], axis=0)
        uh_ref[owner], ul_ref[owner] = split(u)

    if direct:
        for b in range(nr):
            cut(b)
    else:
        pl.loop(0, nr)(cut)
    image = jnp.zeros((rows, w), jnp.float32)
    for owner, block_ref in zip(owners(r), first_refs):
        image = image + block_term(block_ref, uh_ref[owner], ul_ref[owner], rows)
    part_ref[...] = image


def row_order(names, c, rows, nc, slots, direct):
    n = names.shape[1]
    z = c // 2
    lg = log2(nc)
    row = c * rows + lax.broadcasted_iota(jnp.int32, (rows, n), 0)
    rank = jnp.sum(one_hot(names < row), axis=1, keepdims=True).astype(jnp.int32)
    member = jnp.sum(one_hot(names == row), axis=1, keepdims=True)
    turn = rank & (nc - 1)
    ahead = (count(names < c * rows) - turn + nc - 1) >> lg
    block = turn >> 1
    if direct:
        block = (block - z) & (nc // 2 - 1)
    block = 2 * block + (turn & 1)
    slot = jnp.where(member > 0.5, block * slots + (rank >> lg) - ahead, -1)
    at = lax.broadcasted_iota(jnp.int32, (rows, nc * slots), 1)
    return one_hot(at == slot).T.astype(BF16)


def near_kernel(direct, slots, owners, structure_ref, uh_ref, ul_ref, part_ref, *refs):
    block_refs, (image_ref, to_ref) = refs[:-2], refs[-2:]
    rows = part_ref.shape[0]
    image = part_ref[...]
    for owner, block_ref in zip(owners(lax.axis_index("prow")), block_refs):
        image = image + block_term(block_ref, uh_ref[owner], ul_ref[owner], rows)
    image_ref[...] = image
    nc = to_ref.shape[0] // slots
    to_ref[...] = row_order(structure_ref[...].reshape(1, -1), lax.axis_index("pcol"), rows, nc, slots, direct)


def image_kernel(n_out, owners, uh_ref, ul_ref, part_ref, to_ref, *refs):
    block_refs, out_refs = refs[:-n_out], refs[-n_out:]
    rows = part_ref.shape[0]
    image = part_ref[...]
    if owners is None:
        stack = block_refs[0]
        add = lambda b, v: v + block_term(stack.at[b], uh_ref[b], ul_ref[b], rows)
        image = lax.fori_loop(0, stack.shape[0], add, image)
    else:
        for owner, block_ref in zip(owners(lax.axis_index("prow")), block_refs):
            image = image + block_term(block_ref, uh_ref[owner], ul_ref[owner], rows)
    image = pick_rows(to_ref[...], image)
    size = image.shape[0] // n_out
    for k, out_ref in enumerate(out_refs):
        out_ref[...] = image[size * k : size * (k + 1)]


def turn_kernel(direct, slots, owners, structure_ref, *refs):
    from_ref, high_ref, low_ref = refs[-3:]
    nz = high_ref.shape[0]
    nc = 2 * nz
    rows = slots * nc
    n = structure_ref.shape[0]
    m = n // nc
    names = structure_ref[...].reshape(1, -1)
    c = lax.axis_index("pcol")
    z = c // 2

    def put(owner, u_ref):
        where = ((owner - z) & (nz - 1)) if direct else owner
        high_ref[where], low_ref[where] = split(u_ref[...].T)

    each(refs[:-3], owners(lax.axis_index("prow")) if direct else None, put)

    own = lax.broadcasted_iota(jnp.int32, (m, n), 1) - nc * lax.broadcasted_iota(jnp.int32, (m, n), 0)
    at = lax.broadcasted_iota(jnp.int32, (m, 2 * rows), 1)
    for half, column in enumerate((c, jnp.bitwise_xor(c, 1))):
        mine = jnp.where(own == column, names, 0).astype(jnp.float32)
        mine = jnp.sum(mine, axis=1, keepdims=True)
        source = jnp.zeros((m, 1), jnp.int32)
        before = jnp.zeros((m, 1), jnp.int32)
        for k in range(1, nc):
            less = mine < float(k * rows)
            source = source + jnp.where(less, 0, 1)
            before = jnp.where(less, before, count(less))
        block = source >> 1
        if direct:
            block = (z - block) & (nz - 1)
        block = 2 * (block + nz * ((source ^ c) & 1)) + (column & 1)
        slot = block * slots + lax.broadcasted_iota(jnp.int32, (m, 1), 0) - before
        from_ref[m * half : m * (half + 1), :] = one_hot(at == slot).astype(BF16)


def correction_kernel(from_ref, high_ref, low_ref, *refs):
    nz = high_ref.shape[0]
    n_in = 2 if len(refs) == 4 else 2 * nz
    got = jnp.concatenate([ref[...] for ref in refs[:n_in]], axis=0)
    sj_ref, out_refs = refs[n_in], refs[n_in + 1 :]
    both = -pick_rows(from_ref[...], got)
    sj_ref[...] = both[: sj_ref.shape[0]]
    sh, sl = split(both)

    def term(t):
        return dot(high_ref[t], sh) + (dot(high_ref[t], sl) + dot(low_ref[t], sh))

    if len(out_refs) > 1:
        for t, out_ref in enumerate(out_refs):
            out_ref[...] = term(t)
    else:

        @pl.loop(0, nz)
        def _(t):
            out_refs[0][t] = term(t)


def call(kernel, out_shape, *args, flops=0, vmem=20, **kw):
    many = isinstance(out_shape, (list, tuple))
    size = sum(v.size * v.dtype.itemsize for v in jax.tree.leaves((out_shape, args)))
    kw = {"in_specs": [VMEM] * len(args)} | kw
    return pl.pallas_call(
        kernel,
        out_shape=out_shape,
        out_specs=[VMEM] * len(out_shape) if many else VMEM,
        cost_estimate=pl.CostEstimate(flops=flops, bytes_accessed=size, transcendentals=0),
        compiler_params=pltpu.CompilerParams(vmem_limit_bytes=vmem * 2**20),
        **kw,
    )(*args)


def swap(v, axis, size):
    return lax.ppermute(v, axis, [(k, k ^ 1) for k in range(size)])


def spread(v, size):
    blocks = [v, swap(v, "prow", size)]
    for t in range(1, size // 2):
        for flip in range(2):
            blocks.append(lax.ppermute(v, "prow", [(k, ((k + 2 * t) % size) ^ flip) for k in range(size)]))
    return blocks


def relative_owners(size, r):
    out = []
    for t in range(size // 2):
        owner = (r - 2 * t) & (size - 1)
        out += [owner, owner ^ 1]
    return out


def ring_gather(u, nc):
    ring = [2 * z for z in range(nc // 2)] + [2 * z + 1 for z in reversed(range(nc // 2))]
    pairs = [(ring[q - 1], ring[q]) for q in range(nc)]
    back = [(b, a) for a, b in pairs]
    blocks = [u]
    up = down = u
    for step in range(1, nc // 2):
        up, down = lax.ppermute(up, "pcol", pairs), lax.ppermute(down, "pcol", back)
        blocks += [up, down]
    return blocks + [lax.ppermute(up, "pcol", pairs)]


def ring_owners(nc, c):
    q = jnp.where((c & 1) == 0, c >> 1, nc - 1 - (c >> 1))
    out = []
    for k in range(nc):
        step = (k + 1) // 2
        at = (q - step if k % 2 else q + step) & (nc - 1)
        out.append(jnp.where(at < nc // 2, 2 * at, 2 * (nc - 1 - at) + 1))
    return out


def per_device(sigma_top, structure, u_panel, d_term):
    nc, nr = lax.axis_size("pcol"), lax.axis_size("prow")
    c = lax.axis_index("pcol")
    nz = nc // 2
    rows, cols = sigma_top.shape
    m, w = u_panel.shape
    wd = w // 2
    n = structure.shape[0]
    slots = -(-rows // nc)
    direct = nc <= 8
    names = structure
    groups = [[2 * k + x for k in range(nz)] for x in range(2)]
    owners = functools.partial(relative_owners, nr)

    chosen = call(
        select_kernel,
        f32(rows * CAP // LANES, LANES),
        names,
        sigma_top,
        in_specs=[VMEM, HBM],
        scratch_shapes=[pltpu.VMEM((rows, cols), jnp.float32), pltpu.SemaphoreType.DMA((4,))],
        flops=4 * rows * cols * WIDE,
        vmem=52,
    )
    near = [chosen] if direct else []
    if direct:
        u_all = ring_gather(u_panel, nc)
    else:
        u_all = [lax.all_gather(u_panel, "pcol")]
    term = 6 * rows * WIDE * w
    uh, ul, image, *pair = call(
        functools.partial(prepare_kernel, direct, nc, lambda r: owners(r)[:1]),
        [bf16(nr, WIDE, w), bf16(nr, WIDE, w), f32(rows, w)] + [f32(2 * m, wd)] * direct,
        names,
        *u_all,
        *near,
        scratch_shapes=[pltpu.VMEM((-(-w // LANES), n + CAP + 8, LANES), jnp.float32)],
        flops=term,
    )
    beside, later = [], []
    if direct:
        beside.append(swap(chosen, "prow", nr))
        for t in range(1, nr // 2):
            far = lax.ppermute(chosen, "prow", [(k, (k + 2 * t) % nr) for k in range(nr)])
            far, _ = lax.optimization_barrier((far, image))
            beside.append(far)
            later.append(swap(far, "prow", nr))
    else:
        later = [lax.all_gather(chosen, "prow")]
    image, to = call(
        functools.partial(near_kernel, direct, slots, lambda r: owners(r)[1:2] + owners(r)[2::2]),
        [f32(rows, w), bf16(nc * slots, rows)],
        names,
        uh,
        ul,
        image,
        *beside,
        flops=term,
    )
    if direct:
        pair, _ = lax.optimization_barrier((pair[0], beside[1]))
        pairs = spread(pair, nr)
        pairs[1], to = lax.optimization_barrier((pairs[1], to))
    else:
        pair = jnp.concatenate([u_panel, swap(u_panel, "pcol", nc)], axis=0)
        pair = jnp.where(jnp.bitwise_and(c, 1) == 0, pair[:, :wd], pair[:, wd:])
        pairs = [lax.all_gather(pair, "prow")]
    n_out = nz if direct else 1
    sent = call(
        functools.partial(image_kernel, n_out, (lambda r: owners(r)[3::2]) if direct else None),
        [f32(nc * slots // n_out, w)] * n_out,
        uh,
        ul,
        image,
        to,
        *later,
        flops=term,
    )
    if direct:
        got = [sent[0]]
        for t in range(1, nz):
            got.append(lax.ppermute(sent[t], "pcol", [(k, (k + 2 * t) % nc) for k in range(nc)]))
    else:
        blocks = sent[0].reshape(nz, 2 * slots, w)
        blocks = lax.all_to_all(blocks, "pcol", split_axis=0, concat_axis=0, axis_index_groups=groups, tiled=True)
        got = [blocks.reshape(nc * slots, w)]
    got = got + [swap(v, "pcol", nc) for v in got]
    source, high, low = call(
        functools.partial(turn_kernel, direct, slots, owners),
        [bf16(2 * m, 2 * nc * slots), bf16(nz, wd, 2 * m), bf16(nz, wd, 2 * m)],
        names,
        *pairs,
    )
    parts = [f32(wd, w)] * nz if direct else [f32(nz, wd, w)]
    sigma_sj, *terms = call(correction_kernel, [f32(m, w)] + parts, source, high, low, *got, flops=term)
    if direct:
        total = terms[0]
        for t in range(1, nz):
            total = total + lax.ppermute(terms[t], "pcol", [(k, (k + 2 * t) % nc) for k in range(nc)])
    else:
        terms = lax.all_to_all(terms[0], "pcol", split_axis=0, concat_axis=0, axis_index_groups=groups, tiled=True)
        total = jnp.sum(terms, axis=0)
    return sigma_sj, d_term - total


def solution(mesh):
    placed = (P("pcol", "prow"), P(), P("pcol", "prow"), P("pcol", "prow"))
    return jax.shard_map(
        per_device,
        mesh=mesh,
        in_specs=placed,
        out_specs=(P("pcol", "prow"), P("pcol", "prow")),
        check_vma=False,
    )
```

```python
import functools

import jax
import jax.numpy as jnp
from jax import lax
from jax.experimental import pallas as pl
from jax.experimental.pallas import tpu as pltpu
from jax.sharding import PartitionSpec as P

LANES = 128
BLOCK_CAP = 560
CAP = -(-BLOCK_CAP // 64) * 64
FULL = CAP // LANES
WIDE = (FULL + 1) * LANES
BF16 = jnp.bfloat16
VMEM = pl.BlockSpec(memory_space=pltpu.VMEM)
HBM = pl.BlockSpec(memory_space=pltpu.HBM)


def f32(*shape):
    return jax.ShapeDtypeStruct(shape, jnp.float32)


def bf16(*shape):
    return jax.ShapeDtypeStruct(shape, BF16)


def split(v):
    high = v.astype(BF16)
    return high, (v - high.astype(jnp.float32)).astype(BF16)


def split3(v):
    high = v.astype(BF16)
    mid, low = split(v - high.astype(jnp.float32))
    return high, mid, low


def dot(a, b):
    return jnp.dot(a, b, preferred_element_type=jnp.float32)


def pick_rows(place, v):
    high, mid, low = split3(v)
    return dot(place, high) + (dot(place, mid) + dot(place, low))


def one_hot(mask):
    return jnp.where(mask, 1.0, 0.0)


def count(mask):
    return jnp.sum(jnp.where(mask, 1.0, 0.0)).astype(jnp.int32)


def log2(size):
    return size.bit_length() - 1


def each(refs, owners, fn):
    if owners is None:
        pl.loop(0, refs[0].shape[0])(lambda i: fn(i, refs[0].at[i]))
    else:
        for owner, ref in zip(owners, refs):
            fn(owner, ref)


def select_kernel(structure_ref, sigma_ref, out_ref, held_ref, sems):
    rows, cols = held_ref.shape
    n = structure_ref.shape[0]
    parts = sems.shape[0]
    part = rows // parts
    copies = []
    for k in range(parts):
        at = pl.ds(part * k, part)
        copies.append(pltpu.make_async_copy(sigma_ref.at[at, :], held_ref.at[at, :], sems.at[k]))
        copies[-1].start()
    first = lax.axis_index("prow") * cols
    listed = structure_ref[...].reshape(1, -1)
    names = jnp.broadcast_to(listed, (8, n))
    shift = lax.rem(n - count(listed < first), n)
    named = pltpu.roll(names, shift, 1)[:1, :CAP] - first
    named = jnp.concatenate([named, named[:, FULL * LANES :]], axis=1)
    at = lax.broadcasted_iota(jnp.int32, (cols, WIDE), 0)
    place = one_hot(at == named).astype(BF16)
    for k in range(parts):
        copies[k].wait()
        high, low = split(held_ref[part * k : part * (k + 1), :])
        picked = dot(high, place) + dot(low, place)
        for i in range(FULL):
            at = rows * i + part * k
            out_ref[at : at + part, :] = picked[:, LANES * i : LANES * (i + 1)]
        at = rows * FULL + part * (k % (parts // 2))
        if k < parts // 2:
            out_ref[at : at + part, : LANES // 2] = picked[:, FULL * LANES : CAP]
        else:
            out_ref[at : at + part, LANES // 2 :] = picked[:, CAP:]


def block_term(block_ref, uh, ul, rows):
    parts = [block_ref[rows * i : rows * (i + 1), :] for i in range(FULL)]
    tail = block_ref[rows * FULL : rows * FULL + rows // 2, :]
    parts.append(jnp.concatenate([tail, pltpu.roll(tail, LANES // 2, 1)], axis=0))
    halves = [split(p) for p in parts]
    highs, lows = [h for h, _ in halves], [l for _, l in halves]
    left = jnp.concatenate(highs + highs + lows, axis=1)
    return dot(left, jnp.concatenate([uh, ul, uh], axis=0))


def prepare_kernel(direct, nc, owners, structure_ref, *refs):
    uh_ref, ul_ref, part_ref, own_ref, us_ref = refs[-5:]
    nr, _, w = uh_ref.shape
    n_u = nc if direct else 1
    u_refs, first_refs = refs[:n_u], refs[n_u:-5]
    n = structure_ref.shape[0]
    m = n // nc
    c = lax.axis_index("pcol")
    r = lax.axis_index("prow")
    rows = part_ref.shape[0]
    names = structure_ref[...].reshape(1, -1)

    def place(owner, u):
        if w % LANES:
            u = jnp.concatenate([u, jnp.zeros((m, LANES - w % LANES), jnp.float32)], axis=1)
        for i in range(us_ref.shape[0]):
            us_ref[i, pl.ds(owner, u.shape[0], stride=nc), :] = u[:, LANES * i : LANES * (i + 1)]

    if direct:
        for owner, u_ref in zip(ring_owners(nc, c), u_refs):
            place(owner, u_ref[...])
    else:
        pl.loop(0, nc)(lambda k: place(k, u_refs[0][k]))
    us_ref[:, n:, :] = jnp.zeros((us_ref.shape[0], us_ref.shape[1] - n, LANES), jnp.float32)

    width = rows * 2

    def rows_of(owner, lane_blocks):
        start = count(names < owner * width)
        base = pl.multiple_of((start // 8) * 8, 8)
        size = CAP + 8
        lanes = [pltpu.roll(us_ref[k, pl.ds(base, size), :], size - (start - base), 0)[:CAP] for k in lane_blocks]
        return jnp.concatenate(lanes, axis=1)

    def cut(owner):
        u = rows_of(owner, range(us_ref.shape[0]))[:, :w]
        u = jnp.concatenate([u, jnp.zeros((WIDE - CAP, w), jnp.float32)], axis=0)
        uh_ref[owner], ul_ref[owner] = split(u)

    own_ref[...] = rows_of(c // 2, [c & 1]) if direct else rows_of(c // 2, [0])[:, :w]

    if direct:
        for b in range(nr):
            cut(b)
    else:
        pl.loop(0, nr)(cut)
    image = jnp.zeros((rows, w), jnp.float32)
    for owner, block_ref in zip(owners(r), first_refs):
        image = image + block_term(block_ref, uh_ref[owner], ul_ref[owner], rows)
    part_ref[...] = image


def row_order(names, c, rows, nc, slots, direct):
    n = names.shape[1]
    z = c // 2
    lg = log2(nc)
    row = c * rows + lax.broadcasted_iota(jnp.int32, (rows, n), 0)
    rank = jnp.sum(one_hot(names < row), axis=1, keepdims=True).astype(jnp.int32)
    member = jnp.sum(one_hot(names == row), axis=1, keepdims=True)
    turn = rank & (nc - 1)
    ahead = (count(names < c * rows) - turn + nc - 1) >> lg
    block = turn >> 1
    if direct:
        block = (block - z) & (nc // 2 - 1)
    block = 2 * block + (turn & 1)
    slot = jnp.where(member > 0.5, block * slots + (rank >> lg) - ahead, -1)
    at = lax.broadcasted_iota(jnp.int32, (rows, nc * slots), 1)
    return one_hot(at == slot).T.astype(BF16)


def near_kernel(direct, slots, owners, structure_ref, uh_ref, ul_ref, part_ref, *refs):
    block_refs, (image_ref, to_ref) = refs[:-2], refs[-2:]
    rows = part_ref.shape[0]
    image = part_ref[...]
    for owner, block_ref in zip(owners(lax.axis_index("prow")), block_refs):
        image = image + block_term(block_ref, uh_ref[owner], ul_ref[owner], rows)
    image_ref[...] = image
    nc = to_ref.shape[0] // slots
    to_ref[...] = row_order(structure_ref[...].reshape(1, -1), lax.axis_index("pcol"), rows, nc, slots, direct)


def image_kernel(direct, owners, uh_ref, ul_ref, part_ref, to_ref, *refs):
    n_out = len(refs) - (1 if not direct else len(owners(0)))
    block_refs, out_refs = refs[:-n_out], refs[-n_out:]
    rows = part_ref.shape[0]
    image = part_ref[...]
    if direct:
        for owner, block_ref in zip(owners(lax.axis_index("prow")), block_refs):
            image = image + block_term(block_ref, uh_ref[owner], ul_ref[owner], rows)
    else:
        stack = block_refs[0]
        add = lambda b, v: v + block_term(stack.at[b], uh_ref[b], ul_ref[b], rows)
        image = lax.fori_loop(0, stack.shape[0], add, image)
    image = pick_rows(to_ref[...], image)
    out_refs[0][...] = image
    size = image.shape[0] // n_out
    for k in range(1, n_out):
        out_refs[k][...] = image[size * k : size * (k + 1)]


def turn_kernel(direct, slots, owners, structure_ref, *refs):
    from_ref, high_ref, low_ref = refs[-3:]
    nz = high_ref.shape[0]
    nc = 2 * nz
    lg = log2(nc)
    rows = slots * nc
    n = structure_ref.shape[0]
    m = n // nc
    names = structure_ref[...].reshape(1, -1)
    c = lax.axis_index("pcol")
    z, x = c // 2, c & 1

    start, middle = count(names < 2 * z * rows), count(names < (2 * z + 1) * rows)
    named = pltpu.roll(jnp.broadcast_to(names, (8, n)), lax.rem(n - start, n), 1)[:1, :CAP]
    index = start + lax.broadcasted_iota(jnp.int32, (1, CAP), 1)
    half = jnp.where(named >= (2 * z + 1) * rows, 1, 0)
    turn = index & (nc - 1)
    ahead = (jnp.where(half == 1, middle, start) - turn + nc - 1) >> lg
    block = turn >> 1
    if direct:
        block = (block - z) & (nz - 1)
    slot = (2 * block + (turn & 1)) * slots + (index >> lg) - ahead + (half ^ x) * rows
    slot = jnp.where((named >= 2 * z * rows) & (named < (2 * z + 2) * rows), slot, -1)
    at = lax.broadcasted_iota(jnp.int32, (2 * rows, CAP), 0)
    place = one_hot(at == slot).astype(BF16)

    def put(owner, u_ref):
        where = ((owner - z) & (nz - 1)) if direct else owner
        for out_ref, part in zip((high_ref, low_ref), split(u_ref[...].T)):
            turned = lax.dot_general(part, place, (((1,), (1,)), ((), ())), preferred_element_type=jnp.float32)
            out_ref[where] = turned.astype(BF16)

    each(refs[:-3], owners(lax.axis_index("prow")) if direct else None, put)

    own = lax.broadcasted_iota(jnp.int32, (m, n), 1) - nc * lax.broadcasted_iota(jnp.int32, (m, n), 0)
    mine = jnp.sum(jnp.where(own == c, names, 0).astype(jnp.float32), axis=1, keepdims=True)
    source = jnp.zeros((m, 1), jnp.int32)
    before = jnp.zeros((m, 1), jnp.int32)
    for k in range(1, nc):
        less = mine < float(k * rows)
        source = source + jnp.where(less, 0, 1)
        before = jnp.where(less, before, count(less))
    block = source >> 1
    if direct:
        block = (z - block) & (nz - 1)
    block = block + nz * ((source ^ c) & 1)
    slot = block * slots + lax.broadcasted_iota(jnp.int32, (m, 1), 0) - before
    at = lax.broadcasted_iota(jnp.int32, (m, rows), 1)
    from_ref[...] = one_hot(at == slot).astype(BF16)


def correction_kernel(slots, n_got, high_ref, low_ref, whole_ref, other_ref, *refs):
    got_refs, (mine_ref, theirs_ref), out_refs = refs[:n_got], refs[n_got : n_got + 2], refs[n_got + 2 :]
    sh, sl = split(jnp.concatenate([whole_ref[...], other_ref[...]], axis=0))

    def term(t):
        return dot(high_ref[t], sh) + (dot(high_ref[t], sl) + dot(low_ref[t], sh))

    if len(out_refs) > 1:
        for t, out_ref in enumerate(out_refs):
            out_ref[...] = term(t)
    else:

        @pl.loop(0, out_refs[0].shape[0])
        def _(t):
            out_refs[0][t] = term(t)

    first = (lax.axis_index("pcol") & 1) == 0
    mine, theirs = [], []
    for ref, k in [(whole_ref, 0)] * (n_got > 1) + [(ref, k) for ref in got_refs for k in range(ref.shape[0] // (2 * slots))]:
        low = ref[2 * slots * k : 2 * slots * k + slots, :]
        high = ref[2 * slots * k + slots : 2 * slots * (k + 1), :]
        mine.append(jnp.where(first, low, high))
        theirs.append(jnp.where(first, high, low))
    mine_ref[...] = jnp.concatenate(mine, axis=0)
    theirs_ref[...] = jnp.concatenate(theirs, axis=0)


def pick_kernel(from_ref, mine_ref, other_ref, out_ref):
    out_ref[...] = -pick_rows(from_ref[...], jnp.concatenate([mine_ref[...], other_ref[...]], axis=0))


def call(kernel, out_shape, *args, flops=0, vmem=20, **kw):
    many = isinstance(out_shape, (list, tuple))
    size = sum(v.size * v.dtype.itemsize for v in jax.tree.leaves((out_shape, args)))
    kw = {"in_specs": [VMEM] * len(args)} | kw
    return pl.pallas_call(
        kernel,
        out_shape=out_shape,
        out_specs=[VMEM] * len(out_shape) if many else VMEM,
        cost_estimate=pl.CostEstimate(flops=flops, bytes_accessed=size, transcendentals=0),
        compiler_params=pltpu.CompilerParams(vmem_limit_bytes=vmem * 2**20),
        **kw,
    )(*args)


def swap(v, axis, size):
    return lax.ppermute(v, axis, [(k, k ^ 1) for k in range(size)])


def spread(v, near, size, after):
    blocks = [v, near]
    for t in range(1, size // 2):
        far = lax.ppermute(v, "prow", [(k, (k + 2 * t) % size) for k in range(size)])
        far, _ = lax.optimization_barrier((far, after))
        blocks += [far, swap(far, "prow", size)]
    return blocks


def relative_owners(size, r):
    out = []
    for t in range(size // 2):
        owner = (r - 2 * t) & (size - 1)
        out += [owner, owner ^ 1]
    return out


def ring_gather(u, nc):
    ring = [2 * z for z in range(nc // 2)] + [2 * z + 1 for z in reversed(range(nc // 2))]
    pairs = [(ring[q - 1], ring[q]) for q in range(nc)]
    back = [(b, a) for a, b in pairs]
    blocks = [u]
    up = down = u
    for step in range(1, nc // 2):
        up, down = lax.ppermute(up, "pcol", pairs), lax.ppermute(down, "pcol", back)
        up, down = lax.optimization_barrier((up, down))
        blocks += [up, down]
    return blocks + [lax.ppermute(up, "pcol", pairs)]


def ring_owners(nc, c):
    q = jnp.where((c & 1) == 0, c >> 1, nc - 1 - (c >> 1))
    out = []
    for k in range(nc):
        step = (k + 1) // 2
        at = (q - step if k % 2 else q + step) & (nc - 1)
        out.append(jnp.where(at < nc // 2, 2 * at, 2 * (nc - 1 - at) + 1))
    return out


def per_device(sigma_top, structure, u_panel, d_term):
    nc, nr = lax.axis_size("pcol"), lax.axis_size("prow")
    c = lax.axis_index("pcol")
    nz = nc // 2
    rows, cols = sigma_top.shape
    m, w = u_panel.shape
    wd = w // 2
    n = structure.shape[0]
    slots = -(-rows // nc)
    direct = nc <= 8
    names = structure
    groups = [[2 * k + x for k in range(nz)] for x in range(2)]
    owners = functools.partial(relative_owners, nr)

    chosen = call(
        select_kernel,
        f32(rows * CAP // LANES, LANES),
        names,
        sigma_top,
        in_specs=[VMEM, HBM],
        scratch_shapes=[pltpu.VMEM((rows, cols), jnp.float32), pltpu.SemaphoreType.DMA((4,))],
        flops=4 * rows * cols * WIDE,
        vmem=52,
    )
    near = [chosen] if direct else []
    if direct:
        u_all = ring_gather(u_panel, nc)
    else:
        u_all = [lax.all_gather(u_panel, "pcol")]
    term = 6 * rows * WIDE * w
    uh, ul, image, own = call(
        functools.partial(prepare_kernel, direct, nc, lambda r: owners(r)[:1]),
        [bf16(nr, WIDE, w), bf16(nr, WIDE, w), f32(rows, w), f32(CAP, wd if direct else w)],
        names,
        *u_all,
        *near,
        scratch_shapes=[pltpu.VMEM((-(-w // LANES), n + CAP + 8, LANES), jnp.float32)],
        flops=15 * term // 2,
    )
    beside, later = [], []
    if direct:
        beside.append(swap(chosen, "prow", nr))
        for t in range(1, nr // 2):
            far = lax.ppermute(chosen, "prow", [(k, (k + 2 * t) % nr) for k in range(nr)])
            far, _ = lax.optimization_barrier((far, image))
            beside.append(far)
            later.append(swap(far, "prow", nr))
    else:
        later = [lax.all_gather(chosen, "prow")]
    image, to = call(
        functools.partial(near_kernel, direct, slots, lambda r: owners(r)[1:2] + owners(r)[2::2]),
        [f32(rows, w), bf16(nc * slots, rows)],
        names,
        uh,
        ul,
        image,
        *beside,
        flops=term,
    )
    if direct:
        own, _ = lax.optimization_barrier((own, beside[1]))
        near = swap(own, "prow", nr)
        near, to = lax.optimization_barrier((near, to))
    sent = call(
        functools.partial(image_kernel, direct, lambda r: owners(r)[3::2]),
        [f32(nc * slots, w)] + [f32(2 * slots, w)] * ((nz - 1) * direct),
        uh,
        ul,
        image,
        to,
        *later,
        flops=term,
    )
    whole = sent[0]
    other = swap(whole, "pcol", nc)
    if direct:
        got = []
        for t in range(1, nz):
            got.append(lax.ppermute(sent[t], "pcol", [(k, (k + 2 * t) % nc) for k in range(nc)]))
        owned = spread(own, near, nr, whole)
    else:
        blocks = whole.reshape(nz, 2 * slots, w)
        blocks = lax.all_to_all(blocks, "pcol", split_axis=0, concat_axis=0, axis_index_groups=groups, tiled=True)
        got = [blocks.reshape(nc * slots, w)]
        own = jnp.where(jnp.bitwise_and(c, 1) == 0, own[:, :wd], own[:, wd:])
        owned = [lax.all_gather(own, "prow")]

    turned = bf16(nz, wd, 2 * nc * slots)
    source, high, low = call(
        functools.partial(turn_kernel, direct, slots, owners),
        [bf16(m, nc * slots), turned, turned],
        names,
        *owned,
        flops=8 * nz * wd * nc * slots * CAP,
    )
    parts = [f32(wd, w)] * nz if direct else [f32(nz, wd, w)]
    mine, theirs, *terms = call(
        functools.partial(correction_kernel, slots, len(got)),
        [f32(nz * slots, w)] * 2 + parts,
        high,
        low,
        whole,
        other,
        *got,
        flops=term,
    )
    sigma_sj = call(pick_kernel, f32(m, w), source, mine, swap(theirs, "pcol", nc), flops=term // 4)
    if direct:
        total = terms[0]
        for t in range(1, nz):
            total = total + lax.ppermute(terms[t], "pcol", [(k, (k + 2 * t) % nc) for k in range(nc)])
    else:
        terms = lax.all_to_all(terms[0], "pcol", split_axis=0, concat_axis=0, axis_index_groups=groups, tiled=True)
        total = jnp.sum(terms, axis=0)
    sigma_sj, d_term = lax.optimization_barrier((sigma_sj, d_term))
    return sigma_sj, d_term + total


def solution(mesh):
    placed = (P("pcol", "prow"), P(), P("pcol", "prow"), P("pcol", "prow"))
    return jax.shard_map(
        per_device,
        mesh=mesh,
        in_specs=placed,
        out_specs=(P("pcol", "prow"), P("pcol", "prow")),
        check_vma=False,
    )
```

```python
import functools

import jax
import jax.numpy as jnp
from jax import lax
from jax.experimental import pallas as pl
from jax.experimental.pallas import tpu as pltpu
from jax.sharding import PartitionSpec as P

LANES = 128
BLOCK_CAP = 560
CAP = -(-BLOCK_CAP // 64) * 64
FULL = CAP // LANES
WIDE = (FULL + 1) * LANES
BF16 = jnp.bfloat16
VMEM = pl.BlockSpec(memory_space=pltpu.VMEM)
HBM = pl.BlockSpec(memory_space=pltpu.HBM)


def f32(*shape):
    return jax.ShapeDtypeStruct(shape, jnp.float32)


def bf16(*shape):
    return jax.ShapeDtypeStruct(shape, BF16)


def split(v):
    high = v.astype(BF16)
    return high, (v - high.astype(jnp.float32)).astype(BF16)


def split3(v):
    high = v.astype(BF16)
    mid, low = split(v - high.astype(jnp.float32))
    return high, mid, low


def dot(a, b):
    return jnp.dot(a, b, preferred_element_type=jnp.float32)


def pick_rows(place, v):
    high, mid, low = split3(v)
    return dot(place, high) + (dot(place, mid) + dot(place, low))


def one_hot(mask):
    return jnp.where(mask, 1.0, 0.0)


def count(mask):
    return jnp.sum(jnp.where(mask, 1.0, 0.0)).astype(jnp.int32)


def log2(size):
    return size.bit_length() - 1


def each(refs, owners, fn):
    if owners is None:
        pl.loop(0, refs[0].shape[0])(lambda i: fn(i, refs[0].at[i]))
    else:
        for owner, ref in zip(owners, refs):
            fn(owner, ref)


def select_kernel(structure_ref, sigma_ref, out_ref, held_ref, sems):
    rows, cols = held_ref.shape
    n = structure_ref.shape[0]
    parts = sems.shape[0]
    part = rows // parts
    copies = []
    for k in range(parts):
        at = pl.ds(part * k, part)
        copies.append(pltpu.make_async_copy(sigma_ref.at[at, :], held_ref.at[at, :], sems.at[k]))
        copies[-1].start()
    first = lax.axis_index("prow") * cols
    listed = structure_ref[...].reshape(1, -1)
    names = jnp.broadcast_to(listed, (8, n))
    shift = lax.rem(n - count(listed < first), n)
    named = pltpu.roll(names, shift, 1)[:1, :CAP] - first
    named = jnp.concatenate([named, named[:, FULL * LANES :]], axis=1)
    at = lax.broadcasted_iota(jnp.int32, (cols, WIDE), 0)
    place = one_hot(at == named).astype(BF16)
    for k in range(parts):
        copies[k].wait()
        picked = dot(jnp.concatenate(split(held_ref[part * k : part * (k + 1), :]), axis=0), place)
        picked = picked[:part] + picked[part:]
        for i in range(FULL):
            at = rows * i + part * k
            out_ref[at : at + part, :] = picked[:, LANES * i : LANES * (i + 1)]
        at = rows * FULL + part * (k % (parts // 2))
        if k < parts // 2:
            out_ref[at : at + part, : LANES // 2] = picked[:, FULL * LANES : CAP]
        else:
            out_ref[at : at + part, LANES // 2 :] = picked[:, CAP:]


def block_term(block_ref, uh, ul, rows):
    parts = [block_ref[rows * i : rows * (i + 1), :] for i in range(FULL)]
    tail = block_ref[rows * FULL : rows * FULL + rows // 2, :]
    parts.append(jnp.concatenate([tail, pltpu.roll(tail, LANES // 2, 1)], axis=0))
    halves = [split(p) for p in parts]
    highs, lows = [h for h, _ in halves], [l for _, l in halves]
    left = jnp.concatenate(highs + highs + lows, axis=1)
    return dot(left, jnp.concatenate([uh, ul, uh], axis=0))


def prepare_kernel(direct, nc, owners, structure_ref, *refs):
    uh_ref, ul_ref, part_ref, own_ref, us_ref = refs[-5:]
    nr, _, w = uh_ref.shape
    n_u = nc if direct else 1
    u_refs, first_refs = refs[:n_u], refs[n_u:-5]
    n = structure_ref.shape[0]
    m = n // nc
    c = lax.axis_index("pcol")
    r = lax.axis_index("prow")
    rows = part_ref.shape[0]
    names = structure_ref[...].reshape(1, -1)

    def place(owner, u):
        if w % LANES:
            u = jnp.concatenate([u, jnp.zeros((m, LANES - w % LANES), jnp.float32)], axis=1)
        for i in range(us_ref.shape[0]):
            us_ref[i, pl.ds(owner, u.shape[0], stride=nc), :] = u[:, LANES * i : LANES * (i + 1)]

    if direct:
        for owner, u_ref in zip(ring_owners(nc, c), u_refs):
            place(owner, u_ref[...])
    else:
        pl.loop(0, nc)(lambda k: place(k, u_refs[0][k]))
    us_ref[:, n:, :] = jnp.zeros((us_ref.shape[0], us_ref.shape[1] - n, LANES), jnp.float32)

    width = rows * 2

    def rows_of(owner, lane_blocks):
        start = count(names < owner * width)
        base = pl.multiple_of((start // 8) * 8, 8)
        size = CAP + 8
        lanes = [pltpu.roll(us_ref[k, pl.ds(base, size), :], size - (start - base), 0)[:CAP] for k in lane_blocks]
        return jnp.concatenate(lanes, axis=1)

    def cut(owner):
        u = rows_of(owner, range(us_ref.shape[0]))[:, :w]
        u = jnp.concatenate([u, jnp.zeros((WIDE - CAP, w), jnp.float32)], axis=0)
        uh_ref[owner], ul_ref[owner] = split(u)

    own_ref[...] = rows_of(c // 2, [c & 1]) if direct else rows_of(c // 2, [0])[:, :w]

    if direct:
        for b in range(nr):
            cut(b)
    else:
        pl.loop(0, nr)(cut)
    image = jnp.zeros((rows, w), jnp.float32)
    for owner, block_ref in zip(owners(r), first_refs):
        image = image + block_term(block_ref, uh_ref[owner], ul_ref[owner], rows)
    part_ref[...] = image


def row_order(names, c, rows, nc, slots, direct):
    n = names.shape[1]
    z = c // 2
    lg = log2(nc)
    row = c * rows + lax.broadcasted_iota(jnp.int32, (rows, n), 0)
    rank = jnp.sum(one_hot(names < row), axis=1, keepdims=True).astype(jnp.int32)
    member = jnp.sum(one_hot(names == row), axis=1, keepdims=True)
    turn = rank & (nc - 1)
    ahead = (count(names < c * rows) - turn + nc - 1) >> lg
    block = turn >> 1
    if direct:
        block = (block - z) & (nc // 2 - 1)
    block = 2 * block + (turn & 1)
    slot = jnp.where(member > 0.5, block * slots + (rank >> lg) - ahead, -1)
    at = lax.broadcasted_iota(jnp.int32, (rows, nc * slots), 1)
    return one_hot(at == slot).T.astype(BF16)


def order_kernel(direct, slots, structure_ref, to_ref):
    nc = to_ref.shape[0] // slots
    rows = to_ref.shape[1]
    names = structure_ref[...].reshape(1, -1)
    to_ref[...] = row_order(names, lax.axis_index("pcol"), rows, nc, slots, direct)


def near_kernel(owners, uh_ref, ul_ref, part_ref, *refs):
    block_refs, image_ref = refs[:-1], refs[-1]
    rows = part_ref.shape[0]
    image = part_ref[...]
    for owner, block_ref in zip(owners(lax.axis_index("prow")), block_refs):
        image = image + block_term(block_ref, uh_ref[owner], ul_ref[owner], rows)
    image_ref[...] = image


def image_kernel(direct, owners, uh_ref, ul_ref, part_ref, to_ref, *refs):
    n_out = len(refs) - (1 if not direct else len(owners(0)))
    block_refs, out_refs = refs[:-n_out], refs[-n_out:]
    rows = part_ref.shape[0]
    image = part_ref[...]
    if direct:
        for owner, block_ref in zip(owners(lax.axis_index("prow")), block_refs):
            image = image + block_term(block_ref, uh_ref[owner], ul_ref[owner], rows)
    else:
        stack = block_refs[0]
        add = lambda b, v: v + block_term(stack.at[b], uh_ref[b], ul_ref[b], rows)
        image = lax.fori_loop(0, stack.shape[0], add, image)
    image = pick_rows(to_ref[...], image)
    out_refs[0][...] = image
    size = image.shape[0] // n_out
    for k in range(1, n_out):
        out_refs[k][...] = image[size * k : size * (k + 1)]


def turn_kernel(direct, slots, owners, structure_ref, *refs):
    from_ref, high_ref, low_ref, held_ref = refs[-4:]
    nz, wd = high_ref.shape[:2]
    nc = 2 * nz
    lg = log2(nc)
    rows = slots * nc
    n = structure_ref.shape[0]
    m = n // nc
    names = structure_ref[...].reshape(1, -1)
    c = lax.axis_index("pcol")
    z, x = c // 2, c & 1

    start, middle = count(names < 2 * z * rows), count(names < (2 * z + 1) * rows)
    named = pltpu.roll(jnp.broadcast_to(names, (8, n)), lax.rem(n - start, n), 1)[:1, :CAP]
    index = start + lax.broadcasted_iota(jnp.int32, (1, CAP), 1)
    half = jnp.where(named >= (2 * z + 1) * rows, 1, 0)
    turn = index & (nc - 1)
    ahead = (jnp.where(half == 1, middle, start) - turn + nc - 1) >> lg
    block = turn >> 1
    if direct:
        block = (block - z) & (nz - 1)
    slot = (2 * block + (turn & 1)) * slots + (index >> lg) - ahead + (half ^ x) * rows
    slot = jnp.where((named >= 2 * z * rows) & (named < (2 * z + 2) * rows), slot, -1)
    at = lax.broadcasted_iota(jnp.int32, (2 * rows, CAP), 0)
    place = one_hot(at == slot).astype(BF16)

    def put(owner, u_ref):
        where = ((owner - z) & (nz - 1)) if direct else owner
        high, low = split(u_ref[...].T)
        held_ref[pl.ds(pl.multiple_of(where * wd, wd), wd), :] = high
        held_ref[pl.ds(pl.multiple_of((where + nz) * wd, wd), wd), :] = low

    each(refs[:-4], owners(lax.axis_index("prow")) if direct else None, put)
    turned = lax.dot_general(held_ref[...], place, (((1,), (1,)), ((), ())), preferred_element_type=jnp.float32)
    turned = turned.astype(BF16).reshape(2, nz, wd, 2 * rows)
    high_ref[...] = turned[0]
    low_ref[...] = turned[1]

    own = lax.broadcasted_iota(jnp.int32, (m, n), 1) - nc * lax.broadcasted_iota(jnp.int32, (m, n), 0)
    mine = jnp.sum(jnp.where(own == c, names, 0).astype(jnp.float32), axis=1, keepdims=True)
    source = jnp.zeros((m, 1), jnp.int32)
    before = jnp.zeros((m, 1), jnp.int32)
    for k in range(1, nc):
        less = mine < float(k * rows)
        source = source + jnp.where(less, 0, 1)
        before = jnp.where(less, before, count(less))
    block = source >> 1
    if direct:
        block = (z - block) & (nz - 1)
    block = block + nz * ((source ^ c) & 1)
    slot = block * slots + lax.broadcasted_iota(jnp.int32, (m, 1), 0) - before
    at = lax.broadcasted_iota(jnp.int32, (m, rows), 1)
    from_ref[...] = one_hot(at == slot).astype(BF16)


def correction_kernel(high_ref, low_ref, mine_ref, other_ref, *out_refs):
    sh, sl = split(jnp.concatenate([mine_ref[...], other_ref[...]], axis=0))

    def term(t):
        return dot(high_ref[t], sh) + (dot(high_ref[t], sl) + dot(low_ref[t], sh))

    if len(out_refs) > 1:
        for t, out_ref in enumerate(out_refs):
            out_ref[...] = term(t)
    else:

        @pl.loop(0, out_refs[0].shape[0])
        def _(t):
            out_refs[0][t] = term(t)


def part_kernel(slots, *refs):
    mine_ref, theirs_ref = refs[-2:]
    first = (lax.axis_index("pcol") & 1) == 0
    blocks = mine_ref.shape[0] // slots
    mine, theirs = [], []
    for ref in refs[:-2]:
        for k in range(blocks // len(refs[:-2])):
            low = ref[2 * slots * k : 2 * slots * k + slots, :]
            high = ref[2 * slots * k + slots : 2 * slots * (k + 1), :]
            mine.append(jnp.where(first, low, high))
            theirs.append(jnp.where(first, high, low))
    mine_ref[...] = jnp.concatenate(mine, axis=0)
    theirs_ref[...] = jnp.concatenate(theirs, axis=0)


def pick_kernel(from_ref, mine_ref, other_ref, out_ref):
    out_ref[...] = -pick_rows(from_ref[...], jnp.concatenate([mine_ref[...], other_ref[...]], axis=0))


def call(kernel, out_shape, *args, flops=0, vmem=20, **kw):
    many = isinstance(out_shape, (list, tuple))
    size = sum(v.size * v.dtype.itemsize for v in jax.tree.leaves((out_shape, args)))
    kw = {"in_specs": [VMEM] * len(args)} | kw
    return pl.pallas_call(
        kernel,
        out_shape=out_shape,
        out_specs=[VMEM] * len(out_shape) if many else VMEM,
        cost_estimate=pl.CostEstimate(flops=flops, bytes_accessed=size, transcendentals=0),
        compiler_params=pltpu.CompilerParams(vmem_limit_bytes=vmem * 2**20),
        **kw,
    )(*args)


def swap(v, axis, size):
    return lax.ppermute(v, axis, [(k, k ^ 1) for k in range(size)])


def spread(v, size):
    blocks = [v, swap(v, "prow", size)]
    for t in range(1, size // 2):
        for flip in range(2):
            blocks.append(lax.ppermute(v, "prow", [(k, ((k + 2 * t) % size) ^ flip) for k in range(size)]))
    return blocks


def relative_owners(size, r):
    out = []
    for t in range(size // 2):
        owner = (r - 2 * t) & (size - 1)
        out += [owner, owner ^ 1]
    return out


def ring_gather(u, nc, aside):
    ring = [2 * z for z in range(nc // 2)] + [2 * z + 1 for z in reversed(range(nc // 2))]
    pairs = [(ring[q - 1], ring[q]) for q in range(nc)]
    back = [(b, a) for a, b in pairs]
    blocks = [u]
    up = down = u
    for step in range(1, nc // 2):
        up, down = lax.ppermute(up, "pcol", pairs), lax.ppermute(down, "pcol", back)
        if step == 1:
            up, down = lax.optimization_barrier((up, down))
        blocks += [up, down]
    last, aside = lax.optimization_barrier((lax.ppermute(up, "pcol", pairs), aside))
    return blocks + [last], aside


def ring_owners(nc, c):
    q = jnp.where((c & 1) == 0, c >> 1, nc - 1 - (c >> 1))
    out = []
    for k in range(nc):
        step = (k + 1) // 2
        at = (q - step if k % 2 else q + step) & (nc - 1)
        out.append(jnp.where(at < nc // 2, 2 * at, 2 * (nc - 1 - at) + 1))
    return out


def per_device(sigma_top, structure, u_panel, d_term):
    nc, nr = lax.axis_size("pcol"), lax.axis_size("prow")
    c = lax.axis_index("pcol")
    nz = nc // 2
    rows, cols = sigma_top.shape
    m, w = u_panel.shape
    wd = w // 2
    n = structure.shape[0]
    slots = -(-rows // nc)
    direct = nc <= 8
    names = structure
    groups = [[2 * k + x for k in range(nz)] for x in range(2)]
    owners = functools.partial(relative_owners, nr)

    chosen = call(
        select_kernel,
        f32(rows * CAP // LANES, LANES),
        names,
        sigma_top,
        in_specs=[VMEM, HBM],
        scratch_shapes=[pltpu.VMEM((rows, cols), jnp.float32), pltpu.SemaphoreType.DMA((2,))],
        flops=4 * rows * cols * WIDE,
        vmem=52,
    )
    near = [chosen] if direct else []
    to = call(functools.partial(order_kernel, direct, slots), bf16(nc * slots, rows), names)
    if direct:
        u_all, to = ring_gather(u_panel, nc, to)
    else:
        u_all = [lax.all_gather(u_panel, "pcol")]
    term = 6 * rows * WIDE * w
    uh, ul, image, own = call(
        functools.partial(prepare_kernel, direct, nc, lambda r: owners(r)[:1]),
        [bf16(nr, WIDE, w), bf16(nr, WIDE, w), f32(rows, w), f32(CAP, wd if direct else w)],
        names,
        *u_all,
        *near,
        scratch_shapes=[pltpu.VMEM((-(-w // LANES), n + CAP + 8, LANES), jnp.float32)],
        flops=15 * term // 2,
    )
    beside, later = [], []
    if direct:
        beside.append(swap(chosen, "prow", nr))
        for t in range(1, nr // 2):
            far = lax.ppermute(chosen, "prow", [(k, (k + 2 * t) % nr) for k in range(nr)])
            far, _ = lax.optimization_barrier((far, image))
            beside.append(far)
            later.append(swap(far, "prow", nr))
    else:
        later = [lax.all_gather(chosen, "prow")]
    if direct:
        image = call(
            functools.partial(near_kernel, lambda r: owners(r)[1:2] + owners(r)[2::2]),
            f32(rows, w),
            uh,
            ul,
            image,
            *beside,
            flops=term,
        )
    if direct:
        own, _ = lax.optimization_barrier((own, beside[1]))
        owned = spread(own, nr)
        owned[1], to = lax.optimization_barrier((owned[1], to))
    sent = call(
        functools.partial(image_kernel, direct, lambda r: owners(r)[3::2]),
        [f32(nc * slots, w)] + [f32(2 * slots, w)] * ((nz - 1) * direct),
        uh,
        ul,
        image,
        to,
        *later,
        flops=term,
    )
    whole = sent[0]
    other = swap(whole, "pcol", nc)
    if direct:
        got = [whole]
        for t in range(1, nz):
            got.append(lax.ppermute(sent[t], "pcol", [(k, (k + 2 * t) % nc) for k in range(nc)]))
    else:
        blocks = whole.reshape(nz, 2 * slots, w)
        blocks = lax.all_to_all(blocks, "pcol", split_axis=0, concat_axis=0, axis_index_groups=groups, tiled=True)
        got = [blocks.reshape(nc * slots, w)]
        own = jnp.where(jnp.bitwise_and(c, 1) == 0, own[:, :wd], own[:, wd:])
        owned = [lax.all_gather(own, "prow")]

    turned = bf16(nz, wd, 2 * nc * slots)
    source, high, low = call(
        functools.partial(turn_kernel, direct, slots, owners),
        [bf16(m, nc * slots), turned, turned],
        names,
        *owned,
        scratch_shapes=[pltpu.VMEM((2 * nz * wd, CAP), BF16)],
        flops=8 * nz * wd * nc * slots * CAP,
    )
    parts = [f32(wd, w)] * nz if direct else [f32(nz, wd, w)]
    got, _ = lax.optimization_barrier((got, source))
    mine, theirs = call(functools.partial(part_kernel, slots), [f32(nz * slots, w)] * 2, *got, flops=2 * term)
    other, _ = lax.optimization_barrier((other, mine))
    terms = call(correction_kernel, parts, high, low, whole, other, flops=term)
    theirs, _ = lax.optimization_barrier((theirs, terms[0]))
    sigma_sj = call(pick_kernel, f32(m, w), source, mine, swap(theirs, "pcol", nc), flops=term // 4)
    if direct:
        total = terms[0]
        for t in range(1, nz):
            total = total + lax.ppermute(terms[t], "pcol", [(k, (k + 2 * t) % nc) for k in range(nc)])
    else:
        terms = lax.all_to_all(terms[0], "pcol", split_axis=0, concat_axis=0, axis_index_groups=groups, tiled=True)
        total = jnp.sum(terms, axis=0)
    sigma_sj, d_term = lax.optimization_barrier((sigma_sj, d_term))
    return sigma_sj, d_term + total


def solution(mesh):
    placed = (P("pcol", "prow"), P(), P("pcol", "prow"), P("pcol", "prow"))
    return jax.shard_map(
        per_device,
        mesh=mesh,
        in_specs=placed,
        out_specs=(P("pcol", "prow"), P("pcol", "prow")),
        check_vma=False,
    )
```

```python
import functools

import jax
import jax.numpy as jnp
from jax import lax
from jax.experimental import pallas as pl
from jax.experimental.pallas import tpu as pltpu
from jax.sharding import PartitionSpec as P

LANES = 128
BLOCK_CAP = 560
CAP = -(-BLOCK_CAP // 64) * 64
FULL = CAP // LANES
WIDE = (FULL + 1) * LANES
BF16 = jnp.bfloat16
VMEM = pl.BlockSpec(memory_space=pltpu.VMEM)
HBM = pl.BlockSpec(memory_space=pltpu.HBM)


def f32(*shape):
    return jax.ShapeDtypeStruct(shape, jnp.float32)


def bf16(*shape):
    return jax.ShapeDtypeStruct(shape, BF16)


def split(v):
    high = v.astype(BF16)
    return high, (v - high.astype(jnp.float32)).astype(BF16)


def split3(v):
    high = v.astype(BF16)
    mid, low = split(v - high.astype(jnp.float32))
    return high, mid, low


def dot(a, b):
    return jnp.dot(a, b, preferred_element_type=jnp.float32)


def pick_rows(place, v):
    high, mid, low = split3(v)
    return dot(place, high) + (dot(place, mid) + dot(place, low))


def one_hot(mask):
    return jnp.where(mask, 1.0, 0.0)


def count(mask):
    return jnp.sum(jnp.where(mask, 1.0, 0.0)).astype(jnp.int32)


def log2(size):
    return size.bit_length() - 1


def each(refs, owners, fn):
    if owners is None:
        pl.loop(0, refs[0].shape[0])(lambda i: fn(i, refs[0].at[i]))
    else:
        for owner, ref in zip(owners, refs):
            fn(owner, ref)


def select_kernel(structure_ref, sigma_ref, out_ref, held_ref, sems):
    rows, cols = held_ref.shape
    n = structure_ref.shape[0]
    parts = sems.shape[0]
    part = rows // parts
    copies = []
    for k in range(parts):
        at = pl.ds(part * k, part)
        copies.append(pltpu.make_async_copy(sigma_ref.at[at, :], held_ref.at[at, :], sems.at[k]))
        copies[-1].start()
    first = lax.axis_index("prow") * cols
    listed = structure_ref[...].reshape(1, -1)
    names = jnp.broadcast_to(listed, (8, n))
    shift = lax.rem(n - count(listed < first), n)
    named = pltpu.roll(names, shift, 1)[:1, :CAP] - first
    named = jnp.concatenate([named, named[:, FULL * LANES :]], axis=1)
    at = lax.broadcasted_iota(jnp.int32, (cols, WIDE), 0)
    place = one_hot(at == named).astype(BF16)
    for k in range(parts):
        copies[k].wait()
        picked = dot(jnp.concatenate(split(held_ref[part * k : part * (k + 1), :]), axis=0), place)
        picked = picked[:part] + picked[part:]
        for i in range(FULL):
            at = rows * i + part * k
            out_ref[at : at + part, :] = picked[:, LANES * i : LANES * (i + 1)]
        at = rows * FULL + part * (k % (parts // 2))
        if k < parts // 2:
            out_ref[at : at + part, : LANES // 2] = picked[:, FULL * LANES : CAP]
        else:
            out_ref[at : at + part, LANES // 2 :] = picked[:, CAP:]


def block_term(block_ref, uh, ul, rows):
    parts = [block_ref[rows * i : rows * (i + 1), :] for i in range(FULL)]
    tail = block_ref[rows * FULL : rows * FULL + rows // 2, :]
    parts.append(jnp.concatenate([tail, pltpu.roll(tail, LANES // 2, 1)], axis=0))
    halves = [split(p) for p in parts]
    highs, lows = [h for h, _ in halves], [l for _, l in halves]
    left = jnp.concatenate(highs + highs + lows, axis=1)
    return dot(left, jnp.concatenate([uh, ul, uh], axis=0))


def place_rows(us_ref, u, owner):
    m, w = u.shape
    nc = (us_ref.shape[1] - CAP - 8) // m
    if w % LANES:
        u = jnp.concatenate([u, jnp.zeros((m, LANES - w % LANES), jnp.float32)], axis=1)
    for i in range(us_ref.shape[0]):
        us_ref[i, pl.ds(owner, m, stride=nc), :] = u[:, LANES * i : LANES * (i + 1)]


def rows_of(us_ref, names, owner, width, lane_blocks):
    start = count(names < owner * width)
    base = pl.multiple_of((start // 8) * 8, 8)
    size = CAP + 8
    lanes = [pltpu.roll(us_ref[k, pl.ds(base, size), :], size - (start - base), 0)[:CAP] for k in lane_blocks]
    return jnp.concatenate(lanes, axis=1)


def cut(us_ref, names, owner, width, w):
    u = rows_of(us_ref, names, owner, width, range(us_ref.shape[0]))[:, :w]
    return split(jnp.concatenate([u, jnp.zeros((WIDE - CAP, w), jnp.float32)], axis=0))


def place_kernel(direct, nc, *refs):
    u_refs, us_ref = refs[:-1], refs[-1]
    end = us_ref.shape[1] - CAP - 8
    us_ref[:, end:, :] = jnp.zeros((us_ref.shape[0], CAP + 8, LANES), jnp.float32)
    if direct:
        for owner, u_ref in zip(ring_owners(nc, lax.axis_index("pcol")), u_refs):
            place_rows(us_ref, u_ref[...], owner)
    else:
        pl.loop(0, nc)(lambda k: place_rows(us_ref, u_refs[0][k], k))


def last_kernel(nc, width, structure_ref, before_ref, *refs):
    us_ref, own_ref = refs[-2:]
    c = lax.axis_index("pcol")
    us_ref[...] = before_ref[...]
    if len(refs) > 2:
        place_rows(us_ref, refs[0][...], ring_owners(nc, c)[-1])
    names = structure_ref[...].reshape(1, -1)
    w = own_ref.shape[1]
    own_ref[...] = rows_of(us_ref, names, c // 2, width, [c & 1] if len(refs) > 2 else [0])[:, :w]


def row_order(names, c, rows, nc, slots, direct):
    n = names.shape[1]
    z = c // 2
    lg = log2(nc)
    row = c * rows + lax.broadcasted_iota(jnp.int32, (rows, n), 0)
    rank = jnp.sum(one_hot(names < row), axis=1, keepdims=True).astype(jnp.int32)
    member = jnp.sum(one_hot(names == row), axis=1, keepdims=True)
    turn = rank & (nc - 1)
    ahead = (count(names < c * rows) - turn + nc - 1) >> lg
    block = turn >> 1
    if direct:
        block = (block - z) & (nc // 2 - 1)
    block = 2 * block + (turn & 1)
    slot = jnp.where(member > 0.5, block * slots + (rank >> lg) - ahead, -1)
    at = lax.broadcasted_iota(jnp.int32, (rows, nc * slots), 1)
    return one_hot(at == slot).T.astype(BF16)


def order_kernel(direct, slots, structure_ref, to_ref):
    nc = to_ref.shape[0] // slots
    rows = to_ref.shape[1]
    names = structure_ref[...].reshape(1, -1)
    to_ref[...] = row_order(names, lax.axis_index("pcol"), rows, nc, slots, direct)


def near_kernel(owners, rest, structure_ref, us_ref, *refs):
    block_refs, (image_ref, uh_ref, ul_ref) = refs[:-3], refs[-3:]
    rows, w = image_ref.shape
    width = rows * 2
    names = structure_ref[...].reshape(1, -1)
    r = lax.axis_index("prow")
    image = jnp.zeros((rows, w), jnp.float32)
    for owner, block_ref in zip(owners(r), block_refs):
        image = image + block_term(block_ref, *cut(us_ref, names, owner, width, w), rows)
    image_ref[...] = image
    if rest is None:

        @pl.loop(0, uh_ref.shape[0])
        def _(k):
            uh_ref[k], ul_ref[k] = cut(us_ref, names, k, width, w)

    else:
        for k, owner in enumerate(rest(r)):
            uh_ref[k], ul_ref[k] = cut(us_ref, names, owner, width, w)


def image_kernel(direct, uh_ref, ul_ref, part_ref, to_ref, *refs):
    n_in = uh_ref.shape[0] if direct else 1
    block_refs, out_refs = refs[:n_in], refs[n_in:]
    n_out = len(out_refs)
    rows = part_ref.shape[0]
    image = part_ref[...]
    if direct:
        for k, block_ref in enumerate(block_refs):
            image = image + block_term(block_ref, uh_ref[k], ul_ref[k], rows)
    else:
        stack = block_refs[0]
        add = lambda b, v: v + block_term(stack.at[b], uh_ref[b], ul_ref[b], rows)
        image = lax.fori_loop(0, stack.shape[0], add, image)
    image = pick_rows(to_ref[...], image)
    out_refs[0][...] = image
    size = image.shape[0] // n_out
    for k in range(1, n_out):
        out_refs[k][...] = image[size * k : size * (k + 1)]


def turn_kernel(direct, slots, owners, structure_ref, *refs):
    from_ref, high_ref, low_ref, held_ref = refs[-4:]
    nz, wd = high_ref.shape[:2]
    nc = 2 * nz
    lg = log2(nc)
    rows = slots * nc
    n = structure_ref.shape[0]
    m = n // nc
    names = structure_ref[...].reshape(1, -1)
    c = lax.axis_index("pcol")
    z, x = c // 2, c & 1

    start, middle = count(names < 2 * z * rows), count(names < (2 * z + 1) * rows)
    named = pltpu.roll(jnp.broadcast_to(names, (8, n)), lax.rem(n - start, n), 1)[:1, :CAP]
    index = start + lax.broadcasted_iota(jnp.int32, (1, CAP), 1)
    half = jnp.where(named >= (2 * z + 1) * rows, 1, 0)
    turn = index & (nc - 1)
    ahead = (jnp.where(half == 1, middle, start) - turn + nc - 1) >> lg
    block = turn >> 1
    if direct:
        block = (block - z) & (nz - 1)
    slot = (2 * block + (turn & 1)) * slots + (index >> lg) - ahead + (half ^ x) * rows
    slot = jnp.where((named >= 2 * z * rows) & (named < (2 * z + 2) * rows), slot, -1)
    at = lax.broadcasted_iota(jnp.int32, (2 * rows, CAP), 0)
    place = one_hot(at == slot).astype(BF16)

    def put(owner, u_ref):
        where = ((owner - z) & (nz - 1)) if direct else owner
        high, low = split(u_ref[...].T)
        held_ref[pl.ds(pl.multiple_of(where * wd, wd), wd), :] = high
        held_ref[pl.ds(pl.multiple_of((where + nz) * wd, wd), wd), :] = low

    each(refs[:-4], owners(lax.axis_index("prow")) if direct else None, put)
    turned = lax.dot_general(held_ref[...], place, (((1,), (1,)), ((), ())), preferred_element_type=jnp.float32)
    turned = turned.astype(BF16).reshape(2, nz, wd, 2 * rows)
    high_ref[...] = turned[0]
    low_ref[...] = turned[1]

    own = lax.broadcasted_iota(jnp.int32, (m, n), 1) - nc * lax.broadcasted_iota(jnp.int32, (m, n), 0)
    mine = jnp.sum(jnp.where(own == c, names, 0).astype(jnp.float32), axis=1, keepdims=True)
    source = jnp.zeros((m, 1), jnp.int32)
    before = jnp.zeros((m, 1), jnp.int32)
    for k in range(1, nc):
        less = mine < float(k * rows)
        source = source + jnp.where(less, 0, 1)
        before = jnp.where(less, before, count(less))
    block = source >> 1
    if direct:
        block = (z - block) & (nz - 1)
    block = block + nz * ((source ^ c) & 1)
    slot = block * slots + lax.broadcasted_iota(jnp.int32, (m, 1), 0) - before
    at = lax.broadcasted_iota(jnp.int32, (m, rows), 1)
    from_ref[...] = one_hot(at == slot).astype(BF16)


def correction_kernel(high_ref, low_ref, mine_ref, other_ref, *out_refs):
    sh, sl = split(jnp.concatenate([mine_ref[...], other_ref[...]], axis=0))

    def term(t):
        return dot(high_ref[t], sh) + (dot(high_ref[t], sl) + dot(low_ref[t], sh))

    if len(out_refs) > 1:
        for t, out_ref in enumerate(out_refs):
            out_ref[...] = term(t)
    else:

        @pl.loop(0, out_refs[0].shape[0])
        def _(t):
            out_refs[0][t] = term(t)


def part_kernel(slots, *refs):
    mine_ref, theirs_ref = refs[-2:]
    first = (lax.axis_index("pcol") & 1) == 0
    blocks = mine_ref.shape[0] // slots
    mine, theirs = [], []
    for ref in refs[:-2]:
        for k in range(blocks // len(refs[:-2])):
            low = ref[2 * slots * k : 2 * slots * k + slots, :]
            high = ref[2 * slots * k + slots : 2 * slots * (k + 1), :]
            mine.append(jnp.where(first, low, high))
            theirs.append(jnp.where(first, high, low))
    mine_ref[...] = jnp.concatenate(mine, axis=0)
    theirs_ref[...] = jnp.concatenate(theirs, axis=0)


def pick_kernel(from_ref, mine_ref, other_ref, out_ref):
    out_ref[...] = -pick_rows(from_ref[...], jnp.concatenate([mine_ref[...], other_ref[...]], axis=0))


def call(kernel, out_shape, *args, flops=0, vmem=20, **kw):
    many = isinstance(out_shape, (list, tuple))
    size = sum(v.size * v.dtype.itemsize for v in jax.tree.leaves((out_shape, args)))
    kw = {"in_specs": [VMEM] * len(args)} | kw
    return pl.pallas_call(
        kernel,
        out_shape=out_shape,
        out_specs=[VMEM] * len(out_shape) if many else VMEM,
        cost_estimate=pl.CostEstimate(flops=flops, bytes_accessed=size, transcendentals=0),
        compiler_params=pltpu.CompilerParams(vmem_limit_bytes=vmem * 2**20),
        **kw,
    )(*args)


def swap(v, axis, size):
    return lax.ppermute(v, axis, [(k, k ^ 1) for k in range(size)])


def spread(v, size):
    blocks = [v, swap(v, "prow", size)]
    for t in range(1, size // 2):
        for flip in range(2):
            blocks.append(lax.ppermute(v, "prow", [(k, ((k + 2 * t) % size) ^ flip) for k in range(size)]))
    return blocks


def relative_owners(size, r):
    out = []
    for t in range(size // 2):
        owner = (r - 2 * t) & (size - 1)
        out += [owner, owner ^ 1]
    return out


def ring_gather(u, nc, aside):
    ring = [2 * z for z in range(nc // 2)] + [2 * z + 1 for z in reversed(range(nc // 2))]
    pairs = [(ring[q - 1], ring[q]) for q in range(nc)]
    back = [(b, a) for a, b in pairs]
    blocks = [u]
    up = down = u
    for step in range(1, nc // 2):
        up, down = lax.ppermute(up, "pcol", pairs), lax.ppermute(down, "pcol", back)
        if step == 1:
            up, down = lax.optimization_barrier((up, down))
        blocks += [up, down]
    last, aside = lax.optimization_barrier((lax.ppermute(up, "pcol", pairs), aside))
    return blocks + [last], aside


def ring_owners(nc, c):
    q = jnp.where((c & 1) == 0, c >> 1, nc - 1 - (c >> 1))
    out = []
    for k in range(nc):
        step = (k + 1) // 2
        at = (q - step if k % 2 else q + step) & (nc - 1)
        out.append(jnp.where(at < nc // 2, 2 * at, 2 * (nc - 1 - at) + 1))
    return out


def per_device(sigma_top, structure, u_panel, d_term):
    nc, nr = lax.axis_size("pcol"), lax.axis_size("prow")
    c = lax.axis_index("pcol")
    nz = nc // 2
    rows, cols = sigma_top.shape
    m, w = u_panel.shape
    wd = w // 2
    n = structure.shape[0]
    slots = -(-rows // nc)
    direct = nc <= 8
    names = structure
    groups = [[2 * k + x for k in range(nz)] for x in range(2)]
    owners = functools.partial(relative_owners, nr)

    chosen = call(
        select_kernel,
        f32(rows * CAP // LANES, LANES),
        names,
        sigma_top,
        in_specs=[VMEM, HBM],
        scratch_shapes=[pltpu.VMEM((rows, cols), jnp.float32), pltpu.SemaphoreType.DMA((2,))],
        flops=4 * rows * cols * WIDE,
        vmem=52,
    )
    to = call(functools.partial(order_kernel, direct, slots), bf16(nc * slots, rows), names)
    if direct:
        u_all, to = ring_gather(u_panel, nc, to)
    else:
        u_all = [lax.all_gather(u_panel, "pcol")]
    term = 6 * rows * WIDE * w
    placed = f32(-(-w // LANES), n + CAP + 8, LANES)
    early, late = (u_all[:-1], u_all[-1:]) if direct else (u_all, [])
    before = call(functools.partial(place_kernel, direct, nc), placed, *early, flops=8 * term)
    us, own = call(
        functools.partial(last_kernel, nc, cols),
        [placed, f32(CAP, wd if direct else w)],
        names,
        before,
        *late,
        flops=term,
    )
    near, later = [], []
    if direct:
        near = [chosen, swap(chosen, "prow", nr)]
        for t in range(1, nr // 2):
            far = lax.ppermute(chosen, "prow", [(k, (k + 2 * t) % nr) for k in range(nr)])
            far, _ = lax.optimization_barrier((far, own))
            near.append(far)
            later.append(swap(far, "prow", nr))
    else:
        later = [lax.all_gather(chosen, "prow")]
    halves = bf16(len(later) if direct else nr, WIDE, w)
    image, uh, ul = call(
        functools.partial(
            near_kernel, lambda r: owners(r)[:2] + owners(r)[2::2], (lambda r: owners(r)[3::2]) if direct else None
        ),
        [f32(rows, w), halves, halves],
        names,
        us,
        *near,
        flops=3 * term,
    )
    if direct:
        own, _ = lax.optimization_barrier((own, near[2]))
        owned = spread(own, nr)
        owned[1], to = lax.optimization_barrier((owned[1], to))
    sent = call(
        functools.partial(image_kernel, direct),
        [f32(nc * slots, w)] + [f32(2 * slots, w)] * ((nz - 1) * direct),
        uh,
        ul,
        image,
        to,
        *later,
        flops=term,
    )
    whole = sent[0]
    other = swap(whole, "pcol", nc)
    if direct:
        got = [whole]
        for t in range(1, nz):
            got.append(lax.ppermute(sent[t], "pcol", [(k, (k + 2 * t) % nc) for k in range(nc)]))
    else:
        blocks = whole.reshape(nz, 2 * slots, w)
        blocks = lax.all_to_all(blocks, "pcol", split_axis=0, concat_axis=0, axis_index_groups=groups, tiled=True)
        got = [blocks.reshape(nc * slots, w)]
        own = jnp.where(jnp.bitwise_and(c, 1) == 0, own[:, :wd], own[:, wd:])
        owned = [lax.all_gather(own, "prow")]

    turned = bf16(nz, wd, 2 * nc * slots)
    source, high, low = call(
        functools.partial(turn_kernel, direct, slots, owners),
        [bf16(m, nc * slots), turned, turned],
        names,
        *owned,
        scratch_shapes=[pltpu.VMEM((2 * nz * wd, CAP), BF16)],
        flops=8 * nz * wd * nc * slots * CAP,
    )
    parts = [f32(wd, w)] * nz if direct else [f32(nz, wd, w)]
    got, _ = lax.optimization_barrier((got, source))
    mine, theirs = call(functools.partial(part_kernel, slots), [f32(nz * slots, w)] * 2, *got, flops=2 * term)
    other, _ = lax.optimization_barrier((other, mine))
    terms = call(correction_kernel, parts, high, low, whole, other, flops=term)
    theirs, _ = lax.optimization_barrier((theirs, terms[0]))
    sigma_sj = call(pick_kernel, f32(m, w), source, mine, swap(theirs, "pcol", nc), flops=term // 4)
    if direct:
        total = terms[0]
        for t in range(1, nz):
            total = total + lax.ppermute(terms[t], "pcol", [(k, (k + 2 * t) % nc) for k in range(nc)])
    else:
        terms = lax.all_to_all(terms[0], "pcol", split_axis=0, concat_axis=0, axis_index_groups=groups, tiled=True)
        total = jnp.sum(terms, axis=0)
    sigma_sj, d_term = lax.optimization_barrier((sigma_sj, d_term))
    return sigma_sj, d_term + total


def solution(mesh):
    placed = (P("pcol", "prow"), P(), P("pcol", "prow"), P("pcol", "prow"))
    return jax.shard_map(
        per_device,
        mesh=mesh,
        in_specs=placed,
        out_specs=(P("pcol", "prow"), P("pcol", "prow")),
        check_vma=False,
    )
```

```python
import functools

import jax
import jax.numpy as jnp
from jax import lax
from jax.experimental import pallas as pl
from jax.experimental.pallas import tpu as pltpu
from jax.sharding import PartitionSpec as P

LANES = 128
BLOCK_CAP = 560
CAP = -(-BLOCK_CAP // 64) * 64
FULL = CAP // LANES
WIDE = (FULL + 1) * LANES
BF16 = jnp.bfloat16
VMEM = pl.BlockSpec(memory_space=pltpu.VMEM)
HBM = pl.BlockSpec(memory_space=pltpu.HBM)


def f32(*shape):
    return jax.ShapeDtypeStruct(shape, jnp.float32)


def bf16(*shape):
    return jax.ShapeDtypeStruct(shape, BF16)


def split(v):
    high = v.astype(BF16)
    return high, (v - high.astype(jnp.float32)).astype(BF16)


def split3(v):
    high = v.astype(BF16)
    mid, low = split(v - high.astype(jnp.float32))
    return high, mid, low


def dot(a, b):
    return jnp.dot(a, b, preferred_element_type=jnp.float32)


def pick_rows(place, v):
    high, mid, low = split3(v)
    return dot(place, high) + (dot(place, mid) + dot(place, low))


def one_hot(mask):
    return jnp.where(mask, 1.0, 0.0)


def count(mask):
    return jnp.sum(jnp.where(mask, 1.0, 0.0)).astype(jnp.int32)


def log2(size):
    return size.bit_length() - 1


def each(refs, owners, fn):
    if owners is None:
        pl.loop(0, refs[0].shape[0])(lambda i: fn(i, refs[0].at[i]))
    else:
        for owner, ref in zip(owners, refs):
            fn(owner, ref)


def select_kernel(structure_ref, sigma_ref, out_ref, held_ref, sems):
    rows, cols = held_ref.shape
    n = structure_ref.shape[0]
    parts = sems.shape[0]
    part = rows // parts
    copies = []
    for k in range(parts):
        at = pl.ds(part * k, part)
        copies.append(pltpu.make_async_copy(sigma_ref.at[at, :], held_ref.at[at, :], sems.at[k]))
        copies[-1].start()
    first = lax.axis_index("prow") * cols
    listed = structure_ref[...].reshape(1, -1)
    names = jnp.broadcast_to(listed, (8, n))
    shift = lax.rem(n - count(listed < first), n)
    named = pltpu.roll(names, shift, 1)[:1, :CAP] - first
    named = jnp.concatenate([named, named[:, FULL * LANES :]], axis=1)
    step = 2 * LANES
    places = []
    for k in range(0, WIDE, step):
        at = lax.broadcasted_iota(jnp.int32, (cols - k, min(step, WIDE - k)), 0) + k
        places.append(one_hot(at == named[:, k : k + step]).astype(BF16))
    for k in range(parts):
        copies[k].wait()
        both = jnp.concatenate(split(held_ref[part * k : part * (k + 1), :]), axis=0)
        picked = [dot(both[:, step * i :], place) for i, place in enumerate(places)]
        picked = jnp.concatenate(picked, axis=1)
        picked = picked[:part] + picked[part:]
        for i in range(FULL):
            at = rows * i + part * k
            out_ref[at : at + part, :] = picked[:, LANES * i : LANES * (i + 1)]
        at = rows * FULL + part * (k % (parts // 2))
        if k < parts // 2:
            out_ref[at : at + part, : LANES // 2] = picked[:, FULL * LANES : CAP]
        else:
            out_ref[at : at + part, LANES // 2 :] = picked[:, CAP:]


def block_term(block_ref, uh, ul, rows):
    parts = [block_ref[rows * i : rows * (i + 1), :] for i in range(FULL)]
    tail = block_ref[rows * FULL : rows * FULL + rows // 2, :]
    parts.append(jnp.concatenate([tail, pltpu.roll(tail, LANES // 2, 1)], axis=0))
    halves = [split(p) for p in parts]
    highs, lows = [h for h, _ in halves], [l for _, l in halves]
    left = jnp.concatenate(highs + highs + lows, axis=1)
    return dot(left, jnp.concatenate([uh, ul, uh], axis=0))


def place_rows(us_ref, u, owner):
    m, w = u.shape
    nc = (us_ref.shape[1] - CAP - 8) // m
    if w % LANES:
        u = jnp.concatenate([u, jnp.zeros((m, LANES - w % LANES), jnp.float32)], axis=1)
    for i in range(us_ref.shape[0]):
        us_ref[i, pl.ds(owner, m, stride=nc), :] = u[:, LANES * i : LANES * (i + 1)]


def rows_of(us_ref, names, owner, width, lane_blocks):
    start = count(names < owner * width)
    base = pl.multiple_of((start // 8) * 8, 8)
    size = CAP + 8
    lanes = [pltpu.roll(us_ref[k, pl.ds(base, size), :], size - (start - base), 0)[:CAP] for k in lane_blocks]
    return jnp.concatenate(lanes, axis=1)


def cut(us_ref, names, owner, width, w):
    u = rows_of(us_ref, names, owner, width, range(us_ref.shape[0]))[:, :w]
    return split(jnp.concatenate([u, jnp.zeros((WIDE - CAP, w), jnp.float32)], axis=0))


def place_kernel(direct, nc, *refs):
    u_refs, us_ref = refs[:-1], refs[-1]
    end = us_ref.shape[1] - CAP - 8
    us_ref[:, end:, :] = jnp.zeros((us_ref.shape[0], CAP + 8, LANES), jnp.float32)
    if direct:
        for owner, u_ref in zip(ring_owners(nc, lax.axis_index("pcol")), u_refs):
            place_rows(us_ref, u_ref[...], owner)
    else:
        pl.loop(0, nc)(lambda k: place_rows(us_ref, u_refs[0][k], k))


def last_kernel(nc, width, structure_ref, before_ref, *refs):
    us_ref, own_ref = refs[-2:]
    c = lax.axis_index("pcol")
    us_ref[...] = before_ref[...]
    if len(refs) > 2:
        place_rows(us_ref, refs[0][...], ring_owners(nc, c)[-1])
    names = structure_ref[...].reshape(1, -1)
    w = own_ref.shape[1]
    own_ref[...] = rows_of(us_ref, names, c // 2, width, [c & 1] if len(refs) > 2 else [0])[:, :w]


def row_order(names, c, rows, nc, slots, direct):
    n = names.shape[1]
    z = c // 2
    lg = log2(nc)
    row = c * rows + lax.broadcasted_iota(jnp.int32, (rows, n), 0)
    rank = jnp.sum(one_hot(names < row), axis=1, keepdims=True).astype(jnp.int32)
    member = jnp.sum(one_hot(names == row), axis=1, keepdims=True)
    turn = rank & (nc - 1)
    ahead = (count(names < c * rows) - turn + nc - 1) >> lg
    block = turn >> 1
    if direct:
        block = (block - z) & (nc // 2 - 1)
    block = 2 * block + (turn & 1)
    slot = jnp.where(member > 0.5, block * slots + (rank >> lg) - ahead, -1)
    at = lax.broadcasted_iota(jnp.int32, (rows, nc * slots), 1)
    return one_hot(at == slot).T.astype(BF16)


def order_kernel(direct, slots, structure_ref, to_ref, place_ref, from_ref):
    nc = to_ref.shape[0] // slots
    rows = to_ref.shape[1]
    nz = nc // 2
    lg = log2(nc)
    names = structure_ref[...].reshape(1, -1)
    n = names.shape[1]
    m = n // nc
    c = lax.axis_index("pcol")
    z, x = c // 2, c & 1
    to_ref[...] = row_order(names, c, rows, nc, slots, direct)

    start, middle = count(names < 2 * z * rows), count(names < (2 * z + 1) * rows)
    named = pltpu.roll(jnp.broadcast_to(names, (8, n)), lax.rem(n - start, n), 1)[:1, :CAP]
    index = start + lax.broadcasted_iota(jnp.int32, (1, CAP), 1)
    half = jnp.where(named >= (2 * z + 1) * rows, 1, 0)
    turn = index & (nc - 1)
    ahead = (jnp.where(half == 1, middle, start) - turn + nc - 1) >> lg
    block = turn >> 1
    if direct:
        block = (block - z) & (nz - 1)
    slot = (2 * block + (turn & 1)) * slots + (index >> lg) - ahead + (half ^ x) * rows
    slot = jnp.where((named >= 2 * z * rows) & (named < (2 * z + 2) * rows), slot, -1)
    at = lax.broadcasted_iota(jnp.int32, (2 * rows, CAP), 0)
    place_ref[...] = one_hot(at == slot).T.astype(BF16)

    own = lax.broadcasted_iota(jnp.int32, (m, n), 1) - nc * lax.broadcasted_iota(jnp.int32, (m, n), 0)
    mine = jnp.sum(jnp.where(own == c, names, 0).astype(jnp.float32), axis=1, keepdims=True)
    source = jnp.zeros((m, 1), jnp.int32)
    before = jnp.zeros((m, 1), jnp.int32)
    for k in range(1, nc):
        less = mine < float(k * rows)
        source = source + jnp.where(less, 0, 1)
        before = jnp.where(less, before, count(less))
    block = source >> 1
    if direct:
        block = (z - block) & (nz - 1)
    block = block + nz * ((source ^ c) & 1)
    slot = block * slots + lax.broadcasted_iota(jnp.int32, (m, 1), 0) - before
    at = lax.broadcasted_iota(jnp.int32, (m, rows), 1)
    from_ref[...] = one_hot(at == slot).astype(BF16)


def near_kernel(owners, rest, structure_ref, us_ref, *refs):
    block_refs, (image_ref, uh_ref, ul_ref) = refs[:-3], refs[-3:]
    rows, w = image_ref.shape
    width = rows * 2
    names = structure_ref[...].reshape(1, -1)
    r = lax.axis_index("prow")
    image = jnp.zeros((rows, w), jnp.float32)
    for owner, block_ref in zip(owners(r), block_refs):
        image = image + block_term(block_ref, *cut(us_ref, names, owner, width, w), rows)
    image_ref[...] = image
    if rest is None:

        @pl.loop(0, uh_ref.shape[0])
        def _(k):
            uh_ref[k], ul_ref[k] = cut(us_ref, names, k, width, w)

    else:
        for k, owner in enumerate(rest(r)):
            uh_ref[k], ul_ref[k] = cut(us_ref, names, owner, width, w)


def far_terms(first, uh_ref, ul_ref, image, block_refs):
    rows = image.shape[0]
    for k, block_ref in enumerate(block_refs):
        image = image + block_term(block_ref, uh_ref[first + 2 * k], ul_ref[first + 2 * k], rows)
    return image


def far_kernel(first, uh_ref, ul_ref, part_ref, *refs):
    refs[-1][...] = far_terms(first, uh_ref, ul_ref, part_ref[...], refs[:-1])


def image_kernel(direct, uh_ref, ul_ref, part_ref, to_ref, *refs):
    n_in = uh_ref.shape[0] // 2 if direct else 1
    block_refs, out_refs = refs[:n_in], refs[n_in:]
    n_out = len(out_refs)
    rows = part_ref.shape[0]
    image = part_ref[...]
    if direct:
        image = far_terms(1, uh_ref, ul_ref, image, block_refs)
    else:
        stack = block_refs[0]
        add = lambda b, v: v + block_term(stack.at[b], uh_ref[b], ul_ref[b], rows)
        image = lax.fori_loop(0, stack.shape[0], add, image)
    image = pick_rows(to_ref[...], image)
    out_refs[0][...] = image
    size = image.shape[0] // n_out
    for k in range(1, n_out):
        out_refs[k][...] = image[size * k : size * (k + 1)]


def turn_kernel(direct, owners, place_ref, *refs):
    high_ref, low_ref, held_ref = refs[-3:]
    nz, wd, size = high_ref.shape
    z = lax.axis_index("pcol") // 2

    def put(owner, u_ref):
        where = ((owner - z) & (nz - 1)) if direct else owner
        high, low = split(u_ref[...].T)
        held_ref[pl.ds(pl.multiple_of(where * wd, wd), wd), :] = high
        held_ref[pl.ds(pl.multiple_of((where + nz) * wd, wd), wd), :] = low

    each(refs[:-3], owners(lax.axis_index("prow")) if direct else None, put)
    turned = dot(held_ref[...], place_ref[...]).astype(BF16).reshape(2, nz, wd, size)
    high_ref[...] = turned[0]
    low_ref[...] = turned[1]


def correction_kernel(high_ref, low_ref, mine_ref, other_ref, *out_refs):
    sh, sl = split(jnp.concatenate([mine_ref[...], other_ref[...]], axis=0))

    def term(t):
        return dot(high_ref[t], sh) + (dot(high_ref[t], sl) + dot(low_ref[t], sh))

    if len(out_refs) > 1:
        for t, out_ref in enumerate(out_refs):
            out_ref[...] = term(t)
    else:

        @pl.loop(0, out_refs[0].shape[0])
        def _(t):
            out_refs[0][t] = term(t)


def part_kernel(slots, *refs):
    mine_ref, theirs_ref = refs[-2:]
    first = (lax.axis_index("pcol") & 1) == 0
    blocks = mine_ref.shape[0] // slots
    mine, theirs = [], []
    for ref in refs[:-2]:
        for k in range(blocks // len(refs[:-2])):
            low = ref[2 * slots * k : 2 * slots * k + slots, :]
            high = ref[2 * slots * k + slots : 2 * slots * (k + 1), :]
            mine.append(jnp.where(first, low, high))
            theirs.append(jnp.where(first, high, low))
    mine_ref[...] = jnp.concatenate(mine, axis=0)
    theirs_ref[...] = jnp.concatenate(theirs, axis=0)


def pick_kernel(from_ref, mine_ref, other_ref, out_ref):
    out_ref[...] = -pick_rows(from_ref[...], jnp.concatenate([mine_ref[...], other_ref[...]], axis=0))


def call(kernel, out_shape, *args, flops=0, vmem=20, **kw):
    many = isinstance(out_shape, (list, tuple))
    size = sum(v.size * v.dtype.itemsize for v in jax.tree.leaves((out_shape, args)))
    kw = {"in_specs": [VMEM] * len(args)} | kw
    return pl.pallas_call(
        kernel,
        out_shape=out_shape,
        out_specs=[VMEM] * len(out_shape) if many else VMEM,
        cost_estimate=pl.CostEstimate(flops=flops, bytes_accessed=size, transcendentals=0),
        compiler_params=pltpu.CompilerParams(vmem_limit_bytes=vmem * 2**20),
        **kw,
    )(*args)


def swap(v, axis, size):
    return lax.ppermute(v, axis, [(k, k ^ 1) for k in range(size)])


def spread(v, size, after):
    blocks = [v, swap(v, "prow", size)]
    v, _ = lax.optimization_barrier((v, after))
    for t in range(1, size // 2):
        for flip in range(2):
            blocks.append(lax.ppermute(v, "prow", [(k, ((k + 2 * t) % size) ^ flip) for k in range(size)]))
    return blocks


def relative_owners(size, r):
    out = []
    for t in range(size // 2):
        owner = (r - 2 * t) & (size - 1)
        out += [owner, owner ^ 1]
    return out


def ring_gather(u, nc, aside):
    ring = [2 * z for z in range(nc // 2)] + [2 * z + 1 for z in reversed(range(nc // 2))]
    pairs = [(ring[q - 1], ring[q]) for q in range(nc)]
    back = [(b, a) for a, b in pairs]
    blocks = [u]
    up = down = u
    for step in range(1, nc // 2):
        up, down = lax.ppermute(up, "pcol", pairs), lax.ppermute(down, "pcol", back)
        if step == 1:
            up, down = lax.optimization_barrier((up, down))
        blocks += [up, down]
    last, aside = lax.optimization_barrier((lax.ppermute(up, "pcol", pairs), aside))
    return blocks + [last], aside


def ring_owners(nc, c):
    q = jnp.where((c & 1) == 0, c >> 1, nc - 1 - (c >> 1))
    out = []
    for k in range(nc):
        step = (k + 1) // 2
        at = (q - step if k % 2 else q + step) & (nc - 1)
        out.append(jnp.where(at < nc // 2, 2 * at, 2 * (nc - 1 - at) + 1))
    return out


def per_device(sigma_top, structure, u_panel, d_term):
    nc, nr = lax.axis_size("pcol"), lax.axis_size("prow")
    c = lax.axis_index("pcol")
    nz = nc // 2
    rows, cols = sigma_top.shape
    m, w = u_panel.shape
    wd = w // 2
    n = structure.shape[0]
    slots = -(-rows // nc)
    direct = nc <= 8
    names = structure
    groups = [[2 * k + x for k in range(nz)] for x in range(2)]
    owners = functools.partial(relative_owners, nr)

    chosen = call(
        select_kernel,
        f32(rows * CAP // LANES, LANES),
        names,
        sigma_top,
        in_specs=[VMEM, HBM],
        scratch_shapes=[pltpu.VMEM((rows, cols), jnp.float32), pltpu.SemaphoreType.DMA((2,))],
        flops=4 * rows * cols * WIDE,
        vmem=52,
    )
    to, place, source = call(
        functools.partial(order_kernel, direct, slots),
        [bf16(nc * slots, rows), bf16(CAP, 2 * nc * slots), bf16(m, nc * slots)],
        names,
    )
    if direct:
        u_all, to = ring_gather(u_panel, nc, to)
    else:
        u_all = [lax.all_gather(u_panel, "pcol")]
    term = 6 * rows * WIDE * w
    placed = f32(-(-w // LANES), n + CAP + 8, LANES)
    early, late = (u_all[:-1], u_all[-1:]) if direct else (u_all, [])
    before = call(functools.partial(place_kernel, direct, nc), placed, *early, flops=8 * term)
    us, own = call(
        functools.partial(last_kernel, nc, cols),
        [placed, f32(CAP, wd if direct else w)],
        names,
        before,
        *late,
        flops=term,
    )
    halves = bf16(nr - 2 if direct else nr, WIDE, w)
    near = []
    if direct:
        again, _ = lax.optimization_barrier((chosen, u_all[1]))
        near = [chosen, swap(again, "prow", nr)]
    image, uh, ul = call(
        functools.partial(near_kernel, lambda r: owners(r)[:2], (lambda r: owners(r)[2:]) if direct else None),
        [f32(rows, w), halves, halves],
        names,
        us,
        *near,
        flops=3 * term,
    )
    if direct:
        beside, later = [], []
        for t in range(1, nr // 2):
            far = lax.ppermute(chosen, "prow", [(k, (k + 2 * t) % nr) for k in range(nr)])
            far, _ = lax.optimization_barrier((far, image))
            beside.append(far)
            later.append(swap(far, "prow", nr))
        image = call(functools.partial(far_kernel, 0), f32(rows, w), uh, ul, image, *beside, flops=term)
    else:
        later = [lax.all_gather(chosen, "prow")]
    if direct:
        owned = spread(own, nr, beside[0])
        owned[1], to = lax.optimization_barrier((owned[1], to))
    sent = call(
        functools.partial(image_kernel, direct),
        [f32(nc * slots, w)] + [f32(2 * slots, w)] * ((nz - 1) * direct),
        uh,
        ul,
        image,
        to,
        *later,
        flops=term,
    )
    whole = sent[0]
    other = swap(whole, "pcol", nc)
    if direct:
        got = [whole]
        for t in range(1, nz):
            got.append(lax.ppermute(sent[t], "pcol", [(k, (k + 2 * t) % nc) for k in range(nc)]))
    else:
        blocks = whole.reshape(nz, 2 * slots, w)
        blocks = lax.all_to_all(blocks, "pcol", split_axis=0, concat_axis=0, axis_index_groups=groups, tiled=True)
        got = [blocks.reshape(nc * slots, w)]
        own = jnp.where(jnp.bitwise_and(c, 1) == 0, own[:, :wd], own[:, wd:])
        owned = [lax.all_gather(own, "prow")]

    turned = bf16(nz, wd, 2 * nc * slots)
    high, low = call(
        functools.partial(turn_kernel, direct, owners),
        [turned, turned],
        place,
        *owned,
        scratch_shapes=[pltpu.VMEM((2 * nz * wd, CAP), BF16)],
        flops=8 * nz * wd * nc * slots * CAP,
    )
    parts = [f32(wd, w)] * nz if direct else [f32(nz, wd, w)]
    got, _ = lax.optimization_barrier((got, high))
    mine, theirs = call(functools.partial(part_kernel, slots), [f32(nz * slots, w)] * 2, *got, flops=2 * term)
    other, _ = lax.optimization_barrier((other, mine))
    terms = call(correction_kernel, parts, high, low, whole, other, flops=term)
    theirs, _ = lax.optimization_barrier((theirs, terms[0]))
    sigma_sj = call(pick_kernel, f32(m, w), source, mine, swap(theirs, "pcol", nc), flops=term // 4)
    if direct:
        total = terms[0]
        for t in range(1, nz):
            total = total + lax.ppermute(terms[t], "pcol", [(k, (k + 2 * t) % nc) for k in range(nc)])
    else:
        terms = lax.all_to_all(terms[0], "pcol", split_axis=0, concat_axis=0, axis_index_groups=groups, tiled=True)
        total = jnp.sum(terms, axis=0)
    sigma_sj, d_term = lax.optimization_barrier((sigma_sj, d_term))
    return sigma_sj, d_term + total


def solution(mesh):
    placed = (P("pcol", "prow"), P(), P("pcol", "prow"), P("pcol", "prow"))
    return jax.shard_map(
        per_device,
        mesh=mesh,
        in_specs=placed,
        out_specs=(P("pcol", "prow"), P("pcol", "prow")),
        check_vma=False,
    )
```

```python
import functools

import jax
import jax.numpy as jnp
from jax import lax
from jax.experimental import pallas as pl
from jax.experimental.pallas import tpu as pltpu
from jax.sharding import PartitionSpec as P

LANES = 128
BLOCK_CAP = 560
CAP = -(-BLOCK_CAP // 64) * 64
FULL = CAP // LANES
WIDE = (FULL + 1) * LANES
BF16 = jnp.bfloat16
VMEM = pl.BlockSpec(memory_space=pltpu.VMEM)
HBM = pl.BlockSpec(memory_space=pltpu.HBM)


def f32(*shape):
    return jax.ShapeDtypeStruct(shape, jnp.float32)


def bf16(*shape):
    return jax.ShapeDtypeStruct(shape, BF16)


def split(v):
    high = v.astype(BF16)
    return high, (v - high.astype(jnp.float32)).astype(BF16)


def split3(v):
    high = v.astype(BF16)
    mid, low = split(v - high.astype(jnp.float32))
    return high, mid, low


def dot(a, b):
    return jnp.dot(a, b, preferred_element_type=jnp.float32)


def pick_rows(place, v):
    high, mid, low = split3(v)
    return dot(place, high) + (dot(place, mid) + dot(place, low))


def one_hot(mask):
    return jnp.where(mask, 1.0, 0.0)


def count(mask):
    return jnp.sum(jnp.where(mask, 1.0, 0.0)).astype(jnp.int32)


def log2(size):
    return size.bit_length() - 1


def each(refs, owners, fn):
    if owners is None:
        pl.loop(0, refs[0].shape[0])(lambda i: fn(i, refs[0].at[i]))
    else:
        for owner, ref in zip(owners, refs):
            fn(owner, ref)


def select_kernel(structure_ref, sigma_ref, out_ref, held_ref, sems):
    rows, cols = held_ref.shape
    n = structure_ref.shape[0]
    parts = sems.shape[0]
    part = rows // parts
    copies = []
    for k in range(parts):
        at = pl.ds(part * k, part)
        copies.append(pltpu.make_async_copy(sigma_ref.at[at, :], held_ref.at[at, :], sems.at[k]))
        copies[-1].start()
    first = lax.axis_index("prow") * cols
    listed = structure_ref[...].reshape(1, -1)
    names = jnp.broadcast_to(listed, (8, n))
    shift = lax.rem(n - count(listed < first), n)
    named = pltpu.roll(names, shift, 1)[:1, :CAP] - first
    named = jnp.concatenate([named, named[:, FULL * LANES :]], axis=1)
    step = 2 * LANES
    places = []
    for k in range(0, WIDE, step):
        at = lax.broadcasted_iota(jnp.int32, (cols - k, min(step, WIDE - k)), 0) + k
        places.append(one_hot(at == named[:, k : k + step]).astype(BF16))
    for k in range(parts):
        copies[k].wait()
        both = jnp.concatenate(split(held_ref[part * k : part * (k + 1), :]), axis=0)
        picked = [dot(both[:, step * i :], place) for i, place in enumerate(places)]
        picked = jnp.concatenate(picked, axis=1)
        picked = picked[:part] + picked[part:]
        for i in range(FULL):
            at = rows * i + part * k
            out_ref[at : at + part, :] = picked[:, LANES * i : LANES * (i + 1)]
        at = rows * FULL + part * (k % (parts // 2))
        if k < parts // 2:
            out_ref[at : at + part, : LANES // 2] = picked[:, FULL * LANES : CAP]
        else:
            out_ref[at : at + part, LANES // 2 :] = picked[:, CAP:]


def block_term(block_ref, uh, ul, rows):
    parts = [block_ref[rows * i : rows * (i + 1), :] for i in range(FULL)]
    tail = block_ref[rows * FULL : rows * FULL + rows // 2, :]
    parts.append(jnp.concatenate([tail, pltpu.roll(tail, LANES // 2, 1)], axis=0))
    halves = [split(p) for p in parts]
    highs, lows = [h for h, _ in halves], [l for _, l in halves]
    left = jnp.concatenate(highs + highs + lows, axis=1)
    return dot(left, jnp.concatenate([uh, ul, uh], axis=0))


def place_rows(us_ref, u, owner):
    m, w = u.shape
    nc = (us_ref.shape[1] - CAP - 8) // m
    if w % LANES:
        u = jnp.concatenate([u, jnp.zeros((m, LANES - w % LANES), jnp.float32)], axis=1)
    for i in range(us_ref.shape[0]):
        us_ref[i, pl.ds(owner, m, stride=nc), :] = u[:, LANES * i : LANES * (i + 1)]


def rows_of(us_ref, names, owner, width, lane_blocks):
    start = count(names < owner * width)
    base = pl.multiple_of((start // 8) * 8, 8)
    size = CAP + 8
    lanes = [pltpu.roll(us_ref[k, pl.ds(base, size), :], size - (start - base), 0)[:CAP] for k in lane_blocks]
    return jnp.concatenate(lanes, axis=1)


def cut(us_ref, names, owner, width, w):
    u = rows_of(us_ref, names, owner, width, range(us_ref.shape[0]))[:, :w]
    return split(jnp.concatenate([u, jnp.zeros((WIDE - CAP, w), jnp.float32)], axis=0))


def place_kernel(direct, nc, *refs):
    u_refs, us_ref = refs[:-1], refs[-1]
    end = us_ref.shape[1] - CAP - 8
    us_ref[:, end:, :] = jnp.zeros((us_ref.shape[0], CAP + 8, LANES), jnp.float32)
    if direct:
        for owner, u_ref in zip(ring_owners(nc, lax.axis_index("pcol")), u_refs):
            place_rows(us_ref, u_ref[...], owner)
    else:
        pl.loop(0, nc)(lambda k: place_rows(us_ref, u_refs[0][k], k))


def last_kernel(nc, width, structure_ref, before_ref, *refs):
    us_ref, own_ref = refs[-2:]
    c = lax.axis_index("pcol")
    us_ref[...] = before_ref[...]
    if len(refs) > 2:
        place_rows(us_ref, refs[0][...], ring_owners(nc, c)[-1])
    names = structure_ref[...].reshape(1, -1)
    w = own_ref.shape[1]
    own_ref[...] = rows_of(us_ref, names, c // 2, width, [c & 1] if len(refs) > 2 else [0])[:, :w]


def row_order(names, c, rows, nc, slots, direct):
    n = names.shape[1]
    z = c // 2
    lg = log2(nc)
    row = c * rows + lax.broadcasted_iota(jnp.int32, (rows, n), 0)
    rank = jnp.sum(one_hot(names < row), axis=1, keepdims=True).astype(jnp.int32)
    member = jnp.sum(one_hot(names == row), axis=1, keepdims=True)
    turn = rank & (nc - 1)
    ahead = (count(names < c * rows) - turn + nc - 1) >> lg
    block = turn >> 1
    if direct:
        block = (block - z) & (nc // 2 - 1)
    block = 2 * block + (turn & 1)
    slot = jnp.where(member > 0.5, block * slots + (rank >> lg) - ahead, -1)
    at = lax.broadcasted_iota(jnp.int32, (rows, nc * slots), 1)
    return one_hot(at == slot).T.astype(BF16)


def order_kernel(direct, slots, structure_ref, to_ref, place_ref, from_ref):
    nc = to_ref.shape[0] // slots
    rows = to_ref.shape[1]
    nz = nc // 2
    lg = log2(nc)
    names = structure_ref[...].reshape(1, -1)
    n = names.shape[1]
    m = n // nc
    c = lax.axis_index("pcol")
    z, x = c // 2, c & 1
    to_ref[...] = row_order(names, c, rows, nc, slots, direct)

    start, middle = count(names < 2 * z * rows), count(names < (2 * z + 1) * rows)
    named = pltpu.roll(jnp.broadcast_to(names, (8, n)), lax.rem(n - start, n), 1)[:1, :CAP]
    index = start + lax.broadcasted_iota(jnp.int32, (1, CAP), 1)
    half = jnp.where(named >= (2 * z + 1) * rows, 1, 0)
    turn = index & (nc - 1)
    ahead = (jnp.where(half == 1, middle, start) - turn + nc - 1) >> lg
    block = turn >> 1
    if direct:
        block = (block - z) & (nz - 1)
    slot = (2 * block + (turn & 1)) * slots + (index >> lg) - ahead + (half ^ x) * rows
    slot = jnp.where((named >= 2 * z * rows) & (named < (2 * z + 2) * rows), slot, -1)
    at = lax.broadcasted_iota(jnp.int32, (2 * rows, CAP), 0)
    place_ref[...] = one_hot(at == slot).T.astype(BF16)

    own = lax.broadcasted_iota(jnp.int32, (m, n), 1) - nc * lax.broadcasted_iota(jnp.int32, (m, n), 0)
    mine = jnp.sum(jnp.where(own == c, names, 0).astype(jnp.float32), axis=1, keepdims=True)
    source = jnp.zeros((m, 1), jnp.int32)
    before = jnp.zeros((m, 1), jnp.int32)
    for k in range(1, nc):
        less = mine < float(k * rows)
        source = source + jnp.where(less, 0, 1)
        before = jnp.where(less, before, count(less))
    block = source >> 1
    if direct:
        block = (z - block) & (nz - 1)
    block = block + nz * ((source ^ c) & 1)
    slot = block * slots + lax.broadcasted_iota(jnp.int32, (m, 1), 0) - before
    at = lax.broadcasted_iota(jnp.int32, (m, rows), 1)
    from_ref[...] = one_hot(at == slot).astype(BF16)


def near_kernel(owners, rest, structure_ref, us_ref, *refs):
    block_refs, (image_ref, uh_ref, ul_ref) = refs[:-3], refs[-3:]
    rows, w = image_ref.shape
    width = rows * 2
    names = structure_ref[...].reshape(1, -1)
    r = lax.axis_index("prow")
    image = jnp.zeros((rows, w), jnp.float32)
    for owner, block_ref in zip(owners(r), block_refs):
        image = image + block_term(block_ref, *cut(us_ref, names, owner, width, w), rows)
    image_ref[...] = image
    if rest is None:

        @pl.loop(0, uh_ref.shape[0])
        def _(k):
            uh_ref[k], ul_ref[k] = cut(us_ref, names, k, width, w)

    else:
        for k, owner in enumerate(rest(r)):
            uh_ref[k], ul_ref[k] = cut(us_ref, names, owner, width, w)


def far_terms(places, uh_ref, ul_ref, image, block_refs):
    rows = image.shape[0]
    for k, block_ref in zip(places, block_refs):
        image = image + block_term(block_ref, uh_ref[k], ul_ref[k], rows)
    return image


def far_kernel(uh_ref, ul_ref, part_ref, *refs):
    places = [0] + list(range(1, uh_ref.shape[0], 2))
    refs[-1][...] = far_terms(places, uh_ref, ul_ref, part_ref[...], refs[:-1])


def image_kernel(direct, uh_ref, ul_ref, part_ref, to_ref, *refs):
    n_in = (uh_ref.shape[0] - 1) // 2 if direct else 1
    block_refs, out_refs = refs[:n_in], refs[n_in:]
    n_out = len(out_refs)
    rows = part_ref.shape[0]
    image = part_ref[...]
    if direct:
        image = far_terms(range(2, uh_ref.shape[0], 2), uh_ref, ul_ref, image, block_refs)
    else:
        stack = block_refs[0]
        add = lambda b, v: v + block_term(stack.at[b], uh_ref[b], ul_ref[b], rows)
        image = lax.fori_loop(0, stack.shape[0], add, image)
    image = pick_rows(to_ref[...], image)
    out_refs[0][...] = image
    size = image.shape[0] // n_out
    for k in range(1, n_out):
        out_refs[k][...] = image[size * k : size * (k + 1)]


def turn_kernel(direct, owners, place_ref, *refs):
    high_ref, low_ref, held_ref = refs[-3:]
    nz, wd, size = high_ref.shape
    z = lax.axis_index("pcol") // 2

    def put(owner, u_ref):
        where = ((owner - z) & (nz - 1)) if direct else owner
        high, low = split(u_ref[...].T)
        held_ref[pl.ds(pl.multiple_of(where * wd, wd), wd), :] = high
        held_ref[pl.ds(pl.multiple_of((where + nz) * wd, wd), wd), :] = low

    each(refs[:-3], owners(lax.axis_index("prow")) if direct else None, put)
    turned = dot(held_ref[...], place_ref[...]).astype(BF16).reshape(2, nz, wd, size)
    high_ref[...] = turned[0]
    low_ref[...] = turned[1]


def correction_kernel(high_ref, low_ref, mine_ref, other_ref, *out_refs):
    sh, sl = split(jnp.concatenate([mine_ref[...], other_ref[...]], axis=0))

    def term(t):
        return dot(high_ref[t], sh) + (dot(high_ref[t], sl) + dot(low_ref[t], sh))

    if len(out_refs) > 1:
        for t, out_ref in enumerate(out_refs):
            out_ref[...] = term(t)
    else:

        @pl.loop(0, out_refs[0].shape[0])
        def _(t):
            out_refs[0][t] = term(t)


def part_kernel(slots, *refs):
    mine_ref, theirs_ref = refs[-2:]
    first = (lax.axis_index("pcol") & 1) == 0
    blocks = mine_ref.shape[0] // slots
    mine, theirs = [], []
    for ref in refs[:-2]:
        for k in range(blocks // len(refs[:-2])):
            low = ref[2 * slots * k : 2 * slots * k + slots, :]
            high = ref[2 * slots * k + slots : 2 * slots * (k + 1), :]
            mine.append(jnp.where(first, low, high))
            theirs.append(jnp.where(first, high, low))
    mine_ref[...] = jnp.concatenate(mine, axis=0)
    theirs_ref[...] = jnp.concatenate(theirs, axis=0)


def pick_kernel(from_ref, mine_ref, other_ref, out_ref):
    out_ref[...] = -pick_rows(from_ref[...], jnp.concatenate([mine_ref[...], other_ref[...]], axis=0))


def call(kernel, out_shape, *args, flops=0, vmem=20, **kw):
    many = isinstance(out_shape, (list, tuple))
    size = flops and sum(v.size * v.dtype.itemsize for v in jax.tree.leaves((out_shape, args)))
    kw = {"in_specs": [VMEM] * len(args)} | kw
    return pl.pallas_call(
        kernel,
        out_shape=out_shape,
        out_specs=[VMEM] * len(out_shape) if many else VMEM,
        cost_estimate=pl.CostEstimate(flops=flops, bytes_accessed=size, transcendentals=0),
        compiler_params=pltpu.CompilerParams(vmem_limit_bytes=vmem * 2**20),
        **kw,
    )(*args)


def swap(v, axis, size):
    return lax.ppermute(v, axis, [(k, k ^ 1) for k in range(size)])


def spread(v, size, after):
    blocks = [v, swap(v, "prow", size)]
    v, _ = lax.optimization_barrier((v, after))
    for t in range(1, size // 2):
        for flip in range(2):
            blocks.append(lax.ppermute(v, "prow", [(k, ((k + 2 * t) % size) ^ flip) for k in range(size)]))
    return blocks


def relative_owners(size, r):
    out = []
    for t in range(size // 2):
        owner = (r - 2 * t) & (size - 1)
        out += [owner, owner ^ 1]
    return out


def ring_gather(u, nc, aside):
    ring = [2 * z for z in range(nc // 2)] + [2 * z + 1 for z in reversed(range(nc // 2))]
    pairs = [(ring[q - 1], ring[q]) for q in range(nc)]
    back = [(b, a) for a, b in pairs]
    blocks = [u]
    up = down = u
    for step in range(1, nc // 2):
        up, down = lax.ppermute(up, "pcol", pairs), lax.ppermute(down, "pcol", back)
        if step == 1:
            up, down = lax.optimization_barrier((up, down))
        blocks += [up, down]
    last, aside = lax.optimization_barrier((lax.ppermute(up, "pcol", pairs), aside))
    return blocks + [last], aside


def ring_owners(nc, c):
    q = jnp.where((c & 1) == 0, c >> 1, nc - 1 - (c >> 1))
    out = []
    for k in range(nc):
        step = (k + 1) // 2
        at = (q - step if k % 2 else q + step) & (nc - 1)
        out.append(jnp.where(at < nc // 2, 2 * at, 2 * (nc - 1 - at) + 1))
    return out


def per_device(sigma_top, structure, u_panel, d_term):
    nc, nr = lax.axis_size("pcol"), lax.axis_size("prow")
    c = lax.axis_index("pcol")
    nz = nc // 2
    rows, cols = sigma_top.shape
    m, w = u_panel.shape
    wd = w // 2
    n = structure.shape[0]
    slots = -(-rows // nc)
    direct = nc <= 8
    names = structure
    groups = [[2 * k + x for k in range(nz)] for x in range(2)]
    owners = functools.partial(relative_owners, nr)

    chosen = call(
        select_kernel,
        f32(rows * CAP // LANES, LANES),
        names,
        sigma_top,
        in_specs=[VMEM, HBM],
        scratch_shapes=[pltpu.VMEM((rows, cols), jnp.float32), pltpu.SemaphoreType.DMA((2,))],
        flops=4 * rows * cols * WIDE,
        vmem=52,
    )
    to, place, source = call(
        functools.partial(order_kernel, direct, slots),
        [bf16(nc * slots, rows), bf16(CAP, 2 * nc * slots), bf16(m, nc * slots)],
        names,
    )
    if direct:
        u_all, to = ring_gather(u_panel, nc, to)
    else:
        u_all = [lax.all_gather(u_panel, "pcol")]
    term = 6 * rows * WIDE * w
    placed = f32(-(-w // LANES), n + CAP + 8, LANES)
    early, late = (u_all[:-1], u_all[-1:]) if direct else (u_all, [])
    before = call(functools.partial(place_kernel, direct, nc), placed, *early, flops=8 * term)
    us, own = call(
        functools.partial(last_kernel, nc, cols),
        [placed, f32(CAP, wd if direct else w)],
        names,
        before,
        *late,
        flops=term,
    )
    halves = bf16(nr - 1 if direct else nr, WIDE, w)
    near = [chosen] if direct else []
    image, uh, ul = call(
        functools.partial(near_kernel, lambda r: owners(r)[:1], (lambda r: owners(r)[1:]) if direct else None),
        [f32(rows, w), halves, halves],
        names,
        us,
        *near,
        flops=0,
    )
    if direct:
        beside, later = [swap(chosen, "prow", nr)], []
        for t in range(1, nr // 2):
            far = lax.ppermute(chosen, "prow", [(k, (k + 2 * t) % nr) for k in range(nr)])
            far, _ = lax.optimization_barrier((far, image))
            beside.append(far)
            later.append(swap(far, "prow", nr))
        image = call(far_kernel, f32(rows, w), uh, ul, image, *beside, flops=1 * term)
    else:
        later = [lax.all_gather(chosen, "prow")]
    if direct:
        owned = spread(own, nr, beside[1])
    sent = call(
        functools.partial(image_kernel, direct),
        [f32(nc * slots, w)] + [f32(2 * slots, w)] * ((nz - 1) * direct),
        uh,
        ul,
        image,
        to,
        *later,
        flops=term,
    )
    whole = sent[0]
    other = swap(whole, "pcol", nc)
    if direct:
        got = [whole]
        for t in range(1, nz):
            got.append(lax.ppermute(sent[t], "pcol", [(k, (k + 2 * t) % nc) for k in range(nc)]))
    else:
        blocks = whole.reshape(nz, 2 * slots, w)
        blocks = lax.all_to_all(blocks, "pcol", split_axis=0, concat_axis=0, axis_index_groups=groups, tiled=True)
        got = [blocks.reshape(nc * slots, w)]
        own = jnp.where(jnp.bitwise_and(c, 1) == 0, own[:, :wd], own[:, wd:])
        owned = [lax.all_gather(own, "prow")]

    turned = bf16(nz, wd, 2 * nc * slots)
    high, low = call(
        functools.partial(turn_kernel, direct, owners),
        [turned, turned],
        place,
        *owned,
        scratch_shapes=[pltpu.VMEM((2 * nz * wd, CAP), BF16)],
        flops=8 * nz * wd * nc * slots * CAP,
    )
    parts = [f32(wd, w)] * nz if direct else [f32(nz, wd, w)]
    got, _ = lax.optimization_barrier((got, high))
    mine, theirs = call(functools.partial(part_kernel, slots), [f32(nz * slots, w)] * 2, *got, flops=2 * term)
    other, _ = lax.optimization_barrier((other, mine))
    terms = call(correction_kernel, parts, high, low, whole, other, flops=term)
    theirs, _ = lax.optimization_barrier((theirs, terms[0]))
    sigma_sj = call(pick_kernel, f32(m, w), source, mine, swap(theirs, "pcol", nc), flops=term // 4)
    if direct:
        total = terms[0]
        for t in range(1, nz):
            total = total + lax.ppermute(terms[t], "pcol", [(k, (k + 2 * t) % nc) for k in range(nc)])
    else:
        terms = lax.all_to_all(terms[0], "pcol", split_axis=0, concat_axis=0, axis_index_groups=groups, tiled=True)
        total = jnp.sum(terms, axis=0)
    sigma_sj, d_term = lax.optimization_barrier((sigma_sj, d_term))
    return sigma_sj, d_term + total


def solution(mesh):
    placed = (P("pcol", "prow"), P(), P("pcol", "prow"), P("pcol", "prow"))
    return jax.shard_map(
        per_device,
        mesh=mesh,
        in_specs=placed,
        out_specs=(P("pcol", "prow"), P("pcol", "prow")),
        check_vma=False,
    )
```

```python
import functools

import jax
import jax.numpy as jnp
from jax import lax
from jax.experimental import pallas as pl
from jax.experimental.pallas import tpu as pltpu
from jax.sharding import PartitionSpec as P

LANES = 128
BLOCK_CAP = 560
CAP = -(-BLOCK_CAP // 64) * 64
FULL = CAP // LANES
WIDE = (FULL + 1) * LANES
BF16 = jnp.bfloat16
VMEM = pl.BlockSpec(memory_space=pltpu.VMEM)
HBM = pl.BlockSpec(memory_space=pltpu.HBM)


def f32(*shape):
    return jax.ShapeDtypeStruct(shape, jnp.float32)


def bf16(*shape):
    return jax.ShapeDtypeStruct(shape, BF16)


def split(v):
    high = v.astype(BF16)
    return high, (v - high.astype(jnp.float32)).astype(BF16)


def split3(v):
    high = v.astype(BF16)
    mid, low = split(v - high.astype(jnp.float32))
    return high, mid, low


def dot(a, b):
    return jnp.dot(a, b, preferred_element_type=jnp.float32)


def pick_rows(place, v):
    high, mid, low = split3(v)
    return dot(place, high) + (dot(place, mid) + dot(place, low))


def one_hot(mask):
    return jnp.where(mask, 1.0, 0.0)


def count(mask):
    return jnp.sum(jnp.where(mask, 1.0, 0.0)).astype(jnp.int32)


def log2(size):
    return size.bit_length() - 1


def each(refs, owners, fn):
    if owners is None:
        pl.loop(0, refs[0].shape[0])(lambda i: fn(i, refs[0].at[i]))
    else:
        for owner, ref in zip(owners, refs):
            fn(owner, ref)


def select_kernel(structure_ref, sigma_ref, out_ref, held_ref, sems):
    rows, cols = held_ref.shape
    n = structure_ref.shape[0]
    parts = sems.shape[0]
    part = rows // parts
    copies = []
    for k in range(parts):
        at = pl.ds(part * k, part)
        copies.append(pltpu.make_async_copy(sigma_ref.at[at, :], held_ref.at[at, :], sems.at[k]))
        copies[-1].start()
    first = lax.axis_index("prow") * cols
    listed = structure_ref[...].reshape(1, -1)
    names = jnp.broadcast_to(listed, (8, n))
    shift = lax.rem(n - count(listed < first), n)
    named = pltpu.roll(names, shift, 1)[:1, :CAP] - first
    named = jnp.concatenate([named, named[:, FULL * LANES :]], axis=1)
    step = 2 * LANES
    places = []
    for k in range(0, WIDE, step):
        at = lax.broadcasted_iota(jnp.int32, (cols - k, min(step, WIDE - k)), 0) + k
        places.append(one_hot(at == named[:, k : k + step]).astype(BF16))
    for k in range(parts):
        copies[k].wait()
        both = jnp.concatenate(split(held_ref[part * k : part * (k + 1), :]), axis=0)
        picked = [dot(both[:, step * i :], place) for i, place in enumerate(places)]
        picked = jnp.concatenate(picked, axis=1)
        picked = picked[:part] + picked[part:]
        for i in range(FULL):
            at = rows * i + part * k
            out_ref[at : at + part, :] = picked[:, LANES * i : LANES * (i + 1)]
        at = rows * FULL + part * (k % (parts // 2))
        if k < parts // 2:
            out_ref[at : at + part, : LANES // 2] = picked[:, FULL * LANES : CAP]
        else:
            out_ref[at : at + part, LANES // 2 :] = picked[:, CAP:]


def block_term(block_ref, uh, ul, rows):
    parts = [block_ref[rows * i : rows * (i + 1), :] for i in range(FULL)]
    tail = block_ref[rows * FULL : rows * FULL + rows // 2, :]
    parts.append(jnp.concatenate([tail, pltpu.roll(tail, LANES // 2, 1)], axis=0))
    halves = [split(p) for p in parts]
    highs, lows = [h for h, _ in halves], [l for _, l in halves]
    left = jnp.concatenate(highs + highs + lows, axis=1)
    return dot(left, jnp.concatenate([uh, ul, uh], axis=0))


def place_rows(us_ref, u, owner):
    m, w = u.shape
    nc = (us_ref.shape[1] - CAP - 8) // m
    if w % LANES:
        u = jnp.concatenate([u, jnp.zeros((m, LANES - w % LANES), jnp.float32)], axis=1)
    for i in range(us_ref.shape[0]):
        us_ref[i, pl.ds(owner, m, stride=nc), :] = u[:, LANES * i : LANES * (i + 1)]


def rows_of(us_ref, names, owner, width, lane_blocks):
    start = count(names < owner * width)
    base = pl.multiple_of((start // 8) * 8, 8)
    size = CAP + 8
    lanes = [pltpu.roll(us_ref[k, pl.ds(base, size), :], size - (start - base), 0)[:CAP] for k in lane_blocks]
    return jnp.concatenate(lanes, axis=1)


def cut(us_ref, names, owner, width, w):
    u = rows_of(us_ref, names, owner, width, range(us_ref.shape[0]))[:, :w]
    return split(jnp.concatenate([u, jnp.zeros((WIDE - CAP, w), jnp.float32)], axis=0))


def place_kernel(direct, nc, *refs):
    u_refs, us_ref = refs[:-1], refs[-1]
    end = us_ref.shape[1] - CAP - 8
    us_ref[:, end:, :] = jnp.zeros((us_ref.shape[0], CAP + 8, LANES), jnp.float32)
    if direct:
        for owner, u_ref in zip(ring_owners(nc, lax.axis_index("pcol")), u_refs):
            place_rows(us_ref, u_ref[...], owner)
    else:
        pl.loop(0, nc)(lambda k: place_rows(us_ref, u_refs[0][k], k))


def last_kernel(nc, width, structure_ref, before_ref, *refs):
    us_ref, own_ref = refs[-2:]
    c = lax.axis_index("pcol")
    us_ref[...] = before_ref[...]
    if len(refs) > 2:
        place_rows(us_ref, refs[0][...], ring_owners(nc, c)[-1])
    names = structure_ref[...].reshape(1, -1)
    w = own_ref.shape[1]
    own_ref[...] = rows_of(us_ref, names, c // 2, width, [c & 1] if len(refs) > 2 else [0])[:, :w]


def row_order(names, c, rows, nc, slots, direct):
    n = names.shape[1]
    z = c // 2
    lg = log2(nc)
    row = c * rows + lax.broadcasted_iota(jnp.int32, (rows, n), 0)
    rank = jnp.sum(one_hot(names < row), axis=1, keepdims=True).astype(jnp.int32)
    member = jnp.sum(one_hot(names == row), axis=1, keepdims=True)
    turn = rank & (nc - 1)
    ahead = (count(names < c * rows) - turn + nc - 1) >> lg
    block = turn >> 1
    if direct:
        block = (block - z) & (nc // 2 - 1)
    block = 2 * block + (turn & 1)
    slot = jnp.where(member > 0.5, block * slots + (rank >> lg) - ahead, -1)
    at = lax.broadcasted_iota(jnp.int32, (rows, nc * slots), 1)
    return one_hot(at == slot).T.astype(BF16)


def order_kernel(direct, slots, structure_ref, to_ref, place_ref, from_ref):
    nc = to_ref.shape[0] // slots
    rows = to_ref.shape[1]
    nz = nc // 2
    lg = log2(nc)
    names = structure_ref[...].reshape(1, -1)
    n = names.shape[1]
    m = n // nc
    c = lax.axis_index("pcol")
    z, x = c // 2, c & 1
    to_ref[...] = row_order(names, c, rows, nc, slots, direct)

    start, middle = count(names < 2 * z * rows), count(names < (2 * z + 1) * rows)
    named = pltpu.roll(jnp.broadcast_to(names, (8, n)), lax.rem(n - start, n), 1)[:1, :CAP]
    index = start + lax.broadcasted_iota(jnp.int32, (1, CAP), 1)
    half = jnp.where(named >= (2 * z + 1) * rows, 1, 0)
    turn = index & (nc - 1)
    ahead = (jnp.where(half == 1, middle, start) - turn + nc - 1) >> lg
    block = turn >> 1
    if direct:
        block = (block - z) & (nz - 1)
    slot = (2 * block + (turn & 1)) * slots + (index >> lg) - ahead + (half ^ x) * rows
    slot = jnp.where((named >= 2 * z * rows) & (named < (2 * z + 2) * rows), slot, -1)
    at = lax.broadcasted_iota(jnp.int32, (2 * rows, CAP), 0)
    place_ref[...] = one_hot(at == slot).T.astype(BF16)

    own = lax.broadcasted_iota(jnp.int32, (m, n), 1) - nc * lax.broadcasted_iota(jnp.int32, (m, n), 0)
    mine = jnp.sum(jnp.where(own == c, names, 0).astype(jnp.float32), axis=1, keepdims=True)
    source = jnp.zeros((m, 1), jnp.int32)
    before = jnp.zeros((m, 1), jnp.int32)
    for k in range(1, nc):
        less = mine < float(k * rows)
        source = source + jnp.where(less, 0, 1)
        before = jnp.where(less, before, count(less))
    block = source >> 1
    if direct:
        block = (z - block) & (nz - 1)
    block = block + nz * ((source ^ c) & 1)
    slot = block * slots + lax.broadcasted_iota(jnp.int32, (m, 1), 0) - before
    at = lax.broadcasted_iota(jnp.int32, (m, rows), 1)
    from_ref[...] = one_hot(at == slot).astype(BF16)


def near_kernel(owners, rest, structure_ref, us_ref, *refs):
    block_refs, (image_ref, uh_ref, ul_ref) = refs[:-3], refs[-3:]
    rows, w = image_ref.shape
    width = rows * 2
    names = structure_ref[...].reshape(1, -1)
    r = lax.axis_index("prow")
    image = jnp.zeros((rows, w), jnp.float32)
    for owner, block_ref in zip(owners(r), block_refs):
        image = image + block_term(block_ref, *cut(us_ref, names, owner, width, w), rows)
    image_ref[...] = image
    if rest is None:

        @pl.loop(0, uh_ref.shape[0])
        def _(k):
            uh_ref[k], ul_ref[k] = cut(us_ref, names, k, width, w)

    else:
        for k, owner in enumerate(rest(r)):
            uh_ref[k], ul_ref[k] = cut(us_ref, names, owner, width, w)


def far_terms(places, uh_ref, ul_ref, image, block_refs):
    rows = image.shape[0]
    for k, block_ref in zip(places, block_refs):
        image = image + block_term(block_ref, uh_ref[k], ul_ref[k], rows)
    return image


def far_kernel(uh_ref, ul_ref, part_ref, *refs):
    places = [0] + list(range(1, uh_ref.shape[0], 2))
    refs[-1][...] = far_terms(places, uh_ref, ul_ref, part_ref[...], refs[:-1])


def image_kernel(direct, uh_ref, ul_ref, part_ref, to_ref, *refs):
    n_in = (uh_ref.shape[0] - 1) // 2 if direct else 1
    block_refs, out_refs = refs[:n_in], refs[n_in:]
    n_out = len(out_refs)
    rows = part_ref.shape[0]
    image = part_ref[...]
    if direct:
        image = far_terms(range(2, uh_ref.shape[0], 2), uh_ref, ul_ref, image, block_refs)
    else:
        stack = block_refs[0]
        add = lambda b, v: v + block_term(stack.at[b], uh_ref[b], ul_ref[b], rows)
        image = lax.fori_loop(0, stack.shape[0], add, image)
    image = pick_rows(to_ref[...], image)
    out_refs[0][...] = image
    size = image.shape[0] // n_out
    for k in range(1, n_out):
        out_refs[k][...] = image[size * k : size * (k + 1)]


def turn_kernel(direct, owners, place_ref, *refs):
    high_ref, low_ref, held_ref = refs[-3:]
    nz, wd, size = high_ref.shape
    z = lax.axis_index("pcol") // 2

    def put(owner, u_ref):
        where = (owner ^ z) if direct else owner
        high, low = split(u_ref[...].T)
        held_ref[pl.ds(pl.multiple_of(where * wd, wd), wd), :] = high
        held_ref[pl.ds(pl.multiple_of((where + nz) * wd, wd), wd), :] = low

    each(refs[:-3], owners(lax.axis_index("prow")) if direct else None, put)
    turned = dot(held_ref[...], place_ref[...]).astype(BF16).reshape(2, nz, wd, size)
    high_ref[...] = turned[0]
    low_ref[...] = turned[1]


def correction_kernel(high_ref, low_ref, mine_ref, other_ref, *out_refs):
    sh, sl = split(jnp.concatenate([mine_ref[...], other_ref[...]], axis=0))

    def term(t):
        return dot(high_ref[t], sh) + (dot(high_ref[t], sl) + dot(low_ref[t], sh))

    if len(out_refs) > 1:
        terms = [term(t) for t in range(4)]
        half = terms[0].shape[1] // 2
        for k, out_ref in enumerate(out_refs):
            lanes = slice(0, half) if k < 2 else slice(half, None)
            picked = ((0, 1), (2, 3), (0, 2), (1, 3))[k]
            out_ref[...] = jnp.concatenate([terms[t][:, lanes] for t in picked], axis=0)
    else:

        @pl.loop(0, out_refs[0].shape[0])
        def _(t):
            out_refs[0][t] = term(t)


def add_kernel(kept_ref, got_ref, mine_ref, next_ref):
    n = mine_ref.shape[0]
    mine_ref[...] = kept_ref[:n, :] + got_ref[:n, :]
    next_ref[...] = kept_ref[n:, :] + got_ref[n:, :]


def sum_kernel(kept_ref, got_ref, out_ref):
    out_ref[...] = kept_ref[...] + got_ref[...]


def final_kernel(d_ref, left_ref, got_ref, right_ref, out_ref):
    half = left_ref.shape[1]
    out_ref[:, :half] = d_ref[:, :half] + (left_ref[...] + got_ref[...])
    out_ref[:, half:] = d_ref[:, half:] + right_ref[...]


def part_kernel(slots, *refs):
    mine_ref, theirs_ref = refs[-2:]
    first = (lax.axis_index("pcol") & 1) == 0
    blocks = mine_ref.shape[0] // slots
    mine, theirs = [], []
    for ref in refs[:-2]:
        for k in range(blocks // len(refs[:-2])):
            low = ref[2 * slots * k : 2 * slots * k + slots, :]
            high = ref[2 * slots * k + slots : 2 * slots * (k + 1), :]
            mine.append(jnp.where(first, low, high))
            theirs.append(jnp.where(first, high, low))
    mine_ref[...] = jnp.concatenate(mine, axis=0)
    theirs_ref[...] = jnp.concatenate(theirs, axis=0)


def pick_kernel(from_ref, mine_ref, other_ref, out_ref):
    out_ref[...] = -pick_rows(from_ref[...], jnp.concatenate([mine_ref[...], other_ref[...]], axis=0))


def call(kernel, out_shape, *args, flops=0, vmem=20, **kw):
    many = isinstance(out_shape, (list, tuple))
    size = flops and sum(v.size * v.dtype.itemsize for v in jax.tree.leaves((out_shape, args)))
    kw = {"in_specs": [VMEM] * len(args)} | kw
    return pl.pallas_call(
        kernel,
        out_shape=out_shape,
        out_specs=[VMEM] * len(out_shape) if many else VMEM,
        cost_estimate=pl.CostEstimate(flops=flops, bytes_accessed=size, transcendentals=0),
        compiler_params=pltpu.CompilerParams(vmem_limit_bytes=vmem * 2**20),
        **kw,
    )(*args)


def swap(v, axis, size):
    return lax.ppermute(v, axis, [(k, k ^ 1) for k in range(size)])


def spread(v, size, after):
    blocks = [v, swap(v, "prow", size)]
    v, _ = lax.optimization_barrier((v, after))
    for t in range(1, size // 2):
        for flip in range(2):
            blocks.append(lax.ppermute(v, "prow", [(k, ((k + 2 * t) % size) ^ flip) for k in range(size)]))
    return blocks


def relative_owners(size, r):
    out = []
    for t in range(size // 2):
        owner = (r - 2 * t) & (size - 1)
        out += [owner, owner ^ 1]
    return out


def ring_gather(u, nc, aside):
    ring = [2 * z for z in range(nc // 2)] + [2 * z + 1 for z in reversed(range(nc // 2))]
    pairs = [(ring[q - 1], ring[q]) for q in range(nc)]
    back = [(b, a) for a, b in pairs]
    blocks = [u]
    up = down = u
    for step in range(1, nc // 2):
        up, down = lax.ppermute(up, "pcol", pairs), lax.ppermute(down, "pcol", back)
        if step == 1:
            up, down = lax.optimization_barrier((up, down))
        blocks += [up, down]
    last, aside = lax.optimization_barrier((lax.ppermute(up, "pcol", pairs), aside))
    return blocks + [last], aside


def ring_owners(nc, c):
    q = jnp.where((c & 1) == 0, c >> 1, nc - 1 - (c >> 1))
    out = []
    for k in range(nc):
        step = (k + 1) // 2
        at = (q - step if k % 2 else q + step) & (nc - 1)
        out.append(jnp.where(at < nc // 2, 2 * at, 2 * (nc - 1 - at) + 1))
    return out


def per_device(sigma_top, structure, u_panel, d_term):
    nc, nr = lax.axis_size("pcol"), lax.axis_size("prow")
    c = lax.axis_index("pcol")
    nz = nc // 2
    rows, cols = sigma_top.shape
    m, w = u_panel.shape
    wd = w // 2
    n = structure.shape[0]
    slots = -(-rows // nc)
    direct = (nr, nc) == (4, 8)
    names = structure
    groups = [[2 * k + x for k in range(nz)] for x in range(2)]
    owners = functools.partial(relative_owners, nr)

    chosen = call(
        select_kernel,
        f32(rows * CAP // LANES, LANES),
        names,
        sigma_top,
        in_specs=[VMEM, HBM],
        scratch_shapes=[pltpu.VMEM((rows, cols), jnp.float32), pltpu.SemaphoreType.DMA((2,))],
        flops=4 * rows * cols * WIDE,
        vmem=52,
    )
    to, place, source = call(
        functools.partial(order_kernel, direct, slots),
        [bf16(nc * slots, rows), bf16(CAP, 2 * nc * slots), bf16(m, nc * slots)],
        names,
    )
    if direct:
        u_all, to = ring_gather(u_panel, nc, to)
    else:
        u_all = [lax.all_gather(u_panel, "pcol")]
    term = 6 * rows * WIDE * w
    placed = f32(-(-w // LANES), n + CAP + 8, LANES)
    early, late = (u_all[:-1], u_all[-1:]) if direct else (u_all, [])
    before = call(functools.partial(place_kernel, direct, nc), placed, *early, flops=8 * term)
    us, own = call(
        functools.partial(last_kernel, nc, cols),
        [placed, f32(CAP, wd if direct else w)],
        names,
        before,
        *late,
        flops=term,
    )
    halves = bf16(nr - 1 if direct else nr, WIDE, w)
    near = [chosen] if direct else []
    image, uh, ul = call(
        functools.partial(near_kernel, lambda r: owners(r)[:1], (lambda r: owners(r)[1:]) if direct else None),
        [f32(rows, w), halves, halves],
        names,
        us,
        *near,
        flops=0,
    )
    if direct:
        beside, later = [swap(chosen, "prow", nr)], []
        for t in range(1, nr // 2):
            far = lax.ppermute(chosen, "prow", [(k, (k + 2 * t) % nr) for k in range(nr)])
            far, _ = lax.optimization_barrier((far, image))
            beside.append(far)
            later.append(swap(far, "prow", nr))
        image = call(far_kernel, f32(rows, w), uh, ul, image, *beside, flops=1 * term)
    else:
        later = [lax.all_gather(chosen, "prow")]
    if direct:
        owned = spread(own, nr, beside[1])
    sent = call(
        functools.partial(image_kernel, direct),
        [f32(nc * slots, w)] + [f32(2 * slots, w)] * ((nz - 1) * direct),
        uh,
        ul,
        image,
        to,
        *later,
        flops=term,
    )
    whole = sent[0]
    other = swap(whole, "pcol", nc)
    if direct:
        got = [whole]
        for t in range(1, nz):
            got.append(lax.ppermute(sent[t], "pcol", [(k, (k + 2 * t) % nc) for k in range(nc)]))
    else:
        blocks = whole.reshape(nz, 2 * slots, w)
        blocks = lax.all_to_all(blocks, "pcol", split_axis=0, concat_axis=0, axis_index_groups=groups, tiled=True)
        got = [blocks.reshape(nc * slots, w)]
        own = jnp.where(jnp.bitwise_and(c, 1) == 0, own[:, :wd], own[:, wd:])
        owned = [lax.all_gather(own, "prow")]

    turned = bf16(nz, wd, 2 * nc * slots)
    high, low = call(
        functools.partial(turn_kernel, direct, owners),
        [turned, turned],
        place,
        *owned,
        scratch_shapes=[pltpu.VMEM((2 * nz * wd, CAP), BF16)],
        flops=8 * nz * wd * nc * slots * CAP,
    )
    parts = [f32(2 * wd, w // 2)] * 4 if direct else [f32(nz, wd, w)]
    got, _ = lax.optimization_barrier((got, high))
    mine, theirs = call(functools.partial(part_kernel, slots), [f32(nz * slots, w)] * 2, *got, flops=2 * term)
    other, _ = lax.optimization_barrier((other, mine))
    terms = call(correction_kernel, parts, high, low, whole, other, flops=term)
    theirs, _ = lax.optimization_barrier((theirs, terms[0]))
    sigma_sj = call(pick_kernel, f32(m, w), source, mine, swap(theirs, "pcol", nc), flops=term // 4)
    sigma_sj, d_term = lax.optimization_barrier((sigma_sj, d_term))
    if direct:
        meet = lambda v, by: lax.ppermute(v, "pcol", [(k, k ^ by) for k in range(nc)])
        pieces = [f32(wd, w // 2)] * 2
        from_far, from_near = meet(terms[1], 4), meet(terms[3], 2)
        right, right_next = call(add_kernel, pieces, terms[2], from_near)
        from_far, _ = lax.optimization_barrier((from_far, right))
        left, left_next = call(add_kernel, pieces, terms[0], from_far)
        right = call(sum_kernel, pieces[0], right, meet(right_next, 4), flops=4 * term)
        sigma_jj = call(final_kernel, f32(wd, w), d_term, left, meet(left_next, 2), right)
        return sigma_sj, sigma_jj
    terms = lax.all_to_all(terms[0], "pcol", split_axis=0, concat_axis=0, axis_index_groups=groups, tiled=True)
    return sigma_sj, d_term + jnp.sum(terms, axis=0)


def solution(mesh):
    placed = (P("pcol", "prow"), P(), P("pcol", "prow"), P("pcol", "prow"))
    return jax.shard_map(
        per_device,
        mesh=mesh,
        in_specs=placed,
        out_specs=(P("pcol", "prow"), P("pcol", "prow")),
        check_vma=False,
    )
```

```python
import functools

import jax
import jax.numpy as jnp
from jax import lax
from jax.experimental import pallas as pl
from jax.experimental.pallas import tpu as pltpu
from jax.sharding import PartitionSpec as P

LANES = 128
BLOCK_CAP = 560
CAP = -(-BLOCK_CAP // 64) * 64
FULL = CAP // LANES
WIDE = (FULL + 1) * LANES
BF16 = jnp.bfloat16
VMEM = pl.BlockSpec(memory_space=pltpu.VMEM)
HBM = pl.BlockSpec(memory_space=pltpu.HBM)


def f32(*shape):
    return jax.ShapeDtypeStruct(shape, jnp.float32)


def bf16(*shape):
    return jax.ShapeDtypeStruct(shape, BF16)


def split(v):
    high = v.astype(BF16)
    return high, (v - high.astype(jnp.float32)).astype(BF16)


def split3(v):
    high = v.astype(BF16)
    mid, low = split(v - high.astype(jnp.float32))
    return high, mid, low


def dot(a, b):
    return jnp.dot(a, b, preferred_element_type=jnp.float32)


def pick_rows(place, v):
    high, mid, low = split3(v)
    return dot(place, high) + (dot(place, mid) + dot(place, low))


def one_hot(mask):
    return jnp.where(mask, 1.0, 0.0)


def count(mask):
    return jnp.sum(jnp.where(mask, 1.0, 0.0)).astype(jnp.int32)


def log2(size):
    return size.bit_length() - 1


def each(refs, owners, fn):
    if owners is None:
        pl.loop(0, refs[0].shape[0])(lambda i: fn(i, refs[0].at[i]))
    else:
        for owner, ref in zip(owners, refs):
            fn(owner, ref)


def select_kernel(structure_ref, sigma_ref, out_ref, held_ref, sems):
    rows, cols = held_ref.shape
    n = structure_ref.shape[0]
    parts = sems.shape[0]
    part = rows // parts
    copies = []
    for k in range(parts):
        at = pl.ds(part * k, part)
        copies.append(pltpu.make_async_copy(sigma_ref.at[at, :], held_ref.at[at, :], sems.at[k]))
        copies[-1].start()
    first = lax.axis_index("prow") * cols
    listed = structure_ref[...].reshape(1, -1)
    names = jnp.broadcast_to(listed, (8, n))
    shift = lax.rem(n - count(listed < first), n)
    named = pltpu.roll(names, shift, 1)[:1, :CAP] - first
    named = jnp.concatenate([named, named[:, FULL * LANES :]], axis=1)
    step = 2 * LANES
    places = []
    for k in range(0, WIDE, step):
        at = lax.broadcasted_iota(jnp.int32, (cols - k, min(step, WIDE - k)), 0) + k
        places.append(one_hot(at == named[:, k : k + step]).astype(BF16))
    for k in range(parts):
        copies[k].wait()
        both = jnp.concatenate(split(held_ref[part * k : part * (k + 1), :]), axis=0)
        picked = [dot(both[:, step * i :], place) for i, place in enumerate(places)]
        picked = jnp.concatenate(picked, axis=1)
        picked = picked[:part] + picked[part:]
        for i in range(FULL):
            at = rows * i + part * k
            out_ref[at : at + part, :] = picked[:, LANES * i : LANES * (i + 1)]
        at = rows * FULL + part * (k % (parts // 2))
        if k < parts // 2:
            out_ref[at : at + part, : LANES // 2] = picked[:, FULL * LANES : CAP]
        else:
            out_ref[at : at + part, LANES // 2 :] = picked[:, CAP:]


def block_term(block_ref, uh, ul, rows):
    parts = [block_ref[rows * i : rows * (i + 1), :] for i in range(FULL)]
    tail = block_ref[rows * FULL : rows * FULL + rows // 2, :]
    parts.append(jnp.concatenate([tail, pltpu.roll(tail, LANES // 2, 1)], axis=0))
    halves = [split(p) for p in parts]
    highs, lows = [h for h, _ in halves], [l for _, l in halves]
    left = jnp.concatenate(highs + highs + lows, axis=1)
    return dot(left, jnp.concatenate([uh, ul, uh], axis=0))


def place_rows(us_ref, u, owner):
    m, w = u.shape
    nc = (us_ref.shape[1] - CAP - 8) // m
    if w % LANES:
        u = jnp.concatenate([u, jnp.zeros((m, LANES - w % LANES), jnp.float32)], axis=1)
    for i in range(us_ref.shape[0]):
        us_ref[i, pl.ds(owner, m, stride=nc), :] = u[:, LANES * i : LANES * (i + 1)]


def rows_of(us_ref, names, owner, width, lane_blocks):
    start = count(names < owner * width)
    base = pl.multiple_of((start // 8) * 8, 8)
    size = CAP + 8
    lanes = [pltpu.roll(us_ref[k, pl.ds(base, size), :], size - (start - base), 0)[:CAP] for k in lane_blocks]
    return jnp.concatenate(lanes, axis=1)


def cut(us_ref, names, owner, width, w):
    u = rows_of(us_ref, names, owner, width, range(us_ref.shape[0]))[:, :w]
    return split(jnp.concatenate([u, jnp.zeros((WIDE - CAP, w), jnp.float32)], axis=0))


def place_kernel(direct, nc, *refs):
    u_refs, us_ref = refs[:-1], refs[-1]
    end = us_ref.shape[1] - CAP - 8
    us_ref[:, end:, :] = jnp.zeros((us_ref.shape[0], CAP + 8, LANES), jnp.float32)
    if direct:
        for owner, u_ref in zip(ring_owners(nc, lax.axis_index("pcol")), u_refs):
            place_rows(us_ref, u_ref[...], owner)
    else:
        pl.loop(0, nc)(lambda k: place_rows(us_ref, u_refs[0][k], k))


def last_kernel(nc, width, structure_ref, before_ref, *refs):
    us_ref, own_ref = refs[-2:]
    c = lax.axis_index("pcol")
    us_ref[...] = before_ref[...]
    if len(refs) > 2:
        place_rows(us_ref, refs[0][...], ring_owners(nc, c)[-1])
    names = structure_ref[...].reshape(1, -1)
    w = own_ref.shape[1]
    own_ref[...] = rows_of(us_ref, names, c // 2, width, [c & 1] if len(refs) > 2 else [0])[:, :w]


def row_order(names, c, rows, nc, slots, direct):
    n = names.shape[1]
    z = c // 2
    lg = log2(nc)
    row = c * rows + lax.broadcasted_iota(jnp.int32, (rows, n), 0)
    rank = jnp.sum(one_hot(names < row), axis=1, keepdims=True).astype(jnp.int32)
    member = jnp.sum(one_hot(names == row), axis=1, keepdims=True)
    turn = rank & (nc - 1)
    ahead = (count(names < c * rows) - turn + nc - 1) >> lg
    block = turn >> 1
    if direct:
        block = block ^ z
    block = 2 * block + (turn & 1)
    slot = jnp.where(member > 0.5, block * slots + (rank >> lg) - ahead, -1)
    at = lax.broadcasted_iota(jnp.int32, (rows, nc * slots), 1)
    return one_hot(at == slot).T.astype(BF16)


def order_kernel(direct, slots, structure_ref, to_ref, place_ref, from_ref):
    nc = to_ref.shape[0] // slots
    rows = to_ref.shape[1]
    nz = nc // 2
    lg = log2(nc)
    names = structure_ref[...].reshape(1, -1)
    n = names.shape[1]
    m = n // nc
    c = lax.axis_index("pcol")
    z, x = c // 2, c & 1
    to_ref[...] = row_order(names, c, rows, nc, slots, direct)

    start, middle = count(names < 2 * z * rows), count(names < (2 * z + 1) * rows)
    named = pltpu.roll(jnp.broadcast_to(names, (8, n)), lax.rem(n - start, n), 1)[:1, :CAP]
    index = start + lax.broadcasted_iota(jnp.int32, (1, CAP), 1)
    half = jnp.where(named >= (2 * z + 1) * rows, 1, 0)
    turn = index & (nc - 1)
    ahead = (jnp.where(half == 1, middle, start) - turn + nc - 1) >> lg
    block = turn >> 1
    if direct:
        block = block ^ z
    slot = (2 * block + (turn & 1)) * slots + (index >> lg) - ahead + (half ^ x) * rows
    slot = jnp.where((named >= 2 * z * rows) & (named < (2 * z + 2) * rows), slot, -1)
    at = lax.broadcasted_iota(jnp.int32, (2 * rows, CAP), 0)
    place_ref[...] = one_hot(at == slot).T.astype(BF16)

    own = lax.broadcasted_iota(jnp.int32, (m, n), 1) - nc * lax.broadcasted_iota(jnp.int32, (m, n), 0)
    mine = jnp.sum(jnp.where(own == c, names, 0).astype(jnp.float32), axis=1, keepdims=True)
    source = jnp.zeros((m, 1), jnp.int32)
    before = jnp.zeros((m, 1), jnp.int32)
    for k in range(1, nc):
        less = mine < float(k * rows)
        source = source + jnp.where(less, 0, 1)
        before = jnp.where(less, before, count(less))
    block = source >> 1
    if direct:
        block = z ^ block
    block = block + nz * ((source ^ c) & 1)
    slot = block * slots + lax.broadcasted_iota(jnp.int32, (m, 1), 0) - before
    at = lax.broadcasted_iota(jnp.int32, (m, rows), 1)
    from_ref[...] = one_hot(at == slot).astype(BF16)


def near_kernel(owners, rest, structure_ref, us_ref, *refs):
    block_refs, (image_ref, uh_ref, ul_ref) = refs[:-3], refs[-3:]
    rows, w = image_ref.shape
    width = rows * 2
    names = structure_ref[...].reshape(1, -1)
    r = lax.axis_index("prow")
    image = jnp.zeros((rows, w), jnp.float32)
    for owner, block_ref in zip(owners(r), block_refs):
        image = image + block_term(block_ref, *cut(us_ref, names, owner, width, w), rows)
    image_ref[...] = image
    if rest is None:

        @pl.loop(0, uh_ref.shape[0])
        def _(k):
            uh_ref[k], ul_ref[k] = cut(us_ref, names, k, width, w)

    else:
        for k, owner in enumerate(rest(r)):
            uh_ref[k], ul_ref[k] = cut(us_ref, names, owner, width, w)


def far_terms(places, uh_ref, ul_ref, image, block_refs):
    rows = image.shape[0]
    for k, block_ref in zip(places, block_refs):
        image = image + block_term(block_ref, uh_ref[k], ul_ref[k], rows)
    return image


def far_kernel(uh_ref, ul_ref, part_ref, *refs):
    places = [0] + list(range(1, uh_ref.shape[0], 2))
    refs[-1][...] = far_terms(places, uh_ref, ul_ref, part_ref[...], refs[:-1])


def image_kernel(direct, uh_ref, ul_ref, part_ref, to_ref, *refs):
    n_in = (uh_ref.shape[0] - 1) // 2 if direct else 1
    block_refs, out_refs = refs[:n_in], refs[n_in:]
    n_out = len(out_refs)
    rows = part_ref.shape[0]
    image = part_ref[...]
    if direct:
        image = far_terms(range(2, uh_ref.shape[0], 2), uh_ref, ul_ref, image, block_refs)
    else:
        stack = block_refs[0]
        add = lambda b, v: v + block_term(stack.at[b], uh_ref[b], ul_ref[b], rows)
        image = lax.fori_loop(0, stack.shape[0], add, image)
    image = pick_rows(to_ref[...], image)
    out_refs[0][...] = image
    size = image.shape[0] // n_out
    for k in range(1, n_out):
        out_refs[k][...] = image[size * k : size * (k + 1)]


def turn_kernel(direct, owners, place_ref, *refs):
    high_ref, low_ref, held_ref = refs[-3:]
    nz, wd, size = high_ref.shape
    z = lax.axis_index("pcol") // 2

    def put(owner, u_ref):
        where = (owner ^ z) if direct else owner
        high, low = split(u_ref[...].T)
        held_ref[pl.ds(pl.multiple_of(where * wd, wd), wd), :] = high
        held_ref[pl.ds(pl.multiple_of((where + nz) * wd, wd), wd), :] = low

    each(refs[:-3], owners(lax.axis_index("prow")) if direct else None, put)
    turned = dot(held_ref[...], place_ref[...]).astype(BF16).reshape(2, nz, wd, size)
    high_ref[...] = turned[0]
    low_ref[...] = turned[1]


def correction_kernel(high_ref, low_ref, mine_ref, other_ref, *out_refs):
    sh, sl = split(jnp.concatenate([mine_ref[...], other_ref[...]], axis=0))

    def term(t):
        return dot(high_ref[t], sh) + (dot(high_ref[t], sl) + dot(low_ref[t], sh))

    if len(out_refs) > 1:
        for t, out_ref in enumerate(out_refs):
            out_ref[...] = term(t)
    else:

        @pl.loop(0, out_refs[0].shape[0])
        def _(t):
            out_refs[0][t] = term(t)


def sum_kernel(*refs):
    total = refs[0][...]
    for ref in refs[1:-1]:
        total = total + ref[...]
    refs[-1][...] = total


def part_kernel(slots, *refs):
    mine_ref, theirs_ref = refs[-2:]
    first = (lax.axis_index("pcol") & 1) == 0
    blocks = mine_ref.shape[0] // slots
    mine, theirs = [], []
    for ref in refs[:-2]:
        for k in range(blocks // len(refs[:-2])):
            low = ref[2 * slots * k : 2 * slots * k + slots, :]
            high = ref[2 * slots * k + slots : 2 * slots * (k + 1), :]
            mine.append(jnp.where(first, low, high))
            theirs.append(jnp.where(first, high, low))
    mine_ref[...] = jnp.concatenate(mine, axis=0)
    theirs_ref[...] = jnp.concatenate(theirs, axis=0)


def pick_kernel(from_ref, mine_ref, other_ref, out_ref):
    out_ref[...] = -pick_rows(from_ref[...], jnp.concatenate([mine_ref[...], other_ref[...]], axis=0))


def call(kernel, out_shape, *args, flops=0, vmem=20, **kw):
    many = isinstance(out_shape, (list, tuple))
    size = flops and sum(v.size * v.dtype.itemsize for v in jax.tree.leaves((out_shape, args)))
    kw = {"in_specs": [VMEM] * len(args)} | kw
    return pl.pallas_call(
        kernel,
        out_shape=out_shape,
        out_specs=[VMEM] * len(out_shape) if many else VMEM,
        cost_estimate=pl.CostEstimate(flops=flops, bytes_accessed=size, transcendentals=0),
        compiler_params=pltpu.CompilerParams(vmem_limit_bytes=vmem * 2**20),
        **kw,
    )(*args)


def swap(v, axis, size):
    return lax.ppermute(v, axis, [(k, k ^ 1) for k in range(size)])


def spread(v, size, after):
    blocks = [v, swap(v, "prow", size)]
    v, _ = lax.optimization_barrier((v, after))
    for t in range(1, size // 2):
        for flip in range(2):
            blocks.append(lax.ppermute(v, "prow", [(k, ((k + 2 * t) % size) ^ flip) for k in range(size)]))
    return blocks


def relative_owners(size, r):
    out = []
    for t in range(size // 2):
        owner = (r - 2 * t) & (size - 1)
        out += [owner, owner ^ 1]
    return out


def ring_gather(u, nc, aside):
    ring = [2 * z for z in range(nc // 2)] + [2 * z + 1 for z in reversed(range(nc // 2))]
    pairs = [(ring[q - 1], ring[q]) for q in range(nc)]
    back = [(b, a) for a, b in pairs]
    blocks = [u]
    up = down = u
    for step in range(1, nc // 2):
        up, down = lax.ppermute(up, "pcol", pairs), lax.ppermute(down, "pcol", back)
        if step == 1:
            up, down = lax.optimization_barrier((up, down))
        blocks += [up, down]
    last, aside = lax.optimization_barrier((lax.ppermute(up, "pcol", pairs), aside))
    return blocks + [last], aside


def ring_owners(nc, c):
    q = jnp.where((c & 1) == 0, c >> 1, nc - 1 - (c >> 1))
    out = []
    for k in range(nc):
        step = (k + 1) // 2
        at = (q - step if k % 2 else q + step) & (nc - 1)
        out.append(jnp.where(at < nc // 2, 2 * at, 2 * (nc - 1 - at) + 1))
    return out


def per_device(sigma_top, structure, u_panel, d_term):
    nc, nr = lax.axis_size("pcol"), lax.axis_size("prow")
    c = lax.axis_index("pcol")
    nz = nc // 2
    rows, cols = sigma_top.shape
    m, w = u_panel.shape
    wd = w // 2
    n = structure.shape[0]
    slots = -(-rows // nc)
    direct = (nr, nc) == (4, 8)
    names = structure
    groups = [[2 * k + x for k in range(nz)] for x in range(2)]
    owners = functools.partial(relative_owners, nr)

    chosen = call(
        select_kernel,
        f32(rows * CAP // LANES, LANES),
        names,
        sigma_top,
        in_specs=[VMEM, HBM],
        scratch_shapes=[pltpu.VMEM((rows, cols), jnp.float32), pltpu.SemaphoreType.DMA((2,))],
        flops=4 * rows * cols * WIDE,
        vmem=52,
    )
    to, place, source = call(
        functools.partial(order_kernel, direct, slots),
        [bf16(nc * slots, rows), bf16(CAP, 2 * nc * slots), bf16(m, nc * slots)],
        names,
    )
    if direct:
        u_all, to = ring_gather(u_panel, nc, to)
    else:
        u_all = [lax.all_gather(u_panel, "pcol")]
    term = 6 * rows * WIDE * w
    placed = f32(-(-w // LANES), n + CAP + 8, LANES)
    early, late = (u_all[:-1], u_all[-1:]) if direct else (u_all, [])
    before = call(functools.partial(place_kernel, direct, nc), placed, *early, flops=8 * term)
    us, own = call(
        functools.partial(last_kernel, nc, cols),
        [placed, f32(CAP, wd if direct else w)],
        names,
        before,
        *late,
        flops=term,
    )
    halves = bf16(nr - 1 if direct else nr, WIDE, w)
    near = [chosen] if direct else []
    image, uh, ul = call(
        functools.partial(near_kernel, lambda r: owners(r)[:1], (lambda r: owners(r)[1:]) if direct else None),
        [f32(rows, w), halves, halves],
        names,
        us,
        *near,
        flops=0,
    )
    if direct:
        beside, later = [swap(chosen, "prow", nr)], []
        for t in range(1, nr // 2):
            far = lax.ppermute(chosen, "prow", [(k, (k + 2 * t) % nr) for k in range(nr)])
            far, _ = lax.optimization_barrier((far, image))
            beside.append(far)
            later.append(swap(far, "prow", nr))
        image = call(far_kernel, f32(rows, w), uh, ul, image, *beside, flops=1 * term)
    else:
        later = [lax.all_gather(chosen, "prow")]
    if direct:
        owned = spread(own, nr, beside[1])
    sent = call(
        functools.partial(image_kernel, direct),
        [f32(nc * slots, w)] + [f32(2 * slots, w)] * ((nz - 1) * direct),
        uh,
        ul,
        image,
        to,
        *later,
        flops=term,
    )
    meet = lambda v, t: lax.ppermute(v, "pcol", [(k, k ^ (2 * t)) for k in range(nc)])
    whole = sent[0]
    other = swap(whole, "pcol", nc)
    if direct:
        got = [whole]
        for t in range(1, nz):
            got.append(meet(sent[t], t))
    else:
        blocks = whole.reshape(nz, 2 * slots, w)
        blocks = lax.all_to_all(blocks, "pcol", split_axis=0, concat_axis=0, axis_index_groups=groups, tiled=True)
        got = [blocks.reshape(nc * slots, w)]
        own = jnp.where(jnp.bitwise_and(c, 1) == 0, own[:, :wd], own[:, wd:])
        owned = [lax.all_gather(own, "prow")]

    turned = bf16(nz, wd, 2 * nc * slots)
    high, low = call(
        functools.partial(turn_kernel, direct, owners),
        [turned, turned],
        place,
        *owned,
        scratch_shapes=[pltpu.VMEM((2 * nz * wd, CAP), BF16)],
        flops=8 * nz * wd * nc * slots * CAP,
    )
    parts = [f32(wd, w)] * nz if direct else [f32(nz, wd, w)]
    got, _ = lax.optimization_barrier((got, high))
    mine, theirs = call(functools.partial(part_kernel, slots), [f32(nz * slots, w)] * 2, *got, flops=2 * term)
    other, _ = lax.optimization_barrier((other, mine))
    terms = call(correction_kernel, parts, high, low, whole, other, flops=term)
    theirs, _ = lax.optimization_barrier((theirs, terms[0]))
    sigma_sj = call(pick_kernel, f32(m, w), source, mine, swap(theirs, "pcol", nc), flops=term // 4)
    sigma_sj, d_term = lax.optimization_barrier((sigma_sj, d_term))
    if direct:
        total = call(sum_kernel, f32(wd, w), terms[0], *[meet(terms[t], t) for t in range(2, nz)], flops=4 * term)
        return sigma_sj, d_term + (total + meet(terms[1], 1))
    terms = lax.all_to_all(terms[0], "pcol", split_axis=0, concat_axis=0, axis_index_groups=groups, tiled=True)
    return sigma_sj, d_term + jnp.sum(terms, axis=0)


def solution(mesh):
    placed = (P("pcol", "prow"), P(), P("pcol", "prow"), P("pcol", "prow"))
    return jax.shard_map(
        per_device,
        mesh=mesh,
        in_specs=placed,
        out_specs=(P("pcol", "prow"), P("pcol", "prow")),
        check_vma=False,
    )
```

```python
import functools

import jax
import jax.numpy as jnp
from jax import lax
from jax.experimental import pallas as pl
from jax.experimental.pallas import tpu as pltpu
from jax.sharding import PartitionSpec as P

LANES = 128
BLOCK_CAP = 560
CAP = -(-BLOCK_CAP // 64) * 64
FULL = CAP // LANES
WIDE = (FULL + 1) * LANES
BF16 = jnp.bfloat16
VMEM = pl.BlockSpec(memory_space=pltpu.VMEM)
HBM = pl.BlockSpec(memory_space=pltpu.HBM)


def f32(*shape):
    return jax.ShapeDtypeStruct(shape, jnp.float32)


def bf16(*shape):
    return jax.ShapeDtypeStruct(shape, BF16)


def split(v):
    high = v.astype(BF16)
    return high, (v - high.astype(jnp.float32)).astype(BF16)


def split3(v):
    high = v.astype(BF16)
    mid, low = split(v - high.astype(jnp.float32))
    return high, mid, low


def dot(a, b):
    return jnp.dot(a, b, preferred_element_type=jnp.float32)


def pick_rows(place, v):
    high, mid, low = split3(v)
    return dot(place, high) + (dot(place, mid) + dot(place, low))


def one_hot(mask):
    return jnp.where(mask, 1.0, 0.0)


def count(mask):
    return jnp.sum(jnp.where(mask, 1.0, 0.0)).astype(jnp.int32)


def log2(size):
    return size.bit_length() - 1


def each(refs, owners, fn):
    if owners is None:
        pl.loop(0, refs[0].shape[0])(lambda i: fn(i, refs[0].at[i]))
    else:
        for owner, ref in zip(owners, refs):
            fn(owner, ref)


def select_kernel(structure_ref, sigma_ref, out_ref, held_ref, sems):
    rows, cols = held_ref.shape
    n = structure_ref.shape[0]
    parts = sems.shape[0]
    part = rows // parts
    copies = []
    for k in range(parts):
        at = pl.ds(part * k, part)
        copies.append(pltpu.make_async_copy(sigma_ref.at[at, :], held_ref.at[at, :], sems.at[k]))
        copies[-1].start()
    first = lax.axis_index("prow") * cols
    listed = structure_ref[...].reshape(1, -1)
    names = jnp.broadcast_to(listed, (8, n))
    shift = lax.rem(n - count(listed < first), n)
    named = pltpu.roll(names, shift, 1)[:1, :CAP] - first
    named = jnp.concatenate([named, named[:, FULL * LANES :]], axis=1)
    step = 2 * LANES
    places = []
    for k in range(0, WIDE, step):
        at = lax.broadcasted_iota(jnp.int32, (cols - k, min(step, WIDE - k)), 0) + k
        places.append(one_hot(at == named[:, k : k + step]).astype(BF16))
    for k in range(parts):
        copies[k].wait()
        both = jnp.concatenate(split(held_ref[part * k : part * (k + 1), :]), axis=0)
        picked = [dot(both[:, step * i :], place) for i, place in enumerate(places)]
        picked = jnp.concatenate(picked, axis=1)
        picked = picked[:part] + picked[part:]
        for i in range(FULL):
            at = rows * i + part * k
            out_ref[at : at + part, :] = picked[:, LANES * i : LANES * (i + 1)]
        at = rows * FULL + part * (k % (parts // 2))
        if k < parts // 2:
            out_ref[at : at + part, : LANES // 2] = picked[:, FULL * LANES : CAP]
        else:
            out_ref[at : at + part, LANES // 2 :] = picked[:, CAP:]


def block_term(block_ref, uh, ul, rows):
    parts = [block_ref[rows * i : rows * (i + 1), :] for i in range(FULL)]
    tail = block_ref[rows * FULL : rows * FULL + rows // 2, :]
    parts.append(jnp.concatenate([tail, pltpu.roll(tail, LANES // 2, 1)], axis=0))
    halves = [split(p) for p in parts]
    highs, lows = [h for h, _ in halves], [l for _, l in halves]
    left = jnp.concatenate(highs + highs + lows, axis=1)
    return dot(left, jnp.concatenate([uh, ul, uh], axis=0))


def place_rows(us_ref, u, owner):
    m, w = u.shape
    nc = (us_ref.shape[1] - CAP - 8) // m
    if w % LANES:
        u = jnp.concatenate([u, jnp.zeros((m, LANES - w % LANES), jnp.float32)], axis=1)
    for i in range(us_ref.shape[0]):
        us_ref[i, pl.ds(owner, m, stride=nc), :] = u[:, LANES * i : LANES * (i + 1)]


def rows_of(us_ref, names, owner, width, lane_blocks):
    start = count(names < owner * width)
    base = pl.multiple_of((start // 8) * 8, 8)
    size = CAP + 8
    lanes = [pltpu.roll(us_ref[k, pl.ds(base, size), :], size - (start - base), 0)[:CAP] for k in lane_blocks]
    return jnp.concatenate(lanes, axis=1)


def cut(us_ref, names, owner, width, w):
    u = rows_of(us_ref, names, owner, width, range(us_ref.shape[0]))[:, :w]
    return split(jnp.concatenate([u, jnp.zeros((WIDE - CAP, w), jnp.float32)], axis=0))


def place_kernel(direct, nc, *refs):
    u_refs, us_ref = refs[:-1], refs[-1]
    end = us_ref.shape[1] - CAP - 8
    us_ref[:, end:, :] = jnp.zeros((us_ref.shape[0], CAP + 8, LANES), jnp.float32)
    if direct:
        for owner, u_ref in zip(ring_owners(nc, lax.axis_index("pcol")), u_refs):
            place_rows(us_ref, u_ref[...], owner)
    else:
        pl.loop(0, nc)(lambda k: place_rows(us_ref, u_refs[0][k], k))


def last_kernel(nc, width, structure_ref, before_ref, *refs):
    us_ref, own_ref = refs[-2:]
    c = lax.axis_index("pcol")
    us_ref[...] = before_ref[...]
    if len(refs) > 2:
        place_rows(us_ref, refs[0][...], ring_owners(nc, c)[-1])
    names = structure_ref[...].reshape(1, -1)
    w = own_ref.shape[1]
    own_ref[...] = rows_of(us_ref, names, c // 2, width, [c & 1] if len(refs) > 2 else [0])[:, :w]


AWAY = (0, 2, 3, 1)


def place_of(t):
    return jnp.where(t == 1, 3, jnp.where(t > 1, t - 1, 0))


def row_order(names, c, rows, nc, slots, direct):
    n = names.shape[1]
    z = c // 2
    lg = log2(nc)
    row = c * rows + lax.broadcasted_iota(jnp.int32, (rows, n), 0)
    rank = jnp.sum(one_hot(names < row), axis=1, keepdims=True).astype(jnp.int32)
    member = jnp.sum(one_hot(names == row), axis=1, keepdims=True)
    turn = rank & (nc - 1)
    ahead = (count(names < c * rows) - turn + nc - 1) >> lg
    block = turn >> 1
    if direct:
        block = place_of(block ^ z)
    block = 2 * block + (turn & 1)
    slot = jnp.where(member > 0.5, block * slots + (rank >> lg) - ahead, -1)
    at = lax.broadcasted_iota(jnp.int32, (rows, nc * slots), 1)
    return one_hot(at == slot).T.astype(BF16)


def order_kernel(direct, slots, structure_ref, to_ref, place_ref, from_ref):
    nc = to_ref.shape[0] // slots
    rows = to_ref.shape[1]
    nz = nc // 2
    lg = log2(nc)
    names = structure_ref[...].reshape(1, -1)
    n = names.shape[1]
    m = n // nc
    c = lax.axis_index("pcol")
    z, x = c // 2, c & 1
    to_ref[...] = row_order(names, c, rows, nc, slots, direct)

    start, middle = count(names < 2 * z * rows), count(names < (2 * z + 1) * rows)
    named = pltpu.roll(jnp.broadcast_to(names, (8, n)), lax.rem(n - start, n), 1)[:1, :CAP]
    index = start + lax.broadcasted_iota(jnp.int32, (1, CAP), 1)
    half = jnp.where(named >= (2 * z + 1) * rows, 1, 0)
    turn = index & (nc - 1)
    ahead = (jnp.where(half == 1, middle, start) - turn + nc - 1) >> lg
    block = turn >> 1
    if direct:
        block = place_of(block ^ z)
    slot = (2 * block + (turn & 1)) * slots + (index >> lg) - ahead + (half ^ x) * rows
    slot = jnp.where((named >= 2 * z * rows) & (named < (2 * z + 2) * rows), slot, -1)
    at = lax.broadcasted_iota(jnp.int32, (2 * rows, CAP), 0)
    place_ref[...] = one_hot(at == slot).T.astype(BF16)

    own = lax.broadcasted_iota(jnp.int32, (m, n), 1) - nc * lax.broadcasted_iota(jnp.int32, (m, n), 0)
    mine = jnp.sum(jnp.where(own == c, names, 0).astype(jnp.float32), axis=1, keepdims=True)
    source = jnp.zeros((m, 1), jnp.int32)
    before = jnp.zeros((m, 1), jnp.int32)
    for k in range(1, nc):
        less = mine < float(k * rows)
        source = source + jnp.where(less, 0, 1)
        before = jnp.where(less, before, count(less))
    block = source >> 1
    if direct:
        block = place_of(block ^ z)
    block = block + nz * ((source ^ c) & 1)
    slot = block * slots + lax.broadcasted_iota(jnp.int32, (m, 1), 0) - before
    at = lax.broadcasted_iota(jnp.int32, (m, rows), 1)
    from_ref[...] = one_hot(at == slot).astype(BF16)


def near_kernel(owners, rest, structure_ref, us_ref, *refs):
    block_refs, (image_ref, uh_ref, ul_ref) = refs[:-3], refs[-3:]
    rows, w = image_ref.shape
    width = rows * 2
    names = structure_ref[...].reshape(1, -1)
    r = lax.axis_index("prow")
    image = jnp.zeros((rows, w), jnp.float32)
    for owner, block_ref in zip(owners(r), block_refs):
        image = image + block_term(block_ref, *cut(us_ref, names, owner, width, w), rows)
    image_ref[...] = image
    if rest is None:

        @pl.loop(0, uh_ref.shape[0])
        def _(k):
            uh_ref[k], ul_ref[k] = cut(us_ref, names, k, width, w)

    else:
        for k, owner in enumerate(rest(r)):
            uh_ref[k], ul_ref[k] = cut(us_ref, names, owner, width, w)


def far_terms(places, uh_ref, ul_ref, image, block_refs):
    rows = image.shape[0]
    for k, block_ref in zip(places, block_refs):
        image = image + block_term(block_ref, uh_ref[k], ul_ref[k], rows)
    return image


def far_kernel(uh_ref, ul_ref, part_ref, *refs):
    places = [0] + list(range(1, uh_ref.shape[0], 2))
    refs[-1][...] = far_terms(places, uh_ref, ul_ref, part_ref[...], refs[:-1])


def image_kernel(direct, uh_ref, ul_ref, part_ref, to_ref, *refs):
    n_in = (uh_ref.shape[0] - 1) // 2 if direct else 1
    block_refs, out_refs = refs[:n_in], refs[n_in:]
    n_out = len(out_refs)
    rows = part_ref.shape[0]
    image = part_ref[...]
    if direct:
        image = far_terms(range(2, uh_ref.shape[0], 2), uh_ref, ul_ref, image, block_refs)
    else:
        stack = block_refs[0]
        add = lambda b, v: v + block_term(stack.at[b], uh_ref[b], ul_ref[b], rows)
        image = lax.fori_loop(0, stack.shape[0], add, image)
    high, low = split(image)
    image = dot(to_ref[...], high) + dot(to_ref[...], low)
    out_refs[0][...] = image
    size = image.shape[0] // n_out
    for k in range(1, n_out):
        out_refs[k][...] = image[size * k : size * (k + 1)]


def turn_kernel(direct, owners, place_ref, *refs):
    high_ref, low_ref, held_ref = refs[-3:]
    nz, wd, size = high_ref.shape
    z = lax.axis_index("pcol") // 2

    def put(owner, u_ref):
        where = (owner ^ z) if direct else owner
        high, low = split(u_ref[...].T)
        held_ref[pl.ds(pl.multiple_of(where * wd, wd), wd), :] = high
        held_ref[pl.ds(pl.multiple_of((where + nz) * wd, wd), wd), :] = low

    each(refs[:-3], owners(lax.axis_index("prow")) if direct else None, put)
    turned = dot(held_ref[...], place_ref[...]).astype(BF16).reshape(2, nz, wd, size)
    high_ref[...] = turned[0]
    low_ref[...] = turned[1]


def correction_kernel(high_ref, low_ref, mine_ref, other_ref, *out_refs):
    sh, sl = split(jnp.concatenate([mine_ref[...], other_ref[...]], axis=0))

    def term(t):
        return dot(high_ref[t], sh) + (dot(high_ref[t], sl) + dot(low_ref[t], sh))

    if len(out_refs) > 1:
        for t, out_ref in enumerate(out_refs):
            out_ref[...] = term(t)
    else:

        @pl.loop(0, out_refs[0].shape[0])
        def _(t):
            out_refs[0][t] = term(t)


def sum_kernel(*refs):
    total = refs[0][...]
    for ref in refs[1:-1]:
        total = total + ref[...]
    refs[-1][...] = total


def part_kernel(slots, *refs):
    mine_ref, theirs_ref = refs[-2:]
    first = (lax.axis_index("pcol") & 1) == 0
    blocks = mine_ref.shape[0] // slots
    mine, theirs = [], []
    for ref in refs[:-2]:
        for k in range(blocks // len(refs[:-2])):
            low = ref[2 * slots * k : 2 * slots * k + slots, :]
            high = ref[2 * slots * k + slots : 2 * slots * (k + 1), :]
            mine.append(jnp.where(first, low, high))
            theirs.append(jnp.where(first, high, low))
    mine_ref[...] = jnp.concatenate(mine, axis=0)
    theirs_ref[...] = jnp.concatenate(theirs, axis=0)


def pick_kernel(from_ref, mine_ref, other_ref, out_ref):
    out_ref[...] = -pick_rows(from_ref[...], jnp.concatenate([mine_ref[...], other_ref[...]], axis=0))


def call(kernel, out_shape, *args, flops=0, vmem=20, **kw):
    many = isinstance(out_shape, (list, tuple))
    size = flops and sum(v.size * v.dtype.itemsize for v in jax.tree.leaves((out_shape, args)))
    kw = {"in_specs": [VMEM] * len(args)} | kw
    return pl.pallas_call(
        kernel,
        out_shape=out_shape,
        out_specs=[VMEM] * len(out_shape) if many else VMEM,
        cost_estimate=pl.CostEstimate(flops=flops, bytes_accessed=size, transcendentals=0),
        compiler_params=pltpu.CompilerParams(vmem_limit_bytes=vmem * 2**20),
        **kw,
    )(*args)


def swap(v, axis, size):
    return lax.ppermute(v, axis, [(k, k ^ 1) for k in range(size)])


def spread(v, size, after):
    blocks = [v, swap(v, "prow", size)]
    v, _ = lax.optimization_barrier((v, after))
    for t in range(1, size // 2):
        for flip in range(2):
            blocks.append(lax.ppermute(v, "prow", [(k, ((k + 2 * t) % size) ^ flip) for k in range(size)]))
    return blocks


def relative_owners(size, r):
    out = []
    for t in range(size // 2):
        owner = (r - 2 * t) & (size - 1)
        out += [owner, owner ^ 1]
    return out


def ring_gather(u, nc, aside):
    ring = [2 * z for z in range(nc // 2)] + [2 * z + 1 for z in reversed(range(nc // 2))]
    pairs = [(ring[q - 1], ring[q]) for q in range(nc)]
    back = [(b, a) for a, b in pairs]
    blocks = [u]
    up = down = u
    for step in range(1, nc // 2):
        up, down = lax.ppermute(up, "pcol", pairs), lax.ppermute(down, "pcol", back)
        if step == 1:
            up, down = lax.optimization_barrier((up, down))
        blocks += [up, down]
    last, aside = lax.optimization_barrier((lax.ppermute(up, "pcol", pairs), aside))
    return blocks + [last], aside


def ring_owners(nc, c):
    q = jnp.where((c & 1) == 0, c >> 1, nc - 1 - (c >> 1))
    out = []
    for k in range(nc):
        step = (k + 1) // 2
        at = (q - step if k % 2 else q + step) & (nc - 1)
        out.append(jnp.where(at < nc // 2, 2 * at, 2 * (nc - 1 - at) + 1))
    return out


def per_device(sigma_top, structure, u_panel, d_term):
    nc, nr = lax.axis_size("pcol"), lax.axis_size("prow")
    c = lax.axis_index("pcol")
    nz = nc // 2
    rows, cols = sigma_top.shape
    m, w = u_panel.shape
    wd = w // 2
    n = structure.shape[0]
    slots = -(-rows // nc)
    direct = (nr, nc) == (4, 8)
    names = structure
    groups = [[2 * k + x for k in range(nz)] for x in range(2)]
    owners = functools.partial(relative_owners, nr)

    chosen = call(
        select_kernel,
        f32(rows * CAP // LANES, LANES),
        names,
        sigma_top,
        in_specs=[VMEM, HBM],
        scratch_shapes=[pltpu.VMEM((rows, cols), jnp.float32), pltpu.SemaphoreType.DMA((2,))],
        flops=4 * rows * cols * WIDE,
        vmem=52,
    )
    to, place, source = call(
        functools.partial(order_kernel, direct, slots),
        [bf16(nc * slots, rows), bf16(CAP, 2 * nc * slots), bf16(m, nc * slots)],
        names,
    )
    if direct:
        u_all, to = ring_gather(u_panel, nc, to)
    else:
        u_all = [lax.all_gather(u_panel, "pcol")]
    term = 6 * rows * WIDE * w
    placed = f32(-(-w // LANES), n + CAP + 8, LANES)
    early, late = (u_all[:-1], u_all[-1:]) if direct else (u_all, [])
    before = call(functools.partial(place_kernel, direct, nc), placed, *early, flops=8 * term)
    us, own = call(
        functools.partial(last_kernel, nc, cols),
        [placed, f32(CAP, wd if direct else w)],
        names,
        before,
        *late,
        flops=term,
    )
    halves = bf16(nr - 1 if direct else nr, WIDE, w)
    near = [chosen] if direct else []
    image, uh, ul = call(
        functools.partial(near_kernel, lambda r: owners(r)[:1], (lambda r: owners(r)[1:]) if direct else None),
        [f32(rows, w), halves, halves],
        names,
        us,
        *near,
        flops=0,
    )
    if direct:
        beside, later = [swap(chosen, "prow", nr)], []
        for t in range(1, nr // 2):
            far = lax.ppermute(chosen, "prow", [(k, (k + 2 * t) % nr) for k in range(nr)])
            far, _ = lax.optimization_barrier((far, image))
            beside.append(far)
            later.append(swap(far, "prow", nr))
        image = call(far_kernel, f32(rows, w), uh, ul, image, *beside, flops=1 * term)
    else:
        later = [lax.all_gather(chosen, "prow")]
    if direct:
        owned = spread(own, nr, beside[1])
    sent = call(
        functools.partial(image_kernel, direct),
        [f32(nc * slots, w)] + [f32(2 * slots, w)] * ((nz - 1) * direct),
        uh,
        ul,
        image,
        to,
        *later,
        flops=term,
    )
    meet = lambda v, t: lax.ppermute(v, "pcol", [(k, k ^ (2 * t)) for k in range(nc)])
    whole = sent[0]
    other = swap(whole, "pcol", nc)
    if direct:
        got = [whole] + [meet(v, t) for v, t in zip(sent[1:], AWAY[1:])]
    else:
        blocks = whole.reshape(nz, 2 * slots, w)
        blocks = lax.all_to_all(blocks, "pcol", split_axis=0, concat_axis=0, axis_index_groups=groups, tiled=True)
        got = [blocks.reshape(nc * slots, w)]
        own = jnp.where(jnp.bitwise_and(c, 1) == 0, own[:, :wd], own[:, wd:])
        owned = [lax.all_gather(own, "prow")]

    turned = bf16(nz, wd, 2 * nc * slots)
    high, low = call(
        functools.partial(turn_kernel, direct, owners),
        [turned, turned],
        place,
        *owned,
        scratch_shapes=[pltpu.VMEM((2 * nz * wd, CAP), BF16)],
        flops=8 * nz * wd * nc * slots * CAP,
    )
    parts = [f32(wd, w)] * nz if direct else [f32(nz, wd, w)]
    got, _ = lax.optimization_barrier((got, high))
    mine, theirs = call(functools.partial(part_kernel, slots), [f32(nz * slots, w)] * 2, *got, flops=2 * term)
    other, _ = lax.optimization_barrier((other, mine))
    terms = call(correction_kernel, parts, high, low, whole, other, flops=term)
    theirs, _ = lax.optimization_barrier((theirs, terms[0]))
    sigma_sj = call(pick_kernel, f32(m, w), source, mine, swap(theirs, "pcol", nc), flops=term // 4)
    sigma_sj, d_term = lax.optimization_barrier((sigma_sj, d_term))
    if direct:
        far = [meet(terms[t], t) for t in range(2, nz)]
        far, _ = lax.optimization_barrier((far, sigma_sj))
        total = call(sum_kernel, f32(wd, w), terms[0], *far, flops=4 * term)
        return sigma_sj, d_term + (total + meet(terms[1], 1))
    terms = lax.all_to_all(terms[0], "pcol", split_axis=0, concat_axis=0, axis_index_groups=groups, tiled=True)
    return sigma_sj, d_term + jnp.sum(terms, axis=0)


def solution(mesh):
    placed = (P("pcol", "prow"), P(), P("pcol", "prow"), P("pcol", "prow"))
    return jax.shard_map(
        per_device,
        mesh=mesh,
        in_specs=placed,
        out_specs=(P("pcol", "prow"), P("pcol", "prow")),
        check_vma=False,
    )
```

```python
import functools

import jax
import jax.numpy as jnp
from jax import lax
from jax.experimental import pallas as pl
from jax.experimental.pallas import tpu as pltpu
from jax.sharding import PartitionSpec as P

LANES = 128
BLOCK_CAP = 560
CAP = -(-BLOCK_CAP // 64) * 64
FULL = CAP // LANES
WIDE = (FULL + 1) * LANES
BF16 = jnp.bfloat16
VMEM = pl.BlockSpec(memory_space=pltpu.VMEM)
HBM = pl.BlockSpec(memory_space=pltpu.HBM)


def f32(*shape):
    return jax.ShapeDtypeStruct(shape, jnp.float32)


def bf16(*shape):
    return jax.ShapeDtypeStruct(shape, BF16)


def split(v):
    high = v.astype(BF16)
    return high, (v - high.astype(jnp.float32)).astype(BF16)


def split3(v):
    high = v.astype(BF16)
    mid, low = split(v - high.astype(jnp.float32))
    return high, mid, low


def dot(a, b):
    return jnp.dot(a, b, preferred_element_type=jnp.float32)


def pick_rows(place, v):
    high, mid, low = split3(v)
    return dot(place, high) + (dot(place, mid) + dot(place, low))


def one_hot(mask):
    return jnp.where(mask, 1.0, 0.0)


def count(mask):
    return jnp.sum(jnp.where(mask, 1.0, 0.0)).astype(jnp.int32)


def log2(size):
    return size.bit_length() - 1


def each(refs, owners, fn):
    if owners is None:
        pl.loop(0, refs[0].shape[0])(lambda i: fn(i, refs[0].at[i]))
    else:
        for owner, ref in zip(owners, refs):
            fn(owner, ref)


def select_kernel(structure_ref, sigma_ref, out_ref, held_ref, sems):
    rows, cols = held_ref.shape
    n = structure_ref.shape[0]
    parts = sems.shape[0]
    part = rows // parts
    copies = []
    for k in range(parts):
        at = pl.ds(part * k, part)
        copies.append(pltpu.make_async_copy(sigma_ref.at[at, :], held_ref.at[at, :], sems.at[k]))
        copies[-1].start()
    first = lax.axis_index("prow") * cols
    listed = structure_ref[...].reshape(1, -1)
    names = jnp.broadcast_to(listed, (8, n))
    shift = lax.rem(n - count(listed < first), n)
    named = pltpu.roll(names, shift, 1)[:1, :CAP] - first
    named = jnp.concatenate([named, named[:, FULL * LANES :]], axis=1)
    step = 2 * LANES
    places = []
    for k in range(0, WIDE, step):
        at = lax.broadcasted_iota(jnp.int32, (cols - k, min(step, WIDE - k)), 0) + k
        places.append(one_hot(at == named[:, k : k + step]).astype(BF16))
    for k in range(parts):
        copies[k].wait()
        both = jnp.concatenate(split(held_ref[part * k : part * (k + 1), :]), axis=0)
        picked = [dot(both[:, step * i :], place) for i, place in enumerate(places)]
        picked = jnp.concatenate(picked, axis=1)
        picked = picked[:part] + picked[part:]
        for i in range(FULL):
            at = rows * i + part * k
            out_ref[at : at + part, :] = picked[:, LANES * i : LANES * (i + 1)]
        at = rows * FULL + part * (k % (parts // 2))
        if k < parts // 2:
            out_ref[at : at + part, : LANES // 2] = picked[:, FULL * LANES : CAP]
        else:
            out_ref[at : at + part, LANES // 2 :] = picked[:, CAP:]


def block_term(block_ref, uh, ul, rows):
    parts = [block_ref[rows * i : rows * (i + 1), :] for i in range(FULL)]
    tail = block_ref[rows * FULL : rows * FULL + rows // 2, :]
    parts.append(jnp.concatenate([tail, pltpu.roll(tail, LANES // 2, 1)], axis=0))
    halves = [split(p) for p in parts]
    highs, lows = [h for h, _ in halves], [l for _, l in halves]
    left = jnp.concatenate(highs + highs + lows, axis=1)
    return dot(left, jnp.concatenate([uh, ul, uh], axis=0))


def place_rows(us_ref, u, owner):
    m, w = u.shape
    nc = (us_ref.shape[1] - CAP - 8) // m
    if w % LANES:
        u = jnp.concatenate([u, jnp.zeros((m, LANES - w % LANES), jnp.float32)], axis=1)
    for i in range(us_ref.shape[0]):
        us_ref[i, pl.ds(owner, m, stride=nc), :] = u[:, LANES * i : LANES * (i + 1)]


def rows_of(us_ref, names, owner, width, lane_blocks):
    start = count(names < owner * width)
    base = pl.multiple_of((start // 8) * 8, 8)
    size = CAP + 8
    lanes = [pltpu.roll(us_ref[k, pl.ds(base, size), :], size - (start - base), 0)[:CAP] for k in lane_blocks]
    return jnp.concatenate(lanes, axis=1)


def cut(us_ref, names, owner, width, w):
    u = rows_of(us_ref, names, owner, width, range(us_ref.shape[0]))[:, :w]
    return split(jnp.concatenate([u, jnp.zeros((WIDE - CAP, w), jnp.float32)], axis=0))


def place_kernel(direct, nc, *refs):
    u_refs, us_ref = refs[:-1], refs[-1]
    end = us_ref.shape[1] - CAP - 8
    us_ref[:, end:, :] = jnp.zeros((us_ref.shape[0], CAP + 8, LANES), jnp.float32)
    if direct:
        for owner, u_ref in zip(ring_owners(nc, lax.axis_index("pcol")), u_refs):
            place_rows(us_ref, u_ref[...], owner)
    else:
        pl.loop(0, nc)(lambda k: place_rows(us_ref, u_refs[0][k], k))


def last_kernel(nc, width, structure_ref, before_ref, *refs):
    us_ref, own_ref = refs[-2:]
    c = lax.axis_index("pcol")
    us_ref[...] = before_ref[...]
    if len(refs) > 2:
        place_rows(us_ref, refs[0][...], ring_owners(nc, c)[-1])
    names = structure_ref[...].reshape(1, -1)
    w = own_ref.shape[1]
    own_ref[...] = rows_of(us_ref, names, c // 2, width, [c & 1] if len(refs) > 2 else [0])[:, :w]


AWAY = (0, 2, 3, 1)


def place_of(t):
    return jnp.where(t == 1, 3, jnp.where(t > 1, t - 1, 0))


def row_order(names, c, rows, nc, slots, direct):
    n = names.shape[1]
    z = c // 2
    lg = log2(nc)
    row = c * rows + lax.broadcasted_iota(jnp.int32, (rows, n), 0)
    rank = jnp.sum(one_hot(names < row), axis=1, keepdims=True).astype(jnp.int32)
    member = jnp.sum(one_hot(names == row), axis=1, keepdims=True)
    turn = rank & (nc - 1)
    ahead = (count(names < c * rows) - turn + nc - 1) >> lg
    block = turn >> 1
    if direct:
        block = place_of(block ^ z)
    block = 2 * block + (turn & 1)
    slot = jnp.where(member > 0.5, block * slots + (rank >> lg) - ahead, -1)
    at = lax.broadcasted_iota(jnp.int32, (rows, nc * slots), 1)
    return one_hot(at == slot).T.astype(BF16)


def order_kernel(direct, slots, structure_ref, to_ref, place_ref, from_ref):
    nc = to_ref.shape[0] // slots
    rows = to_ref.shape[1]
    nz = nc // 2
    lg = log2(nc)
    names = structure_ref[...].reshape(1, -1)
    n = names.shape[1]
    m = n // nc
    c = lax.axis_index("pcol")
    z, x = c // 2, c & 1
    to_ref[...] = row_order(names, c, rows, nc, slots, direct)

    start, middle = count(names < 2 * z * rows), count(names < (2 * z + 1) * rows)
    named = pltpu.roll(jnp.broadcast_to(names, (8, n)), lax.rem(n - start, n), 1)[:1, :CAP]
    index = start + lax.broadcasted_iota(jnp.int32, (1, CAP), 1)
    half = jnp.where(named >= (2 * z + 1) * rows, 1, 0)
    turn = index & (nc - 1)
    ahead = (jnp.where(half == 1, middle, start) - turn + nc - 1) >> lg
    block = turn >> 1
    if direct:
        block = place_of(block ^ z)
    slot = (2 * block + (turn & 1)) * slots + (index >> lg) - ahead + (half ^ x) * rows
    slot = jnp.where((named >= 2 * z * rows) & (named < (2 * z + 2) * rows), slot, -1)
    at = lax.broadcasted_iota(jnp.int32, (2 * rows, CAP), 0)
    place_ref[...] = one_hot(at == slot).T.astype(BF16)

    own = lax.broadcasted_iota(jnp.int32, (m, n), 1) - nc * lax.broadcasted_iota(jnp.int32, (m, n), 0)
    mine = jnp.sum(jnp.where(own == c, names, 0).astype(jnp.float32), axis=1, keepdims=True)
    source = jnp.zeros((m, 1), jnp.int32)
    before = jnp.zeros((m, 1), jnp.int32)
    for k in range(1, nc):
        less = mine < float(k * rows)
        source = source + jnp.where(less, 0, 1)
        before = jnp.where(less, before, count(less))
    block = source >> 1
    if direct:
        block = place_of(block ^ z)
    block = block + nz * ((source ^ c) & 1)
    slot = block * slots + lax.broadcasted_iota(jnp.int32, (m, 1), 0) - before
    at = lax.broadcasted_iota(jnp.int32, (m, rows), 1)
    from_ref[...] = one_hot(at == slot).astype(BF16)


def near_kernel(owners, rest, structure_ref, us_ref, *refs):
    block_refs, (image_ref, uh_ref, ul_ref) = refs[:-3], refs[-3:]
    rows, w = image_ref.shape
    width = rows * 2
    names = structure_ref[...].reshape(1, -1)
    r = lax.axis_index("prow")
    image = jnp.zeros((rows, w), jnp.float32)
    for owner, block_ref in zip(owners(r), block_refs):
        image = image + block_term(block_ref, *cut(us_ref, names, owner, width, w), rows)
    image_ref[...] = image
    if rest is None:

        @pl.loop(0, uh_ref.shape[0])
        def _(k):
            uh_ref[k], ul_ref[k] = cut(us_ref, names, k, width, w)

    else:
        for k, owner in enumerate(rest(r)):
            uh_ref[k], ul_ref[k] = cut(us_ref, names, owner, width, w)


def far_terms(places, uh_ref, ul_ref, image, block_refs):
    rows = image.shape[0]
    for k, block_ref in zip(places, block_refs):
        image = image + block_term(block_ref, uh_ref[k], ul_ref[k], rows)
    return image


def far_kernel(uh_ref, ul_ref, part_ref, *refs):
    places = [0] + list(range(1, uh_ref.shape[0], 2))
    refs[-1][...] = far_terms(places, uh_ref, ul_ref, part_ref[...], refs[:-1])


def image_kernel(direct, uh_ref, ul_ref, part_ref, to_ref, *refs):
    n_in = (uh_ref.shape[0] - 1) // 2 if direct else 1
    block_refs, out_refs = refs[:n_in], refs[n_in:]
    n_out = len(out_refs)
    rows = part_ref.shape[0]
    image = part_ref[...]
    if direct:
        image = far_terms(range(2, uh_ref.shape[0], 2), uh_ref, ul_ref, image, block_refs)
    else:
        stack = block_refs[0]
        add = lambda b, v: v + block_term(stack.at[b], uh_ref[b], ul_ref[b], rows)
        image = lax.fori_loop(0, stack.shape[0], add, image)
    high, low = split(image)
    image = dot(to_ref[...], high) + dot(to_ref[...], low)
    out_refs[0][...] = image
    size = image.shape[0] // n_out
    for k in range(1, n_out):
        out_refs[k][...] = image[size * k : size * (k + 1)]


def turn_kernel(direct, owners, place_ref, *refs):
    high_ref, low_ref, held_ref = refs[-3:]
    nz, wd, size = high_ref.shape
    z = lax.axis_index("pcol") // 2

    def put(owner, u_ref):
        where = (owner ^ z) if direct else owner
        high, low = split(u_ref[...].T)
        held_ref[pl.ds(pl.multiple_of(where * wd, wd), wd), :] = high
        held_ref[pl.ds(pl.multiple_of((where + nz) * wd, wd), wd), :] = low

    each(refs[:-3], owners(lax.axis_index("prow")) if direct else None, put)
    turned = dot(held_ref[...], place_ref[...]).astype(BF16).reshape(2, nz, wd, size)
    high_ref[...] = turned[0]
    low_ref[...] = turned[1]


def correction_kernel(high_ref, low_ref, mine_ref, other_ref, *out_refs):
    sh, sl = split(jnp.concatenate([mine_ref[...], other_ref[...]], axis=0))

    def term(t):
        return dot(high_ref[t], sh) + (dot(high_ref[t], sl) + dot(low_ref[t], sh))

    if len(out_refs) > 1:
        for t, out_ref in enumerate(out_refs):
            out_ref[...] = term(t)
    else:

        @pl.loop(0, out_refs[0].shape[0])
        def _(t):
            out_refs[0][t] = term(t)


def sum_kernel(*refs):
    total = refs[0][...]
    for ref in refs[1:-1]:
        total = total + ref[...]
    refs[-1][...] = total


def part_kernel(slots, *refs):
    mine_ref, theirs_ref = refs[-2:]
    first = (lax.axis_index("pcol") & 1) == 0
    blocks = mine_ref.shape[0] // slots
    mine, theirs = [], []
    for ref in refs[:-2]:
        for k in range(blocks // len(refs[:-2])):
            low = ref[2 * slots * k : 2 * slots * k + slots, :]
            high = ref[2 * slots * k + slots : 2 * slots * (k + 1), :]
            mine.append(jnp.where(first, low, high))
            theirs.append(jnp.where(first, high, low))
    mine_ref[...] = jnp.concatenate(mine, axis=0)
    theirs_ref[...] = jnp.concatenate(theirs, axis=0)


def last_sum_kernel(from_ref, mine_ref, other_ref, d_ref, total_ref, got_ref, sj_ref, jj_ref):
    sj_ref[...] = -pick_rows(from_ref[...], jnp.concatenate([mine_ref[...], other_ref[...]], axis=0))
    jj_ref[...] = d_ref[...] + (total_ref[...] + got_ref[...])


def call(kernel, out_shape, *args, flops=0, vmem=20, **kw):
    many = isinstance(out_shape, (list, tuple))
    size = flops and sum(v.size * v.dtype.itemsize for v in jax.tree.leaves((out_shape, args)))
    kw = {"in_specs": [VMEM] * len(args)} | kw
    return pl.pallas_call(
        kernel,
        out_shape=out_shape,
        out_specs=[VMEM] * len(out_shape) if many else VMEM,
        cost_estimate=pl.CostEstimate(flops=flops, bytes_accessed=size, transcendentals=0),
        compiler_params=pltpu.CompilerParams(vmem_limit_bytes=vmem * 2**20),
        **kw,
    )(*args)


def swap(v, axis, size):
    return lax.ppermute(v, axis, [(k, k ^ 1) for k in range(size)])


def spread(v, size, after):
    blocks = [v, swap(v, "prow", size)]
    v, _ = lax.optimization_barrier((v, after))
    for t in range(1, size // 2):
        for flip in range(2):
            blocks.append(lax.ppermute(v, "prow", [(k, ((k + 2 * t) % size) ^ flip) for k in range(size)]))
    return blocks


def relative_owners(size, r):
    out = []
    for t in range(size // 2):
        owner = (r - 2 * t) & (size - 1)
        out += [owner, owner ^ 1]
    return out


def ring_gather(u, nc, aside):
    ring = [2 * z for z in range(nc // 2)] + [2 * z + 1 for z in reversed(range(nc // 2))]
    pairs = [(ring[q - 1], ring[q]) for q in range(nc)]
    back = [(b, a) for a, b in pairs]
    blocks = [u]
    up = down = u
    for step in range(1, nc // 2):
        up, down = lax.ppermute(up, "pcol", pairs), lax.ppermute(down, "pcol", back)
        if step == 1:
            up, down = lax.optimization_barrier((up, down))
        blocks += [up, down]
    last, aside = lax.optimization_barrier((lax.ppermute(up, "pcol", pairs), aside))
    return blocks + [last], aside


def ring_owners(nc, c):
    q = jnp.where((c & 1) == 0, c >> 1, nc - 1 - (c >> 1))
    out = []
    for k in range(nc):
        step = (k + 1) // 2
        at = (q - step if k % 2 else q + step) & (nc - 1)
        out.append(jnp.where(at < nc // 2, 2 * at, 2 * (nc - 1 - at) + 1))
    return out


def per_device(sigma_top, structure, u_panel, d_term):
    nc, nr = lax.axis_size("pcol"), lax.axis_size("prow")
    c = lax.axis_index("pcol")
    nz = nc // 2
    rows, cols = sigma_top.shape
    m, w = u_panel.shape
    wd = w // 2
    n = structure.shape[0]
    slots = -(-rows // nc)
    direct = (nr, nc) == (4, 8)
    names = structure
    groups = [[2 * k + x for k in range(nz)] for x in range(2)]
    owners = functools.partial(relative_owners, nr)

    chosen = call(
        select_kernel,
        f32(rows * CAP // LANES, LANES),
        names,
        sigma_top,
        in_specs=[VMEM, HBM],
        scratch_shapes=[pltpu.VMEM((rows, cols), jnp.float32), pltpu.SemaphoreType.DMA((2,))],
        flops=4 * rows * cols * WIDE,
        vmem=52,
    )
    to, place, source = call(
        functools.partial(order_kernel, direct, slots),
        [bf16(nc * slots, rows), bf16(CAP, 2 * nc * slots), bf16(m, nc * slots)],
        names,
    )
    if direct:
        u_all, to = ring_gather(u_panel, nc, to)
    else:
        u_all = [lax.all_gather(u_panel, "pcol")]
    term = 6 * rows * WIDE * w
    placed = f32(-(-w // LANES), n + CAP + 8, LANES)
    early, late = (u_all[:-1], u_all[-1:]) if direct else (u_all, [])
    before = call(functools.partial(place_kernel, direct, nc), placed, *early, flops=8 * term)
    us, own = call(
        functools.partial(last_kernel, nc, cols),
        [placed, f32(CAP, wd if direct else w)],
        names,
        before,
        *late,
        flops=term,
    )
    halves = bf16(nr - 1 if direct else nr, WIDE, w)
    near = [chosen] if direct else []
    image, uh, ul = call(
        functools.partial(near_kernel, lambda r: owners(r)[:1], (lambda r: owners(r)[1:]) if direct else None),
        [f32(rows, w), halves, halves],
        names,
        us,
        *near,
        flops=0,
    )
    if direct:
        beside, later = [swap(chosen, "prow", nr)], []
        for t in range(1, nr // 2):
            far = lax.ppermute(chosen, "prow", [(k, (k + 2 * t) % nr) for k in range(nr)])
            far, _ = lax.optimization_barrier((far, image))
            beside.append(far)
            later.append(swap(far, "prow", nr))
        image = call(far_kernel, f32(rows, w), uh, ul, image, *beside, flops=1 * term)
    else:
        later = [lax.all_gather(chosen, "prow")]
    if direct:
        owned = spread(own, nr, beside[1])
    sent = call(
        functools.partial(image_kernel, direct),
        [f32(nc * slots, w)] + [f32(2 * slots, w)] * ((nz - 1) * direct),
        uh,
        ul,
        image,
        to,
        *later,
        flops=term,
    )
    meet = lambda v, t: lax.ppermute(v, "pcol", [(k, k ^ (2 * t)) for k in range(nc)])
    whole = sent[0]
    other = swap(whole, "pcol", nc)
    if direct:
        got = [whole] + [meet(v, t) for v, t in zip(sent[1:], AWAY[1:])]
    else:
        blocks = whole.reshape(nz, 2 * slots, w)
        blocks = lax.all_to_all(blocks, "pcol", split_axis=0, concat_axis=0, axis_index_groups=groups, tiled=True)
        got = [blocks.reshape(nc * slots, w)]
        own = jnp.where(jnp.bitwise_and(c, 1) == 0, own[:, :wd], own[:, wd:])
        owned = [lax.all_gather(own, "prow")]

    turned = bf16(nz, wd, 2 * nc * slots)
    high, low = call(
        functools.partial(turn_kernel, direct, owners),
        [turned, turned],
        place,
        *owned,
        scratch_shapes=[pltpu.VMEM((2 * nz * wd, CAP), BF16)],
        flops=8 * nz * wd * nc * slots * CAP,
    )
    parts = [f32(wd, w)] * nz if direct else [f32(nz, wd, w)]
    got, _ = lax.optimization_barrier((got, high))
    mine, theirs = call(functools.partial(part_kernel, slots), [f32(nz * slots, w)] * 2, *got, flops=2 * term)
    other, _ = lax.optimization_barrier((other, mine))
    terms = call(correction_kernel, parts, high, low, whole, other, flops=term)
    theirs, _ = lax.optimization_barrier((theirs, terms[0]))
    theirs = swap(theirs, "pcol", nc)
    if direct:
        far = [meet(terms[t], t) for t in range(2, nz)]
        total = call(sum_kernel, f32(wd, w), terms[0], *far, flops=4 * term)
        rest = meet(terms[1], 1)
    else:
        terms = lax.all_to_all(terms[0], "pcol", split_axis=0, concat_axis=0, axis_index_groups=groups, tiled=True)
        total, rest = jnp.sum(terms[1:], axis=0), terms[0]
    outs = [f32(m, w), f32(wd, w)]
    return tuple(call(last_sum_kernel, outs, source, mine, theirs, d_term, total, rest, flops=term // 4))


def solution(mesh):
    placed = (P("pcol", "prow"), P(), P("pcol", "prow"), P("pcol", "prow"))
    return jax.shard_map(
        per_device,
        mesh=mesh,
        in_specs=placed,
        out_specs=(P("pcol", "prow"), P("pcol", "prow")),
        check_vma=False,
    )
```

```python
import functools

import jax
import jax.numpy as jnp
from jax import lax
from jax.experimental import pallas as pl
from jax.experimental.pallas import tpu as pltpu
from jax.sharding import PartitionSpec as P

LANES = 128
BLOCK_CAP = 560
CAP = -(-BLOCK_CAP // 64) * 64
FULL = CAP // LANES
WIDE = (FULL + 1) * LANES
BF16 = jnp.bfloat16
VMEM = pl.BlockSpec(memory_space=pltpu.VMEM)
HBM = pl.BlockSpec(memory_space=pltpu.HBM)


def f32(*shape):
    return jax.ShapeDtypeStruct(shape, jnp.float32)


def bf16(*shape):
    return jax.ShapeDtypeStruct(shape, BF16)


def split(v):
    high = v.astype(BF16)
    return high, (v - high.astype(jnp.float32)).astype(BF16)


def split3(v):
    high = v.astype(BF16)
    mid, low = split(v - high.astype(jnp.float32))
    return high, mid, low


def dot(a, b):
    return jnp.dot(a, b, preferred_element_type=jnp.float32)


def pick_rows(place, v):
    high, mid, low = split3(v)
    return dot(place, high) + (dot(place, mid) + dot(place, low))


def one_hot(mask):
    return jnp.where(mask, 1.0, 0.0)


def count(mask):
    return jnp.sum(jnp.where(mask, 1.0, 0.0)).astype(jnp.int32)


def log2(size):
    return size.bit_length() - 1


def each(refs, owners, fn):
    if owners is None:
        pl.loop(0, refs[0].shape[0])(lambda i: fn(i, refs[0].at[i]))
    else:
        for owner, ref in zip(owners, refs):
            fn(owner, ref)


def select_kernel(structure_ref, sigma_ref, out_ref, held_ref, sems):
    rows, cols = held_ref.shape
    n = structure_ref.shape[0]
    parts = sems.shape[0]
    part = rows // parts
    copies = []
    for k in range(parts):
        at = pl.ds(part * k, part)
        copies.append(pltpu.make_async_copy(sigma_ref.at[at, :], held_ref.at[at, :], sems.at[k]))
        copies[-1].start()
    first = lax.axis_index("prow") * cols
    listed = structure_ref[...].reshape(1, -1)
    names = jnp.broadcast_to(listed, (8, n))
    shift = lax.rem(n - count(listed < first), n)
    named = pltpu.roll(names, shift, 1)[:1, :CAP] - first
    named = jnp.concatenate([named, named[:, FULL * LANES :]], axis=1)
    step = 2 * LANES
    places = []
    for k in range(0, WIDE, step):
        at = lax.broadcasted_iota(jnp.int32, (cols - k, min(step, WIDE - k)), 0) + k
        places.append(one_hot(at == named[:, k : k + step]).astype(BF16))
    for k in range(parts):
        copies[k].wait()
        both = jnp.concatenate(split(held_ref[part * k : part * (k + 1), :]), axis=0)
        picked = [dot(both[:, step * i :], place) for i, place in enumerate(places)]
        picked = jnp.concatenate(picked, axis=1)
        picked = picked[:part] + picked[part:]
        for i in range(FULL):
            at = rows * i + part * k
            out_ref[at : at + part, :] = picked[:, LANES * i : LANES * (i + 1)]
        at = rows * FULL + part * (k % (parts // 2))
        if k < parts // 2:
            out_ref[at : at + part, : LANES // 2] = picked[:, FULL * LANES : CAP]
        else:
            out_ref[at : at + part, LANES // 2 :] = picked[:, CAP:]


def block_term(block_ref, uh, ul, rows):
    parts = [block_ref[rows * i : rows * (i + 1), :] for i in range(FULL)]
    tail = block_ref[rows * FULL : rows * FULL + rows // 2, :]
    parts.append(jnp.concatenate([tail, pltpu.roll(tail, LANES // 2, 1)], axis=0))
    halves = [split(p) for p in parts]
    highs, lows = [h for h, _ in halves], [l for _, l in halves]
    left = jnp.concatenate(highs + highs + lows, axis=1)
    return dot(left, jnp.concatenate([uh, ul, uh], axis=0))


def place_rows(us_ref, u, owner):
    m, w = u.shape
    nc = (us_ref.shape[1] - CAP - 8) // m
    if w % LANES:
        u = jnp.concatenate([u, jnp.zeros((m, LANES - w % LANES), jnp.float32)], axis=1)
    for i in range(us_ref.shape[0]):
        us_ref[i, pl.ds(owner, m, stride=nc), :] = u[:, LANES * i : LANES * (i + 1)]


def rows_of(us_ref, names, owner, width, lane_blocks):
    start = count(names < owner * width)
    base = pl.multiple_of((start // 8) * 8, 8)
    size = CAP + 8
    lanes = [pltpu.roll(us_ref[k, pl.ds(base, size), :], size - (start - base), 0)[:CAP] for k in lane_blocks]
    return jnp.concatenate(lanes, axis=1)


def cut(us_ref, names, owner, width, w):
    u = rows_of(us_ref, names, owner, width, range(us_ref.shape[0]))[:, :w]
    return split(jnp.concatenate([u, jnp.zeros((WIDE - CAP, w), jnp.float32)], axis=0))


def place_kernel(direct, nc, *refs):
    u_refs, us_ref = refs[:-1], refs[-1]
    end = us_ref.shape[1] - CAP - 8
    us_ref[:, end:, :] = jnp.zeros((us_ref.shape[0], CAP + 8, LANES), jnp.float32)
    if direct:
        for owner, u_ref in zip(ring_owners(nc, lax.axis_index("pcol")), u_refs):
            place_rows(us_ref, u_ref[...], owner)
    else:
        pl.loop(0, nc)(lambda k: place_rows(us_ref, u_refs[0][k], k))


def last_kernel(nc, width, structure_ref, before_ref, *refs):
    us_ref, own_ref = refs[-2:]
    c = lax.axis_index("pcol")
    us_ref[...] = before_ref[...]
    if len(refs) > 2:
        place_rows(us_ref, refs[0][...], ring_owners(nc, c)[-1])
    names = structure_ref[...].reshape(1, -1)
    w = own_ref.shape[1]
    own_ref[...] = rows_of(us_ref, names, c // 2, width, [c & 1] if len(refs) > 2 else [0])[:, :w]


def row_order(names, c, rows, nc, slots, direct):
    n = names.shape[1]
    z = c // 2
    lg = log2(nc)
    row = c * rows + lax.broadcasted_iota(jnp.int32, (rows, n), 0)
    rank = jnp.sum(one_hot(names < row), axis=1, keepdims=True).astype(jnp.int32)
    member = jnp.sum(one_hot(names == row), axis=1, keepdims=True)
    turn = rank & (nc - 1)
    ahead = (count(names < c * rows) - turn + nc - 1) >> lg
    block = turn >> 1
    if direct:
        block = block ^ z
    block = 2 * block + (turn & 1)
    slot = jnp.where(member > 0.5, block * slots + (rank >> lg) - ahead, -1)
    at = lax.broadcasted_iota(jnp.int32, (rows, nc * slots), 1)
    return one_hot(at == slot).T.astype(BF16)


def order_kernel(direct, slots, structure_ref, to_ref, place_ref, from_ref):
    nc = to_ref.shape[0] // slots
    rows = to_ref.shape[1]
    nz = nc // 2
    lg = log2(nc)
    names = structure_ref[...].reshape(1, -1)
    n = names.shape[1]
    m = n // nc
    c = lax.axis_index("pcol")
    z, x = c // 2, c & 1
    to_ref[...] = row_order(names, c, rows, nc, slots, direct)

    start, middle = count(names < 2 * z * rows), count(names < (2 * z + 1) * rows)
    named = pltpu.roll(jnp.broadcast_to(names, (8, n)), lax.rem(n - start, n), 1)[:1, :CAP]
    index = start + lax.broadcasted_iota(jnp.int32, (1, CAP), 1)
    half = jnp.where(named >= (2 * z + 1) * rows, 1, 0)
    turn = index & (nc - 1)
    ahead = (jnp.where(half == 1, middle, start) - turn + nc - 1) >> lg
    block = turn >> 1
    if direct:
        block = block ^ z
    slot = (2 * block + (turn & 1)) * slots + (index >> lg) - ahead + (half ^ x) * rows
    slot = jnp.where((named >= 2 * z * rows) & (named < (2 * z + 2) * rows), slot, -1)
    at = lax.broadcasted_iota(jnp.int32, (2 * rows, CAP), 0)
    place_ref[...] = one_hot(at == slot).T.astype(BF16)

    own = lax.broadcasted_iota(jnp.int32, (m, n), 1) - nc * lax.broadcasted_iota(jnp.int32, (m, n), 0)
    mine = jnp.sum(jnp.where(own == c, names, 0).astype(jnp.float32), axis=1, keepdims=True)
    source = jnp.zeros((m, 1), jnp.int32)
    before = jnp.zeros((m, 1), jnp.int32)
    for k in range(1, nc):
        less = mine < float(k * rows)
        source = source + jnp.where(less, 0, 1)
        before = jnp.where(less, before, count(less))
    block = source >> 1
    if direct:
        block = block ^ z
    block = block + nz * ((source ^ c) & 1)
    slot = block * slots + lax.broadcasted_iota(jnp.int32, (m, 1), 0) - before
    at = lax.broadcasted_iota(jnp.int32, (m, rows), 1)
    from_ref[...] = one_hot(at == slot).astype(BF16)


def near_kernel(owners, rest, structure_ref, us_ref, *refs):
    block_refs, (image_ref, uh_ref, ul_ref) = refs[:-3], refs[-3:]
    rows, w = image_ref.shape
    width = rows * 2
    names = structure_ref[...].reshape(1, -1)
    r = lax.axis_index("prow")
    image = jnp.zeros((rows, w), jnp.float32)
    for owner, block_ref in zip(owners(r), block_refs):
        image = image + block_term(block_ref, *cut(us_ref, names, owner, width, w), rows)
    image_ref[...] = image
    if rest is None:

        @pl.loop(0, uh_ref.shape[0])
        def _(k):
            uh_ref[k], ul_ref[k] = cut(us_ref, names, k, width, w)

    else:
        for k, owner in enumerate(rest(r)):
            uh_ref[k], ul_ref[k] = cut(us_ref, names, owner, width, w)


def far_terms(places, uh_ref, ul_ref, image, block_refs):
    rows = image.shape[0]
    for k, block_ref in zip(places, block_refs):
        image = image + block_term(block_ref, uh_ref[k], ul_ref[k], rows)
    return image


def far_kernel(uh_ref, ul_ref, part_ref, *refs):
    places = [0] + list(range(1, uh_ref.shape[0], 2))
    refs[-1][...] = far_terms(places, uh_ref, ul_ref, part_ref[...], refs[:-1])


def image_kernel(direct, uh_ref, ul_ref, part_ref, to_ref, *refs):
    n_in = (uh_ref.shape[0] - 1) // 2 if direct else 1
    block_refs, out_refs = refs[:n_in], refs[n_in:]
    n_out = len(out_refs)
    rows = part_ref.shape[0]
    image = part_ref[...]
    if direct:
        image = far_terms(range(2, uh_ref.shape[0], 2), uh_ref, ul_ref, image, block_refs)
    else:
        stack = block_refs[0]
        add = lambda b, v: v + block_term(stack.at[b], uh_ref[b], ul_ref[b], rows)
        image = lax.fori_loop(0, stack.shape[0], add, image)
    high, low = split(image)
    image = dot(to_ref[...], high) + dot(to_ref[...], low)
    out_refs[0][...] = image
    size = image.shape[0] // n_out
    for k in range(1, n_out):
        out_refs[k][...] = image[size * k : size * (k + 1)]


def turn_kernel(direct, owners, place_ref, *refs):
    high_ref, low_ref, held_ref = refs[-3:]
    nz, wd, size = high_ref.shape
    z = lax.axis_index("pcol") // 2

    def put(owner, u_ref):
        where = (owner ^ z) if direct else owner
        high, low = split(u_ref[...].T)
        held_ref[pl.ds(pl.multiple_of(where * wd, wd), wd), :] = high
        held_ref[pl.ds(pl.multiple_of((where + nz) * wd, wd), wd), :] = low

    each(refs[:-3], owners(lax.axis_index("prow")) if direct else None, put)
    turned = dot(held_ref[...], place_ref[...]).astype(BF16).reshape(2, nz, wd, size)
    high_ref[...] = turned[0]
    low_ref[...] = turned[1]


def correction_kernel(high_ref, low_ref, mine_ref, other_ref, *out_refs):
    sh, sl = split(jnp.concatenate([mine_ref[...], other_ref[...]], axis=0))

    def term(t):
        return dot(high_ref[t], sh) + (dot(high_ref[t], sl) + dot(low_ref[t], sh))

    if len(out_refs) > 1:
        for t, out_ref in enumerate(out_refs):
            out_ref[...] = term(t)
    else:

        @pl.loop(0, out_refs[0].shape[0])
        def _(t):
            out_refs[0][t] = term(t)


def sum_kernel(*refs):
    total = refs[0][...]
    for ref in refs[1:-1]:
        total = total + ref[...]
    refs[-1][...] = total


def part_kernel(slots, *refs):
    mine_ref, theirs_ref = refs[-2:]
    first = (lax.axis_index("pcol") & 1) == 0
    blocks = mine_ref.shape[0] // slots
    mine, theirs = [], []
    for ref in refs[:-2]:
        for k in range(blocks // len(refs[:-2])):
            low = ref[2 * slots * k : 2 * slots * k + slots, :]
            high = ref[2 * slots * k + slots : 2 * slots * (k + 1), :]
            mine.append(jnp.where(first, low, high))
            theirs.append(jnp.where(first, high, low))
    mine_ref[...] = jnp.concatenate(mine, axis=0)
    theirs_ref[...] = jnp.concatenate(theirs, axis=0)


def last_sum_kernel(from_ref, mine_ref, other_ref, d_ref, total_ref, got_ref, sj_ref, jj_ref):
    sj_ref[...] = -pick_rows(from_ref[...], jnp.concatenate([mine_ref[...], other_ref[...]], axis=0))
    jj_ref[...] = d_ref[...] + (total_ref[...] + got_ref[...])


def call(kernel, out_shape, *args, flops=0, vmem=20, **kw):
    many = isinstance(out_shape, (list, tuple))
    size = flops and sum(v.size * v.dtype.itemsize for v in jax.tree.leaves((out_shape, args)))
    kw = {"in_specs": [VMEM] * len(args)} | kw
    return pl.pallas_call(
        kernel,
        out_shape=out_shape,
        out_specs=[VMEM] * len(out_shape) if many else VMEM,
        cost_estimate=pl.CostEstimate(flops=flops, bytes_accessed=size, transcendentals=0),
        compiler_params=pltpu.CompilerParams(vmem_limit_bytes=vmem * 2**20),
        **kw,
    )(*args)


def swap(v, axis, size):
    return lax.ppermute(v, axis, [(k, k ^ 1) for k in range(size)])


def spread(v, size, after):
    blocks = [v, swap(v, "prow", size)]
    v, _ = lax.optimization_barrier((v, after))
    for t in range(1, size // 2):
        for flip in range(2):
            blocks.append(lax.ppermute(v, "prow", [(k, ((k + 2 * t) % size) ^ flip) for k in range(size)]))
    return blocks


def relative_owners(size, r):
    out = []
    for t in range(size // 2):
        owner = (r - 2 * t) & (size - 1)
        out += [owner, owner ^ 1]
    return out


def ring_gather(u, nc, aside):
    ring = [2 * z for z in range(nc // 2)] + [2 * z + 1 for z in reversed(range(nc // 2))]
    pairs = [(ring[q - 1], ring[q]) for q in range(nc)]
    back = [(b, a) for a, b in pairs]
    blocks = [u]
    up = down = u
    for step in range(1, nc // 2):
        up, down = lax.ppermute(up, "pcol", pairs), lax.ppermute(down, "pcol", back)
        if step == 1:
            up, down = lax.optimization_barrier((up, down))
        blocks += [up, down]
    last, aside = lax.optimization_barrier((lax.ppermute(up, "pcol", pairs), aside))
    return blocks + [last], aside


def ring_owners(nc, c):
    q = jnp.where((c & 1) == 0, c >> 1, nc - 1 - (c >> 1))
    out = []
    for k in range(nc):
        step = (k + 1) // 2
        at = (q - step if k % 2 else q + step) & (nc - 1)
        out.append(jnp.where(at < nc // 2, 2 * at, 2 * (nc - 1 - at) + 1))
    return out


def per_device(sigma_top, structure, u_panel, d_term):
    nc, nr = lax.axis_size("pcol"), lax.axis_size("prow")
    c = lax.axis_index("pcol")
    nz = nc // 2
    rows, cols = sigma_top.shape
    m, w = u_panel.shape
    wd = w // 2
    n = structure.shape[0]
    slots = -(-rows // nc)
    direct = (nr, nc) == (4, 8)
    names = structure
    groups = [[2 * k + x for k in range(nz)] for x in range(2)]
    owners = functools.partial(relative_owners, nr)

    chosen = call(
        select_kernel,
        f32(rows * CAP // LANES, LANES),
        names,
        sigma_top,
        in_specs=[VMEM, HBM],
        scratch_shapes=[pltpu.VMEM((rows, cols), jnp.float32), pltpu.SemaphoreType.DMA((2,))],
        flops=4 * rows * cols * WIDE,
        vmem=52,
    )
    to, place, source = call(
        functools.partial(order_kernel, direct, slots),
        [bf16(nc * slots, rows), bf16(CAP, 2 * nc * slots), bf16(m, nc * slots)],
        names,
    )
    if direct:
        u_all, to = ring_gather(u_panel, nc, to)
    else:
        u_all = [lax.all_gather(u_panel, "pcol")]
    term = 6 * rows * WIDE * w
    placed = f32(-(-w // LANES), n + CAP + 8, LANES)
    early, late = (u_all[:-1], u_all[-1:]) if direct else (u_all, [])
    before = call(functools.partial(place_kernel, direct, nc), placed, *early, flops=8 * term)
    us, own = call(
        functools.partial(last_kernel, nc, cols),
        [placed, f32(CAP, wd if direct else w)],
        names,
        before,
        *late,
        flops=term,
    )
    halves = bf16(nr - 1 if direct else nr, WIDE, w)
    near = [chosen] if direct else []
    image, uh, ul = call(
        functools.partial(near_kernel, lambda r: owners(r)[:1], (lambda r: owners(r)[1:]) if direct else None),
        [f32(rows, w), halves, halves],
        names,
        us,
        *near,
        flops=0,
    )
    if direct:
        beside, later = [swap(chosen, "prow", nr)], []
        for t in range(1, nr // 2):
            far = lax.ppermute(chosen, "prow", [(k, (k + 2 * t) % nr) for k in range(nr)])
            far, _ = lax.optimization_barrier((far, image))
            beside.append(far)
            later.append(swap(far, "prow", nr))
        image = call(far_kernel, f32(rows, w), uh, ul, image, *beside, flops=1 * term)
    else:
        later = [lax.all_gather(chosen, "prow")]
    if direct:
        owned = spread(own, nr, beside[1])
    sent = call(
        functools.partial(image_kernel, direct),
        [f32(nc * slots, w)] + [f32(2 * slots, w)] * ((nz - 1) * direct),
        uh,
        ul,
        image,
        to,
        *later,
        flops=term,
    )
    meet = lambda v, t: lax.ppermute(v, "pcol", [(k, k ^ (2 * t)) for k in range(nc)])
    whole = sent[0]
    other = swap(whole, "pcol", nc)
    if direct:
        got = [whole] + [meet(sent[t], t) for t in range(1, nz)]
    else:
        blocks = whole.reshape(nz, 2 * slots, w)
        blocks = lax.all_to_all(blocks, "pcol", split_axis=0, concat_axis=0, axis_index_groups=groups, tiled=True)
        got = [blocks.reshape(nc * slots, w)]
        own = jnp.where(jnp.bitwise_and(c, 1) == 0, own[:, :wd], own[:, wd:])
        owned = [lax.all_gather(own, "prow")]

    turned = bf16(nz, wd, 2 * nc * slots)
    high, low = call(
        functools.partial(turn_kernel, direct, owners),
        [turned, turned],
        place,
        *owned,
        scratch_shapes=[pltpu.VMEM((2 * nz * wd, CAP), BF16)],
        flops=8 * nz * wd * nc * slots * CAP,
    )
    parts = [f32(wd, w)] * nz if direct else [f32(nz, wd, w)]
    got, _ = lax.optimization_barrier((got, high))
    mine, theirs = call(functools.partial(part_kernel, slots), [f32(nz * slots, w)] * 2, *got, flops=2 * term)
    other, _ = lax.optimization_barrier((other, mine))
    terms = call(correction_kernel, parts, high, low, whole, other, flops=term)
    theirs, _ = lax.optimization_barrier((theirs, terms[0]))
    theirs = swap(theirs, "pcol", nc)
    if direct:
        far = [meet(terms[t], t) for t in range(2, nz)]
        total = call(sum_kernel, f32(wd, w), terms[0], *far, flops=4 * term)
        rest = meet(terms[1], 1)
    else:
        terms = lax.all_to_all(terms[0], "pcol", split_axis=0, concat_axis=0, axis_index_groups=groups, tiled=True)
        total, rest = jnp.sum(terms[1:], axis=0), terms[0]
    outs = [f32(m, w), f32(wd, w)]
    return tuple(call(last_sum_kernel, outs, source, mine, theirs, d_term, total, rest, flops=term // 4))


def solution(mesh):
    placed = (P("pcol", "prow"), P(), P("pcol", "prow"), P("pcol", "prow"))
    return jax.shard_map(
        per_device,
        mesh=mesh,
        in_specs=placed,
        out_specs=(P("pcol", "prow"), P("pcol", "prow")),
        check_vma=False,
    )
```

```python
import functools

import jax
import jax.numpy as jnp
from jax import lax
from jax.experimental import pallas as pl
from jax.experimental.pallas import tpu as pltpu
from jax.sharding import PartitionSpec as P

LANES = 128
BLOCK_CAP = 560
CAP = -(-BLOCK_CAP // 64) * 64
FULL = CAP // LANES
WIDE = (FULL + 1) * LANES
BF16 = jnp.bfloat16
VMEM = pl.BlockSpec(memory_space=pltpu.VMEM)
HBM = pl.BlockSpec(memory_space=pltpu.HBM)


def f32(*shape):
    return jax.ShapeDtypeStruct(shape, jnp.float32)


def bf16(*shape):
    return jax.ShapeDtypeStruct(shape, BF16)


def split(v):
    high = v.astype(BF16)
    return high, (v - high.astype(jnp.float32)).astype(BF16)


def split3(v):
    high = v.astype(BF16)
    mid, low = split(v - high.astype(jnp.float32))
    return high, mid, low


def dot(a, b):
    return jnp.dot(a, b, preferred_element_type=jnp.float32)


def pick_rows(place, v):
    high, mid, low = split3(v)
    return dot(place, high) + (dot(place, mid) + dot(place, low))


def one_hot(mask):
    return jnp.where(mask, 1.0, 0.0)


def count(mask):
    return jnp.sum(jnp.where(mask, 1.0, 0.0)).astype(jnp.int32)


def log2(size):
    return size.bit_length() - 1


def each(refs, owners, fn):
    if owners is None:
        pl.loop(0, refs[0].shape[0])(lambda i: fn(i, refs[0].at[i]))
    else:
        for owner, ref in zip(owners, refs):
            fn(owner, ref)


def select_kernel(structure_ref, sigma_ref, out_ref, held_ref, sems):
    rows, cols = held_ref.shape
    n = structure_ref.shape[0]
    parts = sems.shape[0]
    part = rows // parts
    copies = []
    for k in range(parts):
        at = pl.ds(part * k, part)
        copies.append(pltpu.make_async_copy(sigma_ref.at[at, :], held_ref.at[at, :], sems.at[k]))
        copies[-1].start()
    first = lax.axis_index("prow") * cols
    listed = structure_ref[...].reshape(1, -1)
    names = jnp.broadcast_to(listed, (8, n))
    shift = lax.rem(n - count(listed < first), n)
    named = pltpu.roll(names, shift, 1)[:1, :CAP] - first
    named = jnp.concatenate([named, named[:, FULL * LANES :]], axis=1)
    step = 2 * LANES
    places = []
    for k in range(0, WIDE, step):
        at = lax.broadcasted_iota(jnp.int32, (cols - k, min(step, WIDE - k)), 0) + k
        places.append(one_hot(at == named[:, k : k + step]).astype(BF16))
    for k in range(parts):
        copies[k].wait()
        both = jnp.concatenate(split(held_ref[part * k : part * (k + 1), :]), axis=0)
        picked = [dot(both[:, step * i :], place) for i, place in enumerate(places)]
        picked = jnp.concatenate(picked, axis=1)
        picked = picked[:part] + picked[part:]
        for i in range(FULL):
            at = rows * i + part * k
            out_ref[at : at + part, :] = picked[:, LANES * i : LANES * (i + 1)]
        at = rows * FULL + part * (k % (parts // 2))
        if k < parts // 2:
            out_ref[at : at + part, : LANES // 2] = picked[:, FULL * LANES : CAP]
        else:
            out_ref[at : at + part, LANES // 2 :] = picked[:, CAP:]


def block_term(block_ref, uh, ul, rows):
    parts = [block_ref[rows * i : rows * (i + 1), :] for i in range(FULL)]
    tail = block_ref[rows * FULL : rows * FULL + rows // 2, :]
    parts.append(jnp.concatenate([tail, pltpu.roll(tail, LANES // 2, 1)], axis=0))
    halves = [split(p) for p in parts]
    highs, lows = [h for h, _ in halves], [l for _, l in halves]
    left = jnp.concatenate(highs + highs + lows, axis=1)
    return dot(left, jnp.concatenate([uh, ul, uh], axis=0))


def place_rows(us_ref, u, owner):
    m, w = u.shape
    nc = (us_ref.shape[1] - CAP - 8) // m
    if w % LANES:
        u = jnp.concatenate([u, jnp.zeros((m, LANES - w % LANES), jnp.float32)], axis=1)
    for i in range(us_ref.shape[0]):
        us_ref[i, pl.ds(owner, m, stride=nc), :] = u[:, LANES * i : LANES * (i + 1)]


def rows_of(us_ref, names, owner, width, lane_blocks):
    start = count(names < owner * width)
    base = pl.multiple_of((start // 8) * 8, 8)
    size = CAP + 8
    lanes = [pltpu.roll(us_ref[k, pl.ds(base, size), :], size - (start - base), 0)[:CAP] for k in lane_blocks]
    return jnp.concatenate(lanes, axis=1)


def cut(us_ref, names, owner, width, w):
    u = rows_of(us_ref, names, owner, width, range(us_ref.shape[0]))[:, :w]
    return split(jnp.concatenate([u, jnp.zeros((WIDE - CAP, w), jnp.float32)], axis=0))


def place_kernel(direct, nc, *refs):
    u_refs, us_ref = refs[:-1], refs[-1]
    end = us_ref.shape[1] - CAP - 8
    us_ref[:, end:, :] = jnp.zeros((us_ref.shape[0], CAP + 8, LANES), jnp.float32)
    if direct:
        for owner, u_ref in zip(ring_owners(nc, lax.axis_index("pcol")), u_refs):
            place_rows(us_ref, u_ref[...], owner)
    else:
        pl.loop(0, nc)(lambda k: place_rows(us_ref, u_refs[0][k], k))


def last_kernel(nc, width, structure_ref, before_ref, *refs):
    us_ref, own_ref = refs[-2:]
    c = lax.axis_index("pcol")
    us_ref[...] = before_ref[...]
    if len(refs) > 2:
        place_rows(us_ref, refs[0][...], ring_owners(nc, c)[-1])
    names = structure_ref[...].reshape(1, -1)
    w = own_ref.shape[1]
    own_ref[...] = rows_of(us_ref, names, c // 2, width, [c & 1] if len(refs) > 2 else [0])[:, :w]


def row_order(names, c, rows, nc, slots, direct):
    n = names.shape[1]
    z = c // 2
    lg = log2(nc)
    row = c * rows + lax.broadcasted_iota(jnp.int32, (rows, n), 0)
    rank = jnp.sum(one_hot(names < row), axis=1, keepdims=True).astype(jnp.int32)
    member = jnp.sum(one_hot(names == row), axis=1, keepdims=True)
    turn = rank & (nc - 1)
    ahead = (count(names < c * rows) - turn + nc - 1) >> lg
    block = turn >> 1
    if direct:
        block = block ^ z
    block = 2 * block + (turn & 1)
    slot = jnp.where(member > 0.5, block * slots + (rank >> lg) - ahead, -1)
    at = lax.broadcasted_iota(jnp.int32, (rows, nc * slots), 1)
    return one_hot(at == slot).T.astype(BF16)


def order_kernel(direct, slots, structure_ref, to_ref, place_ref, from_ref):
    nc = to_ref.shape[0] // slots
    rows = to_ref.shape[1]
    nz = nc // 2
    lg = log2(nc)
    names = structure_ref[...].reshape(1, -1)
    n = names.shape[1]
    m = n // nc
    c = lax.axis_index("pcol")
    z, x = c // 2, c & 1
    to_ref[...] = row_order(names, c, rows, nc, slots, direct)

    start, middle = count(names < 2 * z * rows), count(names < (2 * z + 1) * rows)
    named = pltpu.roll(jnp.broadcast_to(names, (8, n)), lax.rem(n - start, n), 1)[:1, :CAP]
    index = start + lax.broadcasted_iota(jnp.int32, (1, CAP), 1)
    half = jnp.where(named >= (2 * z + 1) * rows, 1, 0)
    turn = index & (nc - 1)
    ahead = (jnp.where(half == 1, middle, start) - turn + nc - 1) >> lg
    block = turn >> 1
    if direct:
        block = block ^ z
    slot = (2 * block + (turn & 1)) * slots + (index >> lg) - ahead + (half ^ x) * rows
    slot = jnp.where((named >= 2 * z * rows) & (named < (2 * z + 2) * rows), slot, -1)
    at = lax.broadcasted_iota(jnp.int32, (2 * rows, CAP), 0)
    place_ref[...] = one_hot(at == slot).T.astype(BF16)

    own = lax.broadcasted_iota(jnp.int32, (m, n), 1) - nc * lax.broadcasted_iota(jnp.int32, (m, n), 0)
    mine = jnp.sum(jnp.where(own == c, names, 0).astype(jnp.float32), axis=1, keepdims=True)
    source = jnp.zeros((m, 1), jnp.int32)
    before = jnp.zeros((m, 1), jnp.int32)
    for k in range(1, nc):
        less = mine < float(k * rows)
        source = source + jnp.where(less, 0, 1)
        before = jnp.where(less, before, count(less))
    block = source >> 1
    if direct:
        block = block ^ z
    block = block + nz * ((source ^ c) & 1)
    slot = block * slots + lax.broadcasted_iota(jnp.int32, (m, 1), 0) - before
    at = lax.broadcasted_iota(jnp.int32, (m, rows), 1)
    from_ref[...] = one_hot(at == slot).astype(BF16)


def near_kernel(owners, rest, structure_ref, us_ref, *refs):
    block_refs, (image_ref, uh_ref, ul_ref) = refs[:-3], refs[-3:]
    rows, w = image_ref.shape
    width = rows * 2
    names = structure_ref[...].reshape(1, -1)
    r = lax.axis_index("prow")
    image = jnp.zeros((rows, w), jnp.float32)
    for owner, block_ref in zip(owners(r), block_refs):
        image = image + block_term(block_ref, *cut(us_ref, names, owner, width, w), rows)
    image_ref[...] = image
    if rest is None:

        @pl.loop(0, uh_ref.shape[0])
        def _(k):
            uh_ref[k], ul_ref[k] = cut(us_ref, names, k, width, w)

    else:
        for k, owner in enumerate(rest(r)):
            uh_ref[k], ul_ref[k] = cut(us_ref, names, owner, width, w)


def far_terms(places, uh_ref, ul_ref, image, block_refs):
    rows = image.shape[0]
    for k, block_ref in zip(places, block_refs):
        image = image + block_term(block_ref, uh_ref[k], ul_ref[k], rows)
    return image


def far_kernel(uh_ref, ul_ref, part_ref, *refs):
    places = [0] + list(range(1, uh_ref.shape[0], 2))
    refs[-1][...] = far_terms(places, uh_ref, ul_ref, part_ref[...], refs[:-1])


def image_kernel(direct, uh_ref, ul_ref, part_ref, to_ref, *refs):
    n_in = (uh_ref.shape[0] - 1) // 2 if direct else 1
    block_refs, out_refs = refs[:n_in], refs[n_in:]
    n_out = len(out_refs)
    rows = part_ref.shape[0]
    image = part_ref[...]
    if direct:
        image = far_terms(range(2, uh_ref.shape[0], 2), uh_ref, ul_ref, image, block_refs)
    else:
        stack = block_refs[0]
        add = lambda b, v: v + block_term(stack.at[b], uh_ref[b], ul_ref[b], rows)
        image = lax.fori_loop(0, stack.shape[0], add, image)
    high, low = split(image)
    image = dot(to_ref[...], high) + dot(to_ref[...], low)
    out_refs[0][...] = image
    size = image.shape[0] // n_out
    for k in range(1, n_out):
        out_refs[k][...] = image[size * k : size * (k + 1)]


def turn_kernel(direct, owners, place_ref, *refs):
    high_ref, low_ref, held_ref = refs[-3:]
    nz, wd, size = high_ref.shape
    z = lax.axis_index("pcol") // 2

    def put(owner, u_ref):
        where = (owner ^ z) if direct else owner
        high, low = split(u_ref[...].T)
        held_ref[pl.ds(pl.multiple_of(where * wd, wd), wd), :] = high
        held_ref[pl.ds(pl.multiple_of((where + nz) * wd, wd), wd), :] = low

    each(refs[:-3], owners(lax.axis_index("prow")) if direct else None, put)
    turned = dot(held_ref[...], place_ref[...]).astype(BF16).reshape(2, nz, wd, size)
    high_ref[...] = turned[0]
    low_ref[...] = turned[1]


def correction_kernel(high_ref, low_ref, mine_ref, other_ref, *out_refs):
    sh, sl = split(jnp.concatenate([mine_ref[...], other_ref[...]], axis=0))

    def term(t):
        return dot(high_ref[t], sh) + (dot(high_ref[t], sl) + dot(low_ref[t], sh))

    if len(out_refs) > 1:
        for t, out_ref in enumerate(out_refs):
            out_ref[...] = term(t)
    else:

        @pl.loop(0, out_refs[0].shape[0])
        def _(t):
            out_refs[0][t] = term(t)


def sum_kernel(*refs):
    total = refs[0][...]
    for ref in refs[1:-1]:
        total = total + ref[...]
    refs[-1][...] = total


def part_kernel(slots, *refs):
    mine_ref, theirs_ref = refs[-2:]
    first = (lax.axis_index("pcol") & 1) == 0
    blocks = mine_ref.shape[0] // slots
    mine, theirs = [], []
    for ref in refs[:-2]:
        for k in range(blocks // len(refs[:-2])):
            low = ref[2 * slots * k : 2 * slots * k + slots, :]
            high = ref[2 * slots * k + slots : 2 * slots * (k + 1), :]
            mine.append(jnp.where(first, low, high))
            theirs.append(jnp.where(first, high, low))
    mine_ref[...] = jnp.concatenate(mine, axis=0)
    theirs_ref[...] = jnp.concatenate(theirs, axis=0)


def last_sum_kernel(from_ref, mine_ref, other_ref, d_ref, total_ref, got_ref, sj_ref, jj_ref):
    sj_ref[...] = -pick_rows(from_ref[...], jnp.concatenate([mine_ref[...], other_ref[...]], axis=0))
    jj_ref[...] = d_ref[...] + (total_ref[...] + got_ref[...])


def call(kernel, out_shape, *args, flops=0, vmem=20, **kw):
    many = isinstance(out_shape, (list, tuple))
    size = flops and sum(v.size * v.dtype.itemsize for v in jax.tree.leaves((out_shape, args)))
    kw = {"in_specs": [VMEM] * len(args)} | kw
    return pl.pallas_call(
        kernel,
        out_shape=out_shape,
        out_specs=[VMEM] * len(out_shape) if many else VMEM,
        cost_estimate=pl.CostEstimate(flops=flops, bytes_accessed=size, transcendentals=0),
        compiler_params=pltpu.CompilerParams(vmem_limit_bytes=vmem * 2**20),
        **kw,
    )(*args)


def swap(v, axis, size):
    return lax.ppermute(v, axis, [(k, k ^ 1) for k in range(size)])


def spread(v, size, after):
    blocks = [v, swap(v, "prow", size)]
    v, _ = lax.optimization_barrier((v, after))
    for t in range(1, size // 2):
        for flip in range(2):
            blocks.append(lax.ppermute(v, "prow", [(k, ((k + 2 * t) % size) ^ flip) for k in range(size)]))
    return blocks


def relative_owners(size, r):
    out = []
    for t in range(size // 2):
        owner = (r - 2 * t) & (size - 1)
        out += [owner, owner ^ 1]
    return out


def ring_gather(u, nc, aside):
    ring = [2 * z for z in range(nc // 2)] + [2 * z + 1 for z in reversed(range(nc // 2))]
    pairs = [(ring[q - 1], ring[q]) for q in range(nc)]
    back = [(b, a) for a, b in pairs]
    blocks = [u]
    up = down = u
    for step in range(1, nc // 2):
        up, down = lax.ppermute(up, "pcol", pairs), lax.ppermute(down, "pcol", back)
        if step == 1:
            up, down = lax.optimization_barrier((up, down))
        blocks += [up, down]
    last, aside = lax.optimization_barrier((lax.ppermute(up, "pcol", pairs), aside))
    return blocks + [last], aside


def ring_owners(nc, c):
    q = jnp.where((c & 1) == 0, c >> 1, nc - 1 - (c >> 1))
    out = []
    for k in range(nc):
        step = (k + 1) // 2
        at = (q - step if k % 2 else q + step) & (nc - 1)
        out.append(jnp.where(at < nc // 2, 2 * at, 2 * (nc - 1 - at) + 1))
    return out


def per_device(sigma_top, structure, u_panel, d_term):
    nc, nr = lax.axis_size("pcol"), lax.axis_size("prow")
    c = lax.axis_index("pcol")
    nz = nc // 2
    rows, cols = sigma_top.shape
    m, w = u_panel.shape
    wd = w // 2
    n = structure.shape[0]
    slots = -(-rows // nc)
    direct = (nr, nc) == (4, 8)
    names = structure
    groups = [[2 * k + x for k in range(nz)] for x in range(2)]
    owners = functools.partial(relative_owners, nr)

    chosen = call(
        select_kernel,
        f32(rows * CAP // LANES, LANES),
        names,
        sigma_top,
        in_specs=[VMEM, HBM],
        scratch_shapes=[pltpu.VMEM((rows, cols), jnp.float32), pltpu.SemaphoreType.DMA((2,))],
        flops=4 * rows * cols * WIDE,
        vmem=52,
    )
    to, place, source = call(
        functools.partial(order_kernel, direct, slots),
        [bf16(nc * slots, rows), bf16(CAP, 2 * nc * slots), bf16(m, nc * slots)],
        names,
    )
    if direct:
        u_all, to = ring_gather(u_panel, nc, to)
    else:
        u_all = [lax.all_gather(u_panel, "pcol")]
    term = 6 * rows * WIDE * w
    placed = f32(-(-w // LANES), n + CAP + 8, LANES)
    early, late = (u_all[:-1], u_all[-1:]) if direct else (u_all, [])
    before = call(functools.partial(place_kernel, direct, nc), placed, *early, flops=8 * term)
    us, own = call(
        functools.partial(last_kernel, nc, cols),
        [placed, f32(CAP, wd if direct else w)],
        names,
        before,
        *late,
        flops=term,
    )
    halves = bf16(nr - 1 if direct else nr, WIDE, w)
    near = [chosen] if direct else []
    image, uh, ul = call(
        functools.partial(near_kernel, lambda r: owners(r)[:1], (lambda r: owners(r)[1:]) if direct else None),
        [f32(rows, w), halves, halves],
        names,
        us,
        *near,
        flops=0,
    )
    if direct:
        beside, later = [swap(chosen, "prow", nr)], []
        for t in range(1, nr // 2):
            far = lax.ppermute(chosen, "prow", [(k, (k + 2 * t) % nr) for k in range(nr)])
            far, _ = lax.optimization_barrier((far, image))
            beside.append(far)
            later.append(swap(far, "prow", nr))
        image = call(far_kernel, f32(rows, w), uh, ul, image, *beside, flops=1 * term)
    else:
        later = [lax.all_gather(chosen, "prow")]
    if direct:
        owned = spread(own, nr, beside[1])
    sent = call(
        functools.partial(image_kernel, direct),
        [f32(nc * slots, w)] + [f32(2 * slots, w)] * ((nz - 1) * direct),
        uh,
        ul,
        image,
        to,
        *later,
        flops=term,
    )
    meet = lambda v, t: lax.ppermute(v, "pcol", [(k, k ^ (2 * t)) for k in range(nc)])
    whole = sent[0]
    other = swap(whole, "pcol", nc)
    if direct:
        got = [whole] + [meet(sent[t], t) for t in range(1, nz)]
    else:
        blocks = whole.reshape(nz, 2 * slots, w)
        blocks = lax.all_to_all(blocks, "pcol", split_axis=0, concat_axis=0, axis_index_groups=groups, tiled=True)
        got = [blocks.reshape(nc * slots, w)]
        own = jnp.where(jnp.bitwise_and(c, 1) == 0, own[:, :wd], own[:, wd:])
        owned = [lax.all_gather(own, "prow")]

    turned = bf16(nz, wd, 2 * nc * slots)
    high, low = call(
        functools.partial(turn_kernel, direct, owners),
        [turned, turned],
        place,
        *owned,
        scratch_shapes=[pltpu.VMEM((2 * nz * wd, CAP), BF16)],
        flops=8 * nz * wd * nc * slots * CAP,
    )
    parts = [f32(wd, w)] * nz if direct else [f32(nz, wd, w)]
    got, _ = lax.optimization_barrier((got, high))
    mine, theirs = call(functools.partial(part_kernel, slots), [f32(nz * slots, w)] * 2, *got, flops=2 * term)
    other, _ = lax.optimization_barrier((other, mine))
    terms = call(correction_kernel, parts, high, low, whole, other, flops=term)
    theirs, _ = lax.optimization_barrier((theirs, terms[0]))
    theirs = swap(theirs, "pcol", nc)
    if direct:
        some = [meet(terms[t], t) for t in range(1, nz - 1)]
        total = call(sum_kernel, f32(wd, w), terms[0], *some, flops=4 * term)
        rest = meet(terms[nz - 1], nz - 1)
    else:
        terms = lax.all_to_all(terms[0], "pcol", split_axis=0, concat_axis=0, axis_index_groups=groups, tiled=True)
        total, rest = jnp.sum(terms[1:], axis=0), terms[0]
    outs = [f32(m, w), f32(wd, w)]
    return tuple(call(last_sum_kernel, outs, source, mine, theirs, d_term, total, rest, flops=term // 4))


def solution(mesh):
    placed = (P("pcol", "prow"), P(), P("pcol", "prow"), P("pcol", "prow"))
    return jax.shard_map(
        per_device,
        mesh=mesh,
        in_specs=placed,
        out_specs=(P("pcol", "prow"), P("pcol", "prow")),
        check_vma=False,
    )
```

```python
import functools

import jax
import jax.numpy as jnp
from jax import lax
from jax.experimental import pallas as pl
from jax.experimental.pallas import tpu as pltpu
from jax.sharding import PartitionSpec as P

LANES = 128
BLOCK_CAP = 560
CAP = -(-BLOCK_CAP // 64) * 64
FULL = CAP // LANES
WIDE = (FULL + 1) * LANES
BF16 = jnp.bfloat16
VMEM = pl.BlockSpec(memory_space=pltpu.VMEM)
HBM = pl.BlockSpec(memory_space=pltpu.HBM)


def f32(*shape):
    return jax.ShapeDtypeStruct(shape, jnp.float32)


def bf16(*shape):
    return jax.ShapeDtypeStruct(shape, BF16)


def split(v):
    high = v.astype(BF16)
    return high, (v - high.astype(jnp.float32)).astype(BF16)


def split3(v):
    high = v.astype(BF16)
    mid, low = split(v - high.astype(jnp.float32))
    return high, mid, low


def dot(a, b):
    return jnp.dot(a, b, preferred_element_type=jnp.float32)


def pick_rows(place, v):
    high, mid, low = split3(v)
    return dot(place, high) + (dot(place, mid) + dot(place, low))


def one_hot(mask):
    return jnp.where(mask, 1.0, 0.0)


def count(mask):
    return jnp.sum(jnp.where(mask, 1.0, 0.0)).astype(jnp.int32)


def log2(size):
    return size.bit_length() - 1


def each(refs, owners, fn):
    if owners is None:
        pl.loop(0, refs[0].shape[0])(lambda i: fn(i, refs[0].at[i]))
    else:
        for owner, ref in zip(owners, refs):
            fn(owner, ref)


def select_kernel(structure_ref, sigma_ref, out_ref, held_ref, sems):
    rows, cols = held_ref.shape
    n = structure_ref.shape[0]
    parts = sems.shape[0]
    part = rows // parts
    copies = []
    for k in range(parts):
        at = pl.ds(part * k, part)
        copies.append(pltpu.make_async_copy(sigma_ref.at[at, :], held_ref.at[at, :], sems.at[k]))
        copies[-1].start()
    first = lax.axis_index("prow") * cols
    listed = structure_ref[...].reshape(1, -1)
    names = jnp.broadcast_to(listed, (8, n))
    shift = lax.rem(n - count(listed < first), n)
    named = pltpu.roll(names, shift, 1)[:1, :CAP] - first
    named = jnp.concatenate([named, named[:, FULL * LANES :]], axis=1)
    step = 2 * LANES
    places = []
    for k in range(0, WIDE, step):
        at = lax.broadcasted_iota(jnp.int32, (cols - k, min(step, WIDE - k)), 0) + k
        places.append(one_hot(at == named[:, k : k + step]).astype(BF16))
    for k in range(parts):
        copies[k].wait()
        both = jnp.concatenate(split(held_ref[part * k : part * (k + 1), :]), axis=0)
        picked = [dot(both[:, step * i :], place) for i, place in enumerate(places)]
        picked = jnp.concatenate(picked, axis=1)
        picked = picked[:part] + picked[part:]
        for i in range(FULL):
            at = rows * i + part * k
            out_ref[at : at + part, :] = picked[:, LANES * i : LANES * (i + 1)]
        at = rows * FULL + part * (k % (parts // 2))
        if k < parts // 2:
            out_ref[at : at + part, : LANES // 2] = picked[:, FULL * LANES : CAP]
        else:
            out_ref[at : at + part, LANES // 2 :] = picked[:, CAP:]


def block_term(block_ref, uh, ul, rows):
    parts = [block_ref[rows * i : rows * (i + 1), :] for i in range(FULL)]
    tail = block_ref[rows * FULL : rows * FULL + rows // 2, :]
    parts.append(jnp.concatenate([tail, pltpu.roll(tail, LANES // 2, 1)], axis=0))
    halves = [split(p) for p in parts]
    highs, lows = [h for h, _ in halves], [l for _, l in halves]
    left = jnp.concatenate(highs + highs + lows, axis=1)
    return dot(left, jnp.concatenate([uh, ul, uh], axis=0))


def place_rows(us_ref, u, owner):
    m, w = u.shape
    nc = (us_ref.shape[1] - CAP - 8) // m
    if w % LANES:
        u = jnp.concatenate([u, jnp.zeros((m, LANES - w % LANES), jnp.float32)], axis=1)
    for i in range(us_ref.shape[0]):
        us_ref[i, pl.ds(owner, m, stride=nc), :] = u[:, LANES * i : LANES * (i + 1)]


def rows_of(us_ref, names, owner, width, lane_blocks):
    start = count(names < owner * width)
    base = pl.multiple_of((start // 8) * 8, 8)
    size = CAP + 8
    lanes = [pltpu.roll(us_ref[k, pl.ds(base, size), :], size - (start - base), 0)[:CAP] for k in lane_blocks]
    return jnp.concatenate(lanes, axis=1)


def cut(us_ref, names, owner, width, w):
    u = rows_of(us_ref, names, owner, width, range(us_ref.shape[0]))[:, :w]
    return split(jnp.concatenate([u, jnp.zeros((WIDE - CAP, w), jnp.float32)], axis=0))


def place_kernel(direct, nc, *refs):
    u_refs, us_ref = refs[:-1], refs[-1]
    end = us_ref.shape[1] - CAP - 8
    us_ref[:, end:, :] = jnp.zeros((us_ref.shape[0], CAP + 8, LANES), jnp.float32)
    if direct:
        for owner, u_ref in zip(ring_owners(nc, lax.axis_index("pcol")), u_refs):
            place_rows(us_ref, u_ref[...], owner)
    else:
        pl.loop(0, nc)(lambda k: place_rows(us_ref, u_refs[0][k], k))


def last_kernel(nc, width, structure_ref, before_ref, *refs):
    us_ref, own_ref = refs[-2:]
    c = lax.axis_index("pcol")
    us_ref[...] = before_ref[...]
    if len(refs) > 2:
        place_rows(us_ref, refs[0][...], ring_owners(nc, c)[-1])
    names = structure_ref[...].reshape(1, -1)
    w = own_ref.shape[1]
    own_ref[...] = rows_of(us_ref, names, c // 2, width, [c & 1] if len(refs) > 2 else range(us_ref.shape[0]))[:, :w]


def row_order(names, c, rows, nc, slots, direct):
    n = names.shape[1]
    z = c // 2
    lg = log2(nc)
    row = c * rows + lax.broadcasted_iota(jnp.int32, (rows, n), 0)
    rank = jnp.sum(one_hot(names < row), axis=1, keepdims=True).astype(jnp.int32)
    member = jnp.sum(one_hot(names == row), axis=1, keepdims=True)
    turn = rank & (nc - 1)
    ahead = (count(names < c * rows) - turn + nc - 1) >> lg
    block = turn >> 1
    if direct:
        block = block ^ z
    block = 2 * block + (turn & 1)
    slot = jnp.where(member > 0.5, block * slots + (rank >> lg) - ahead, -1)
    at = lax.broadcasted_iota(jnp.int32, (rows, nc * slots), 1)
    return one_hot(at == slot).T.astype(BF16)


def order_kernel(direct, slots, structure_ref, to_ref, place_ref, from_ref):
    nc = to_ref.shape[0] // slots
    rows = to_ref.shape[1]
    nz = nc // 2
    lg = log2(nc)
    names = structure_ref[...].reshape(1, -1)
    n = names.shape[1]
    m = n // nc
    c = lax.axis_index("pcol")
    z, x = c // 2, c & 1
    to_ref[...] = row_order(names, c, rows, nc, slots, direct)

    start, middle = count(names < 2 * z * rows), count(names < (2 * z + 1) * rows)
    named = pltpu.roll(jnp.broadcast_to(names, (8, n)), lax.rem(n - start, n), 1)[:1, :CAP]
    index = start + lax.broadcasted_iota(jnp.int32, (1, CAP), 1)
    half = jnp.where(named >= (2 * z + 1) * rows, 1, 0)
    turn = index & (nc - 1)
    ahead = (jnp.where(half == 1, middle, start) - turn + nc - 1) >> lg
    block = turn >> 1
    if direct:
        block = block ^ z
    slot = (2 * block + (turn & 1)) * slots + (index >> lg) - ahead + (half ^ x) * rows
    slot = jnp.where((named >= 2 * z * rows) & (named < (2 * z + 2) * rows), slot, -1)
    at = lax.broadcasted_iota(jnp.int32, (2 * rows, CAP), 0)
    place_ref[...] = one_hot(at == slot).T.astype(BF16)

    own = lax.broadcasted_iota(jnp.int32, (m, n), 1) - nc * lax.broadcasted_iota(jnp.int32, (m, n), 0)
    mine = jnp.sum(jnp.where(own == c, names, 0).astype(jnp.float32), axis=1, keepdims=True)
    source = jnp.zeros((m, 1), jnp.int32)
    before = jnp.zeros((m, 1), jnp.int32)
    for k in range(1, nc):
        less = mine < float(k * rows)
        source = source + jnp.where(less, 0, 1)
        before = jnp.where(less, before, count(less))
    block = source >> 1
    if direct:
        block = block ^ z
    block = block + nz * ((source ^ c) & 1)
    slot = block * slots + lax.broadcasted_iota(jnp.int32, (m, 1), 0) - before
    at = lax.broadcasted_iota(jnp.int32, (m, rows), 1)
    from_ref[...] = one_hot(at == slot).astype(BF16)


def near_kernel(owners, rest, structure_ref, us_ref, *refs):
    block_refs, (image_ref, uh_ref, ul_ref) = refs[:-3], refs[-3:]
    rows, w = image_ref.shape
    width = rows * 2
    names = structure_ref[...].reshape(1, -1)
    r = lax.axis_index("prow")
    image = jnp.zeros((rows, w), jnp.float32)
    for owner, block_ref in zip(owners(r), block_refs):
        image = image + block_term(block_ref, *cut(us_ref, names, owner, width, w), rows)
    image_ref[...] = image
    if rest is None:

        @pl.loop(0, uh_ref.shape[0])
        def _(k):
            uh_ref[k], ul_ref[k] = cut(us_ref, names, k, width, w)

    else:
        for k, owner in enumerate(rest(r)):
            uh_ref[k], ul_ref[k] = cut(us_ref, names, owner, width, w)


def far_terms(places, uh_ref, ul_ref, image, block_refs):
    rows = image.shape[0]
    for k, block_ref in zip(places, block_refs):
        image = image + block_term(block_ref, uh_ref[k], ul_ref[k], rows)
    return image


def far_kernel(uh_ref, ul_ref, part_ref, *refs):
    places = [0] + list(range(1, uh_ref.shape[0], 2))
    refs[-1][...] = far_terms(places, uh_ref, ul_ref, part_ref[...], refs[:-1])


def image_kernel(direct, uh_ref, ul_ref, part_ref, to_ref, *refs):
    n_in = (uh_ref.shape[0] - 1) // 2 if direct else 1
    block_refs, out_refs = refs[:n_in], refs[n_in:]
    n_out = len(out_refs)
    rows = part_ref.shape[0]
    image = part_ref[...]
    if direct:
        image = far_terms(range(2, uh_ref.shape[0], 2), uh_ref, ul_ref, image, block_refs)
    else:
        stack = block_refs[0]
        add = lambda b, v: v + block_term(stack.at[b], uh_ref[b], ul_ref[b], rows)
        image = lax.fori_loop(0, stack.shape[0], add, image)
    high, low = split(image)
    image = dot(to_ref[...], high) + dot(to_ref[...], low)
    out_refs[0][...] = image
    size = image.shape[0] // n_out
    for k in range(1, n_out):
        out_refs[k][...] = image[size * k : size * (k + 1)]


def turn_kernel(direct, owners, place_ref, *refs):
    high_ref, low_ref, held_ref = refs[-3:]
    nz, wd, size = high_ref.shape
    z = lax.axis_index("pcol") // 2

    def put(owner, u_ref):
        where = (owner ^ z) if direct else owner
        high, low = split(u_ref[...].T)
        held_ref[pl.ds(pl.multiple_of(where * wd, wd), wd), :] = high
        held_ref[pl.ds(pl.multiple_of((where + nz) * wd, wd), wd), :] = low

    each(refs[:-3], owners(lax.axis_index("prow")) if direct else None, put)
    turned = dot(held_ref[...], place_ref[...]).astype(BF16).reshape(2, nz, wd, size)
    high_ref[...] = turned[0]
    low_ref[...] = turned[1]


def correction_kernel(high_ref, low_ref, mine_ref, other_ref, *out_refs):
    sh, sl = split(jnp.concatenate([mine_ref[...], other_ref[...]], axis=0))

    def term(t):
        return dot(high_ref[t], sh) + (dot(high_ref[t], sl) + dot(low_ref[t], sh))

    if len(out_refs) > 1:
        for t, out_ref in enumerate(out_refs):
            out_ref[...] = term(t)
    else:

        @pl.loop(0, out_refs[0].shape[0])
        def _(t):
            out_refs[0][t] = term(t)


def sum_kernel(*refs):
    total = refs[0][...]
    for ref in refs[1:-1]:
        total = total + ref[...]
    refs[-1][...] = total


def part_kernel(slots, *refs):
    mine_ref, theirs_ref = refs[-2:]
    first = (lax.axis_index("pcol") & 1) == 0
    blocks = mine_ref.shape[0] // slots
    mine, theirs = [], []
    for ref in refs[:-2]:
        for k in range(blocks // len(refs[:-2])):
            low = ref[2 * slots * k : 2 * slots * k + slots, :]
            high = ref[2 * slots * k + slots : 2 * slots * (k + 1), :]
            mine.append(jnp.where(first, low, high))
            theirs.append(jnp.where(first, high, low))
    mine_ref[...] = jnp.concatenate(mine, axis=0)
    theirs_ref[...] = jnp.concatenate(theirs, axis=0)


def last_sum_kernel(from_ref, mine_ref, other_ref, d_ref, total_ref, got_ref, sj_ref, jj_ref):
    sj_ref[...] = -pick_rows(from_ref[...], jnp.concatenate([mine_ref[...], other_ref[...]], axis=0))
    jj_ref[...] = d_ref[...] + (total_ref[...] + got_ref[...])


def call(kernel, out_shape, *args, flops=0, vmem=20, **kw):
    many = isinstance(out_shape, (list, tuple))
    size = flops and sum(v.size * v.dtype.itemsize for v in jax.tree.leaves((out_shape, args)))
    kw = {"in_specs": [VMEM] * len(args)} | kw
    return pl.pallas_call(
        kernel,
        out_shape=out_shape,
        out_specs=[VMEM] * len(out_shape) if many else VMEM,
        cost_estimate=pl.CostEstimate(flops=flops, bytes_accessed=size, transcendentals=0),
        compiler_params=pltpu.CompilerParams(vmem_limit_bytes=vmem * 2**20),
        **kw,
    )(*args)


def swap(v, axis, size):
    return lax.ppermute(v, axis, [(k, k ^ 1) for k in range(size)])


def spread(v, size, after):
    blocks = [v, swap(v, "prow", size)]
    v, _ = lax.optimization_barrier((v, after))
    for t in range(1, size // 2):
        for flip in range(2):
            blocks.append(lax.ppermute(v, "prow", [(k, ((k + 2 * t) % size) ^ flip) for k in range(size)]))
    return blocks


def relative_owners(size, r):
    out = []
    for t in range(size // 2):
        owner = (r - 2 * t) & (size - 1)
        out += [owner, owner ^ 1]
    return out


def ring_gather(u, nc, aside):
    ring = [2 * z for z in range(nc // 2)] + [2 * z + 1 for z in reversed(range(nc // 2))]
    pairs = [(ring[q - 1], ring[q]) for q in range(nc)]
    back = [(b, a) for a, b in pairs]
    blocks = [u]
    up = down = u
    for step in range(1, nc // 2):
        up, down = lax.ppermute(up, "pcol", pairs), lax.ppermute(down, "pcol", back)
        if step == 1:
            up, down = lax.optimization_barrier((up, down))
        blocks += [up, down]
    last, aside = lax.optimization_barrier((lax.ppermute(up, "pcol", pairs), aside))
    return blocks + [last], aside


def ring_owners(nc, c):
    q = jnp.where((c & 1) == 0, c >> 1, nc - 1 - (c >> 1))
    out = []
    for k in range(nc):
        step = (k + 1) // 2
        at = (q - step if k % 2 else q + step) & (nc - 1)
        out.append(jnp.where(at < nc // 2, 2 * at, 2 * (nc - 1 - at) + 1))
    return out


def per_device(sigma_top, structure, u_panel, d_term):
    nc, nr = lax.axis_size("pcol"), lax.axis_size("prow")
    c = lax.axis_index("pcol")
    nz = nc // 2
    rows, cols = sigma_top.shape
    m, w = u_panel.shape
    wd = w // 2
    n = structure.shape[0]
    slots = -(-rows // nc)
    direct = (nr, nc) == (4, 8)
    names = structure
    groups = [[2 * k + x for k in range(nz)] for x in range(2)]
    owners = functools.partial(relative_owners, nr)

    chosen = call(
        select_kernel,
        f32(rows * CAP // LANES, LANES),
        names,
        sigma_top,
        in_specs=[VMEM, HBM],
        scratch_shapes=[pltpu.VMEM((rows, cols), jnp.float32), pltpu.SemaphoreType.DMA((2,))],
        flops=4 * rows * cols * WIDE,
        vmem=52,
    )
    to, place, source = call(
        functools.partial(order_kernel, direct, slots),
        [bf16(nc * slots, rows), bf16(CAP, 2 * nc * slots), bf16(m, nc * slots)],
        names,
    )
    if direct:
        u_all, to = ring_gather(u_panel, nc, to)
    else:
        u_all = [lax.all_gather(u_panel, "pcol")]
    term = 6 * rows * WIDE * w
    placed = f32(-(-w // LANES), n + CAP + 8, LANES)
    early, late = (u_all[:-1], u_all[-1:]) if direct else (u_all, [])
    before = call(functools.partial(place_kernel, direct, nc), placed, *early, flops=8 * term)
    us, own = call(
        functools.partial(last_kernel, nc, cols),
        [placed, f32(CAP, wd if direct else w)],
        names,
        before,
        *late,
        flops=term,
    )
    halves = bf16(nr - 1 if direct else nr, WIDE, w)
    near = [chosen] if direct else []
    image, uh, ul = call(
        functools.partial(near_kernel, lambda r: owners(r)[:1], (lambda r: owners(r)[1:]) if direct else None),
        [f32(rows, w), halves, halves],
        names,
        us,
        *near,
        flops=0,
    )
    if direct:
        beside, later = [swap(chosen, "prow", nr)], []
        for t in range(1, nr // 2):
            far = lax.ppermute(chosen, "prow", [(k, (k + 2 * t) % nr) for k in range(nr)])
            far, _ = lax.optimization_barrier((far, image))
            beside.append(far)
            later.append(swap(far, "prow", nr))
        image = call(far_kernel, f32(rows, w), uh, ul, image, *beside, flops=1 * term)
    else:
        later = [lax.all_gather(chosen, "prow")]
    if direct:
        owned = spread(own, nr, beside[1])
    sent = call(
        functools.partial(image_kernel, direct),
        [f32(nc * slots, w)] + [f32(2 * slots, w)] * ((nz - 1) * direct),
        uh,
        ul,
        image,
        to,
        *later,
        flops=term,
    )
    meet = lambda v, t: lax.ppermute(v, "pcol", [(k, k ^ (2 * t)) for k in range(nc)])
    whole = sent[0]
    other = swap(whole, "pcol", nc)
    if direct:
        got = [whole] + [meet(sent[t], t) for t in range(1, nz)]
    else:
        blocks = whole.reshape(nz, 2 * slots, w)
        blocks = lax.all_to_all(blocks, "pcol", split_axis=0, concat_axis=0, axis_index_groups=groups, tiled=True)
        got = [blocks.reshape(nc * slots, w)]
        own = jnp.where(jnp.bitwise_and(c, 1) == 0, own[:, :wd], own[:, wd:])
        owned = [lax.all_gather(own, "prow")]

    turned = bf16(nz, wd, 2 * nc * slots)
    high, low = call(
        functools.partial(turn_kernel, direct, owners),
        [turned, turned],
        place,
        *owned,
        scratch_shapes=[pltpu.VMEM((2 * nz * wd, CAP), BF16)],
        flops=8 * nz * wd * nc * slots * CAP,
    )
    parts = [f32(wd, w)] * nz if direct else [f32(nz, wd, w)]
    got, _ = lax.optimization_barrier((got, high))
    mine, theirs = call(functools.partial(part_kernel, slots), [f32(nz * slots, w)] * 2, *got, flops=2 * term)
    other, _ = lax.optimization_barrier((other, mine))
    terms = call(correction_kernel, parts, high, low, whole, other, flops=term)
    theirs, _ = lax.optimization_barrier((theirs, terms[0]))
    theirs = swap(theirs, "pcol", nc)
    if direct:
        far = [meet(terms[t], t) for t in reversed(range(2, nz))]
        total = call(sum_kernel, f32(wd, w), terms[0], *far, flops=4 * term)
        rest = meet(terms[1], 1)
    else:
        terms = lax.all_to_all(terms[0], "pcol", split_axis=0, concat_axis=0, axis_index_groups=groups, tiled=True)
        total, rest = jnp.sum(terms[1:], axis=0), terms[0]
    outs = [f32(m, w), f32(wd, w)]
    return tuple(call(last_sum_kernel, outs, source, mine, theirs, d_term, total, rest, flops=term // 4))


def solution(mesh):
    placed = (P("pcol", "prow"), P(), P("pcol", "prow"), P("pcol", "prow"))
    return jax.shard_map(
        per_device,
        mesh=mesh,
        in_specs=placed,
        out_specs=(P("pcol", "prow"), P("pcol", "prow")),
        check_vma=False,
    )
```

```python
import functools

import jax
import jax.numpy as jnp
from jax import lax
from jax.experimental import pallas as pl
from jax.experimental.pallas import tpu as pltpu
from jax.sharding import PartitionSpec as P

LANES = 128
BLOCK_CAP = 560
CAP = -(-BLOCK_CAP // 64) * 64
FULL = CAP // LANES
WIDE = (FULL + 1) * LANES
BF16 = jnp.bfloat16
VMEM = pl.BlockSpec(memory_space=pltpu.VMEM)
HBM = pl.BlockSpec(memory_space=pltpu.HBM)


def f32(*shape):
    return jax.ShapeDtypeStruct(shape, jnp.float32)


def bf16(*shape):
    return jax.ShapeDtypeStruct(shape, BF16)


def split(v):
    high = v.astype(BF16)
    return high, (v - high.astype(jnp.float32)).astype(BF16)


def split3(v):
    high = v.astype(BF16)
    mid, low = split(v - high.astype(jnp.float32))
    return high, mid, low


def dot(a, b):
    return jnp.dot(a, b, preferred_element_type=jnp.float32)


def pick_rows(place, v):
    high, low = split(v)
    return dot(place, high) + dot(place, low)


def one_hot(mask):
    return jnp.where(mask, 1.0, 0.0)


def count(mask):
    return jnp.sum(jnp.where(mask, 1.0, 0.0)).astype(jnp.int32)


def log2(size):
    return size.bit_length() - 1


def each(refs, owners, fn):
    if owners is None:
        pl.loop(0, refs[0].shape[0])(lambda i: fn(i, refs[0].at[i]))
    else:
        for owner, ref in zip(owners, refs):
            fn(owner, ref)


def select_kernel(structure_ref, sigma_ref, out_ref, held_ref, sems):
    rows, cols = held_ref.shape
    n = structure_ref.shape[0]
    parts = sems.shape[0]
    part = rows // parts
    copies = []
    for k in range(parts):
        at = pl.ds(part * k, part)
        copies.append(pltpu.make_async_copy(sigma_ref.at[at, :], held_ref.at[at, :], sems.at[k]))
        copies[-1].start()
    first = lax.axis_index("prow") * cols
    listed = structure_ref[...].reshape(1, -1)
    names = jnp.broadcast_to(listed, (8, n))
    shift = lax.rem(n - count(listed < first), n)
    named = pltpu.roll(names, shift, 1)[:1, :CAP] - first
    named = jnp.concatenate([named, named[:, FULL * LANES :]], axis=1)
    step = 2 * LANES
    places = []
    for k in range(0, WIDE, step):
        at = lax.broadcasted_iota(jnp.int32, (cols - k, min(step, WIDE - k)), 0) + k
        places.append(one_hot(at == named[:, k : k + step]).astype(BF16))
    for k in range(parts):
        copies[k].wait()
        both = jnp.concatenate(split(held_ref[part * k : part * (k + 1), :]), axis=0)
        picked = [dot(both[:, step * i :], place) for i, place in enumerate(places)]
        picked = jnp.concatenate(picked, axis=1)
        picked = picked[:part] + picked[part:]
        for i in range(FULL):
            at = rows * i + part * k
            out_ref[at : at + part, :] = picked[:, LANES * i : LANES * (i + 1)]
        at = rows * FULL + part * (k % (parts // 2))
        if k < parts // 2:
            out_ref[at : at + part, : LANES // 2] = picked[:, FULL * LANES : CAP]
        else:
            out_ref[at : at + part, LANES // 2 :] = picked[:, CAP:]


def block_term(block_ref, uh, ul, rows):
    parts = [block_ref[rows * i : rows * (i + 1), :] for i in range(FULL)]
    tail = block_ref[rows * FULL : rows * FULL + rows // 2, :]
    parts.append(jnp.concatenate([tail, pltpu.roll(tail, LANES // 2, 1)], axis=0))
    halves = [split(p) for p in parts]
    highs, lows = [h for h, _ in halves], [l for _, l in halves]
    left = jnp.concatenate(highs + highs + lows, axis=1)
    return dot(left, jnp.concatenate([uh, ul, uh], axis=0))


def place_rows(us_ref, u, owner):
    m, w = u.shape
    nc = (us_ref.shape[1] - CAP - 8) // m
    if w % LANES:
        u = jnp.concatenate([u, jnp.zeros((m, LANES - w % LANES), jnp.float32)], axis=1)
    for i in range(us_ref.shape[0]):
        us_ref[i, pl.ds(owner, m, stride=nc), :] = u[:, LANES * i : LANES * (i + 1)]


def rows_of(us_ref, names, owner, width, lane_blocks):
    start = count(names < owner * width)
    base = pl.multiple_of((start // 8) * 8, 8)
    size = CAP + 8
    lanes = [pltpu.roll(us_ref[k, pl.ds(base, size), :], size - (start - base), 0)[:CAP] for k in lane_blocks]
    return jnp.concatenate(lanes, axis=1)


def cut(us_ref, names, owner, width, w):
    u = rows_of(us_ref, names, owner, width, range(us_ref.shape[0]))[:, :w]
    return split(jnp.concatenate([u, jnp.zeros((WIDE - CAP, w), jnp.float32)], axis=0))


def place_kernel(direct, nc, *refs):
    u_refs, us_ref = refs[:-1], refs[-1]
    end = us_ref.shape[1] - CAP - 8
    us_ref[:, end:, :] = jnp.zeros((us_ref.shape[0], CAP + 8, LANES), jnp.float32)
    if direct:
        for owner, u_ref in zip(ring_owners(nc, lax.axis_index("pcol")), u_refs):
            place_rows(us_ref, u_ref[...], owner)
    else:
        pl.loop(0, nc)(lambda k: place_rows(us_ref, u_refs[0][k], k))


def last_kernel(nc, width, structure_ref, before_ref, *refs):
    us_ref, own_ref = refs[-2:]
    c = lax.axis_index("pcol")
    us_ref[...] = before_ref[...]
    if len(refs) > 2:
        place_rows(us_ref, refs[0][...], ring_owners(nc, c)[-1])
    names = structure_ref[...].reshape(1, -1)
    w = own_ref.shape[1]
    own_ref[...] = rows_of(us_ref, names, c // 2, width, [c & 1] if len(refs) > 2 else range(us_ref.shape[0]))[:BLOCK_CAP, :w]


def row_order(names, c, rows, nc, slots, direct):
    n = names.shape[1]
    z = c // 2
    lg = log2(nc)
    row = c * rows + lax.broadcasted_iota(jnp.int32, (rows, n), 0)
    rank = jnp.sum(one_hot(names < row), axis=1, keepdims=True).astype(jnp.int32)
    member = jnp.sum(one_hot(names == row), axis=1, keepdims=True)
    turn = rank & (nc - 1)
    ahead = (count(names < c * rows) - turn + nc - 1) >> lg
    block = turn >> 1
    if direct:
        block = block ^ z
    block = 2 * block + (turn & 1)
    slot = jnp.where(member > 0.5, block * slots + (rank >> lg) - ahead, -1)
    at = lax.broadcasted_iota(jnp.int32, (rows, nc * slots), 1)
    return one_hot(at == slot).T.astype(BF16)


def order_kernel(direct, slots, structure_ref, to_ref, place_ref, from_ref):
    nc = to_ref.shape[0] // slots
    rows = to_ref.shape[1]
    nz = nc // 2
    lg = log2(nc)
    names = structure_ref[...].reshape(1, -1)
    n = names.shape[1]
    m = n // nc
    c = lax.axis_index("pcol")
    z, x = c // 2, c & 1
    to_ref[...] = row_order(names, c, rows, nc, slots, direct)

    start, middle = count(names < 2 * z * rows), count(names < (2 * z + 1) * rows)
    named = pltpu.roll(jnp.broadcast_to(names, (8, n)), lax.rem(n - start, n), 1)[:1, :CAP]
    index = start + lax.broadcasted_iota(jnp.int32, (1, CAP), 1)
    half = jnp.where(named >= (2 * z + 1) * rows, 1, 0)
    turn = index & (nc - 1)
    ahead = (jnp.where(half == 1, middle, start) - turn + nc - 1) >> lg
    block = turn >> 1
    if direct:
        block = block ^ z
    slot = (2 * block + (turn & 1)) * slots + (index >> lg) - ahead + (half ^ x) * rows
    slot = jnp.where((named >= 2 * z * rows) & (named < (2 * z + 2) * rows), slot, -1)
    at = lax.broadcasted_iota(jnp.int32, (2 * rows, CAP), 0)
    place_ref[...] = one_hot(at == slot).T.astype(BF16)[:BLOCK_CAP]

    own = lax.broadcasted_iota(jnp.int32, (m, n), 1) - nc * lax.broadcasted_iota(jnp.int32, (m, n), 0)
    mine = jnp.sum(jnp.where(own == c, names, 0).astype(jnp.float32), axis=1, keepdims=True)
    source = jnp.zeros((m, 1), jnp.int32)
    before = jnp.zeros((m, 1), jnp.int32)
    for k in range(1, nc):
        less = mine < float(k * rows)
        source = source + jnp.where(less, 0, 1)
        before = jnp.where(less, before, count(less))
    block = source >> 1
    if direct:
        block = block ^ z
    block = block + nz * ((source ^ c) & 1)
    slot = block * slots + lax.broadcasted_iota(jnp.int32, (m, 1), 0) - before
    at = lax.broadcasted_iota(jnp.int32, (m, rows), 1)
    from_ref[...] = one_hot(at == slot).astype(BF16)


def near_kernel(owners, rest, structure_ref, us_ref, *refs):
    block_refs, (image_ref, uh_ref, ul_ref) = refs[:-3], refs[-3:]
    rows, w = image_ref.shape
    width = rows * 2
    names = structure_ref[...].reshape(1, -1)
    r = lax.axis_index("prow")
    image = jnp.zeros((rows, w), jnp.float32)
    for owner, block_ref in zip(owners(r), block_refs):
        image = image + block_term(block_ref, *cut(us_ref, names, owner, width, w), rows)
    image_ref[...] = image
    if rest is None:

        @pl.loop(0, uh_ref.shape[0])
        def _(k):
            uh_ref[k], ul_ref[k] = cut(us_ref, names, k, width, w)

    else:
        for k, owner in enumerate(rest(r)):
            uh_ref[k], ul_ref[k] = cut(us_ref, names, owner, width, w)


def far_terms(places, uh_ref, ul_ref, image, block_refs):
    rows = image.shape[0]
    for k, block_ref in zip(places, block_refs):
        image = image + block_term(block_ref, uh_ref[k], ul_ref[k], rows)
    return image


def far_kernel(uh_ref, ul_ref, part_ref, *refs):
    places = [0] + list(range(1, uh_ref.shape[0], 2))
    refs[-1][...] = far_terms(places, uh_ref, ul_ref, part_ref[...], refs[:-1])


def image_kernel(direct, uh_ref, ul_ref, part_ref, to_ref, *refs):
    n_in = (uh_ref.shape[0] - 1) // 2 if direct else 1
    block_refs, out_refs = refs[:n_in], refs[n_in:]
    n_out = len(out_refs)
    rows = part_ref.shape[0]
    image = part_ref[...]
    if direct:
        image = far_terms(range(2, uh_ref.shape[0], 2), uh_ref, ul_ref, image, block_refs)
    else:
        stack = block_refs[0]
        add = lambda b, v: v + block_term(stack.at[b], uh_ref[b], ul_ref[b], rows)
        image = lax.fori_loop(0, stack.shape[0], add, image)
    high, low = split(image)
    image = dot(to_ref[...], high) + dot(to_ref[...], low)
    out_refs[0][...] = image
    size = image.shape[0] // n_out
    for k in range(1, n_out):
        out_refs[k][...] = image[size * k : size * (k + 1)]


def turn_kernel(direct, owners, place_ref, *refs):
    high_ref, low_ref, held_ref = refs[-3:]
    nz, wd, size = high_ref.shape
    z = lax.axis_index("pcol") // 2

    def put(owner, u_ref):
        where = (owner ^ z) if direct else owner
        high, low = split(u_ref[...].T)
        held_ref[pl.ds(pl.multiple_of(where * wd, wd), wd), :] = high
        held_ref[pl.ds(pl.multiple_of((where + nz) * wd, wd), wd), :] = low

    each(refs[:-3], owners(lax.axis_index("prow")) if direct else None, put)
    turned = dot(held_ref[...], place_ref[...]).astype(BF16).reshape(2, nz, wd, size)
    high_ref[...] = turned[0]
    low_ref[...] = turned[1]


def correction_kernel(high_ref, low_ref, mine_ref, other_ref, *out_refs):
    sh, sl = split(jnp.concatenate([mine_ref[...], other_ref[...]], axis=0))

    def term(t):
        return dot(high_ref[t], sh) + (dot(high_ref[t], sl) + dot(low_ref[t], sh))

    if len(out_refs) > 1:
        for t, out_ref in enumerate(out_refs):
            out_ref[...] = term(t)
    else:

        @pl.loop(0, out_refs[0].shape[0])
        def _(t):
            out_refs[0][t] = term(t)


def sum_kernel(*refs):
    total = refs[0][...]
    for ref in refs[1:-1]:
        total = total + ref[...]
    refs[-1][...] = total


def part_kernel(slots, *refs):
    mine_ref, theirs_ref = refs[-2:]
    first = (lax.axis_index("pcol") & 1) == 0
    blocks = mine_ref.shape[0] // slots
    mine, theirs = [], []
    for ref in refs[:-2]:
        for k in range(blocks // len(refs[:-2])):
            low = ref[2 * slots * k : 2 * slots * k + slots, :]
            high = ref[2 * slots * k + slots : 2 * slots * (k + 1), :]
            mine.append(jnp.where(first, low, high))
            theirs.append(jnp.where(first, high, low))
    mine_ref[...] = jnp.concatenate(mine, axis=0)
    theirs_ref[...] = jnp.concatenate(theirs, axis=0)


def last_sum_kernel(from_ref, mine_ref, other_ref, d_ref, total_ref, got_ref, sj_ref, jj_ref):
    sj_ref[...] = -pick_rows(from_ref[...], jnp.concatenate([mine_ref[...], other_ref[...]], axis=0))
    jj_ref[...] = d_ref[...] + (total_ref[...] + got_ref[...])


def call(kernel, out_shape, *args, flops=0, vmem=20, **kw):
    many = isinstance(out_shape, (list, tuple))
    size = flops and sum(v.size * v.dtype.itemsize for v in jax.tree.leaves((out_shape, args)))
    kw = {"in_specs": [VMEM] * len(args)} | kw
    return pl.pallas_call(
        kernel,
        out_shape=out_shape,
        out_specs=[VMEM] * len(out_shape) if many else VMEM,
        cost_estimate=pl.CostEstimate(flops=flops, bytes_accessed=size, transcendentals=0),
        compiler_params=pltpu.CompilerParams(vmem_limit_bytes=vmem * 2**20),
        **kw,
    )(*args)


def swap(v, axis, size):
    return lax.ppermute(v, axis, [(k, k ^ 1) for k in range(size)])


def spread(v, size, after):
    blocks = [v, swap(v, "prow", size)]
    v, _ = lax.optimization_barrier((v, after))
    for t in range(1, size // 2):
        for flip in range(2):
            blocks.append(lax.ppermute(v, "prow", [(k, ((k + 2 * t) % size) ^ flip) for k in range(size)]))
    return blocks


def relative_owners(size, r):
    out = []
    for t in range(size // 2):
        owner = (r - 2 * t) & (size - 1)
        out += [owner, owner ^ 1]
    return out


def ring_gather(u, nc, aside):
    ring = [2 * z for z in range(nc // 2)] + [2 * z + 1 for z in reversed(range(nc // 2))]
    pairs = [(ring[q - 1], ring[q]) for q in range(nc)]
    back = [(b, a) for a, b in pairs]
    blocks = [u]
    up = down = u
    for step in range(1, nc // 2):
        up, down = lax.ppermute(up, "pcol", pairs), lax.ppermute(down, "pcol", back)
        if step == 1:
            up, down = lax.optimization_barrier((up, down))
        blocks += [up, down]
    last, aside = lax.optimization_barrier((lax.ppermute(up, "pcol", pairs), aside))
    return blocks + [last], aside


def ring_owners(nc, c):
    q = jnp.where((c & 1) == 0, c >> 1, nc - 1 - (c >> 1))
    out = []
    for k in range(nc):
        step = (k + 1) // 2
        at = (q - step if k % 2 else q + step) & (nc - 1)
        out.append(jnp.where(at < nc // 2, 2 * at, 2 * (nc - 1 - at) + 1))
    return out


def per_device(sigma_top, structure, u_panel, d_term):
    nc, nr = lax.axis_size("pcol"), lax.axis_size("prow")
    c = lax.axis_index("pcol")
    nz = nc // 2
    rows, cols = sigma_top.shape
    m, w = u_panel.shape
    wd = w // 2
    n = structure.shape[0]
    slots = -(-rows // nc)
    direct = (nr, nc) == (4, 8)
    names = structure
    groups = [[2 * k + x for k in range(nz)] for x in range(2)]
    owners = functools.partial(relative_owners, nr)

    chosen = call(
        select_kernel,
        f32(rows * CAP // LANES, LANES),
        names,
        sigma_top,
        in_specs=[VMEM, HBM],
        scratch_shapes=[pltpu.VMEM((rows, cols), jnp.float32), pltpu.SemaphoreType.DMA((2,))],
        flops=4 * rows * cols * WIDE,
        vmem=52,
    )
    to, place, source = call(
        functools.partial(order_kernel, direct, slots),
        [bf16(nc * slots, rows), bf16(BLOCK_CAP, 2 * nc * slots), bf16(m, nc * slots)],
        names,
    )
    if direct:
        u_all, to = ring_gather(u_panel, nc, to)
    else:
        u_all = [lax.all_gather(u_panel, "pcol")]
    term = 6 * rows * WIDE * w
    placed = f32(-(-w // LANES), n + CAP + 8, LANES)
    early, late = (u_all[:-1], u_all[-1:]) if direct else (u_all, [])
    before = call(functools.partial(place_kernel, direct, nc), placed, *early, flops=8 * term)
    us, own = call(
        functools.partial(last_kernel, nc, cols),
        [placed, f32(BLOCK_CAP, wd if direct else w)],
        names,
        before,
        *late,
        flops=term,
    )
    halves = bf16(nr - 1 if direct else nr, WIDE, w)
    near = [chosen] if direct else []
    image, uh, ul = call(
        functools.partial(near_kernel, lambda r: owners(r)[:1], (lambda r: owners(r)[1:]) if direct else None),
        [f32(rows, w), halves, halves],
        names,
        us,
        *near,
        flops=0,
    )
    if direct:
        beside, later = [swap(chosen, "prow", nr)], []
        for t in range(1, nr // 2):
            far = lax.ppermute(chosen, "prow", [(k, (k + 2 * t) % nr) for k in range(nr)])
            far, _ = lax.optimization_barrier((far, image))
            beside.append(far)
            later.append(swap(far, "prow", nr))
        image = call(far_kernel, f32(rows, w), uh, ul, image, *beside, flops=1 * term)
    else:
        later = [lax.all_gather(chosen, "prow")]
    if direct:
        owned = spread(own, nr, beside[1])
    sent = call(
        functools.partial(image_kernel, direct),
        [f32(nc * slots, w)] + [f32(2 * slots, w)] * ((nz - 1) * direct),
        uh,
        ul,
        image,
        to,
        *later,
        flops=term,
    )
    meet = lambda v, t: lax.ppermute(v, "pcol", [(k, k ^ (2 * t)) for k in range(nc)])
    whole = sent[0]
    other = swap(whole, "pcol", nc)
    if direct:
        got = [whole] + [meet(sent[t], t) for t in range(1, nz)]
    else:
        blocks = whole.reshape(nz, 2 * slots, w)
        blocks = lax.all_to_all(blocks, "pcol", split_axis=0, concat_axis=0, axis_index_groups=groups, tiled=True)
        got = [blocks.reshape(nc * slots, w)]
        own = jnp.where(jnp.bitwise_and(c, 1) == 0, own[:, :wd], own[:, wd:])
        owned = [lax.all_gather(own, "prow")]

    turned = bf16(nz, wd, 2 * nc * slots)
    high, low = call(
        functools.partial(turn_kernel, direct, owners),
        [turned, turned],
        place,
        *owned,
        scratch_shapes=[pltpu.VMEM((2 * nz * wd, BLOCK_CAP), BF16)],
        flops=8 * nz * wd * nc * slots * CAP,
    )
    parts = [f32(wd, w)] * nz if direct else [f32(nz, wd, w)]
    got, _ = lax.optimization_barrier((got, high))
    mine, theirs = call(functools.partial(part_kernel, slots), [f32(nz * slots, w)] * 2, *got, flops=2 * term)
    other, _ = lax.optimization_barrier((other, mine))
    terms = call(correction_kernel, parts, high, low, whole, other, flops=term)
    theirs, _ = lax.optimization_barrier((theirs, terms[0]))
    theirs = swap(theirs, "pcol", nc)
    if direct:
        far = [meet(terms[t], t) for t in range(2, nz)]
        total = call(sum_kernel, f32(wd, w), terms[0], *far, flops=4 * term)
        rest = meet(terms[1], 1)
    else:
        terms = lax.all_to_all(terms[0], "pcol", split_axis=0, concat_axis=0, axis_index_groups=groups, tiled=True)
        total, rest = jnp.sum(terms[1:], axis=0), terms[0]
    outs = [f32(m, w), f32(wd, w)]
    return tuple(call(last_sum_kernel, outs, source, mine, theirs, d_term, total, rest, flops=term // 4))


def solution(mesh):
    placed = (P("pcol", "prow"), P(), P("pcol", "prow"), P("pcol", "prow"))
    return jax.shard_map(
        per_device,
        mesh=mesh,
        in_specs=placed,
        out_specs=(P("pcol", "prow"), P("pcol", "prow")),
        check_vma=False,
    )
```
